32 devices in a mesh: groups: 2 (over y), leaf: 16 (over z, x, core).
Axes of the slice: x: 2, y: 2, z: 4, core: 2. Of those that a mesh axis runs over, the one named last changes fastest.
Arguments:
- rhs: bfloat16 [81920, 64], P(('groups', 'leaf')), parts along dimension 0, may hold values from -6 to 6
- basis: bfloat16 [1280, 64, 32], P(('groups', 'leaf')), parts along dimension 0, may hold values from -0.75 to 0.75
- transfer: bfloat16 [1280, 32, 32], P(('groups', 'leaf')), parts along dimension 0, may hold values from -0.375 to 0.375
- near_rows: bfloat16 [1280, 64, 1728], P(('groups', 'leaf')), parts along dimension 0, may hold values from -0.15625 to 0.15625
- near_source: int32 [1280, 27], P(('groups', 'leaf')), parts along dimension 0, may hold values from 0 to 71, as said below
- far_request: int32 [32, 8, 8], P(('groups', 'leaf')), parts along dimension 0, may hold values from 0 to 40, as said below
- coup_rows: bfloat16 [1280, 32, 512], P(('groups', 'leaf')), parts along dimension 0, may hold values from -0.25 to 0.25
- coup_source: int32 [1280, 16], P(('groups', 'leaf')), parts along dimension 0, may hold values from 0 to 103
- par_rows: bfloat16 [160, 32, 512], P(('groups', 'leaf')), parts along dimension 0, may hold values from -0.25 to 0.25
- par_source: int32 [160, 16], P(('groups', 'leaf')), parts along dimension 0, may hold values from 0 to 44, as said below
Outputs:
- product: bfloat16 [81920, 64], P(('groups', 'leaf')), parts along dimension 0
The draws below stay inside these ranges and needn't reach their ends.
There are 2 independent parts, one for each index of `groups`. The reference program is written for one: setup_inputs(seed, part) draws one part's arguments, and reference() takes and returns one part's arrays. A program takes and returns all parts, laid end to end along the dimension named above; each array names one. Nothing has to cross between parts.
Inputs may be any that keep to these rules, and one draw needn't show every extreme that they name: `near_source`: entry j of leaf i is the position of a source leaf in leaf i's block extended by 16 leaves on each side (position 16 is the block's first leaf); the source lies within 16 leaves of i in tree order and inside the point set. `far_request`: row k of block d lists positions of distinct leaves of block d + o (o as in the reference program); filled slots come first and 40 marks an empty slot; rows that point past the ends of the axis are empty. Every block asks the next block for 8 leaves, and some block is asked for 8 leaves by every block within 4 of it. `par_source`: entry j of parent p is the position of a source parent among the parents of p's block extended by 4 blocks' parents on each side (position 20 is the block's first parent); the source lies within 20 parents of p in tree order and inside the point set.
All inputs are finite; a program needn't handle non-finite values.
Results may differ from the reference program's by a relative error of at most 0.0047.
Values may be sent and summed in bfloat16 or wider, within the bound.
No kernel may reach another device: no remote copies, remote signals or barrier semaphores. Data moves between devices by JAX's collectives and lax.ppermute only.
A program may use at most 128 MiB of HBM per device.

```python
import jax
import jax.numpy as jnp
from jax import lax

LEAF = 64
RANK = 32
NRHS = 64
LEAVES_DEV = 40
HALO = 16
NEAR_PER = 27
COUP_PER = 16
PCOUP_PER = 16
SPAN = 4
CAP = 8
PAR_DEV = 5
NLEAVES = 640
NPAR = 80
NPOINTS = 40960
SLOTS = 104
N_LEAF = 16


def draw_near_source(key, part):
    key = jax.random.fold_in(key, 11)
    offsets = jax.random.randint(key, (NLEAVES, NEAR_PER), -HALO, HALO + 1)
    column = lax.broadcasted_iota(jnp.int32, (NLEAVES, NEAR_PER), 1)
    leaf_ids = lax.broadcasted_iota(jnp.int32, (NLEAVES, NEAR_PER), 0)
    local_pos = leaf_ids % LEAVES_DEV
    offsets = jnp.where(column == 0, 0, offsets)
    offsets = jnp.where((column == 1) & (local_pos == 0), -HALO, offsets)
    offsets = jnp.where((column == 1) & (local_pos == LEAVES_DEV - 1), HALO, offsets)
    target = jnp.clip(leaf_ids + offsets, 0, NLEAVES - 1)
    return (target - leaf_ids + local_pos + HALO).astype(jnp.int32)


def draw_far_request(key, part):
    key = jax.random.fold_in(key, 23)
    key_count, key_score, key_owner = jax.random.split(key, 3)
    counts = jax.random.randint(key_count, (N_LEAF, 2 * SPAN), 0, CAP + 1)
    device_ids = lax.broadcasted_iota(jnp.int32, (N_LEAF, 2 * SPAN), 0)
    offset_ids = lax.broadcasted_iota(jnp.int32, (N_LEAF, 2 * SPAN), 1)
    offsets = jnp.where(offset_ids < SPAN, offset_ids - SPAN, offset_ids - SPAN + 1)
    owner_id = jax.random.randint(key_owner, (), 0, N_LEAF)
    peer_id = device_ids + offsets
    counts = jnp.where(offsets == 1, CAP, counts)
    counts = jnp.where(peer_id == owner_id, CAP, counts)
    counts = jnp.where((peer_id < 0) | (peer_id >= N_LEAF), 0, counts)
    scores = jax.random.randint(key_score, (N_LEAF, 2 * SPAN, LEAVES_DEV), 0, 1 << 20)
    scores = scores * LEAVES_DEV + lax.broadcasted_iota(jnp.int32, (N_LEAF, 2 * SPAN, LEAVES_DEV), 2)
    ordering = jnp.argsort(scores, axis=-1)[:, :, :CAP].astype(jnp.int32)
    slot_ids = lax.broadcasted_iota(jnp.int32, (N_LEAF, 2 * SPAN, CAP), 2)
    return jnp.where(slot_ids < counts[:, :, None], ordering, LEAVES_DEV).astype(jnp.int32)


def draw_par_source(key, part):
    key = jax.random.fold_in(key, 37)
    reach = SPAN * PAR_DEV
    offsets = jax.random.randint(key, (NPAR, PCOUP_PER), -reach, reach + 1)
    column = lax.broadcasted_iota(jnp.int32, (NPAR, PCOUP_PER), 1)
    parent_ids = lax.broadcasted_iota(jnp.int32, (NPAR, PCOUP_PER), 0)
    local_pos = parent_ids % PAR_DEV
    offsets = jnp.where(column == 0, -reach, offsets)
    offsets = jnp.where(column == 1, reach, offsets)
    target = jnp.clip(parent_ids + offsets, 0, NPAR - 1)
    return (target - parent_ids + local_pos + reach).astype(jnp.int32)


def set_ends(result, rng, low, largest):
    place = [jax.random.randint(jax.random.fold_in(rng, axis), (), 0, length) for axis, length in enumerate(result.shape)]
    longest = result.shape.index(max(result.shape))
    beside = place[:longest] + [(place[longest] + 1) % result.shape[longest]] + place[longest + 1:]
    return result.at[tuple(place)].set(low).at[tuple(beside)].set(largest)


def block_scale(key, dims, cuts, smallest, top_value):
    def one(axis_at, parts):
        draws = jax.random.uniform(jax.random.fold_in(jax.random.fold_in(key, 6), axis_at), (parts,), jnp.float32, smallest / len(cuts), top_value / len(cuts))
        return jnp.repeat(jnp.exp(draws), dims[axis_at] // parts).reshape((-1,) + (1,) * (len(dims) - axis_at - 1))

    factor_of = one(*cuts[0])
    for cut in cuts[1:]:
        factor_of = factor_of * one(*cut)
    return factor_of


def noise(key, extent, deviation, bound, shards=(), kind=jnp.bfloat16):
    level = block_scale(key, extent, shards, -0.22, 0.18) if shards else 1.0
    result = jax.random.normal(key, extent, jnp.float32) * deviation * level
    return jnp.minimum(jnp.maximum(result, -bound), bound).astype(kind)


def setup_inputs(seed: int = 0, part: int = 0) -> dict:
    streams_of = jax.random.split(jax.random.key(seed), 11)
    own_keys = jax.random.split(jax.random.fold_in(streams_of[10], part), 11)
    rhs = noise(own_keys[0], (NPOINTS, NRHS), 1.0, 6.0, ((0, 16),))
    basis = noise(own_keys[1], (NLEAVES, LEAF, RANK), LEAF ** -0.5, 0.75, ((0, 16),))
    transfer = noise(own_keys[2], (NLEAVES, RANK, RANK), (8 * RANK) ** -0.5, 0.375, ((0, 16),))
    near_rows = noise(own_keys[3], (NLEAVES, LEAF, NEAR_PER * LEAF), (NEAR_PER * LEAF) ** -0.5, 0.15625, ((0, 16),))
    near_source = draw_near_source(jax.random.fold_in(jax.random.fold_in(streams_of[10], part), 71), part)
    far_request = draw_far_request(jax.random.fold_in(jax.random.fold_in(streams_of[10], part), 71), part)
    coup_rows = noise(own_keys[6], (NLEAVES, RANK, COUP_PER * RANK), (COUP_PER * RANK) ** -0.5, 0.25, ((0, 16),))
    coup_source = set_ends(jax.random.randint(own_keys[7], (NLEAVES, COUP_PER), 0, SLOTS), jax.random.fold_in(own_keys[7], 1), 0, SLOTS - 1).astype(jnp.int32)
    par_rows = noise(own_keys[8], (NPAR, RANK, PCOUP_PER * RANK), (PCOUP_PER * RANK) ** -0.5, 0.25, ((0, 16),))
    par_source = draw_par_source(jax.random.fold_in(jax.random.fold_in(streams_of[10], part), 71), part)
    return {"rhs": rhs, "basis": basis, "transfer": transfer, "near_rows": near_rows, "near_source": near_source, "far_request": far_request, "coup_rows": coup_rows, "coup_source": coup_source, "par_rows": par_rows, "par_source": par_source}


def reference(rhs, basis, transfer, near_rows, near_source, far_request, coup_rows, coup_source, par_rows, par_source):
    leaves_x = rhs.reshape(NLEAVES, LEAF, NRHS)
    skeleton = jnp.einsum('ilr,iln->irn', basis.astype(jnp.float32), leaves_x.astype(jnp.float32)).astype(jnp.bfloat16)
    upward = jnp.einsum('iab,ian->ibn', transfer.astype(jnp.float32), skeleton.astype(jnp.float32))
    parent_skeleton = upward.reshape(NPAR, 8, RANK, NRHS).sum(1).astype(jnp.bfloat16)
    parent_ids = jnp.arange(NPAR, dtype=jnp.int32)
    block_first = (parent_ids // PAR_DEV) * PAR_DEV
    par_index = (block_first[:, None] + par_source - SPAN * PAR_DEV).astype(jnp.int32)
    par_picked = parent_skeleton[par_index.reshape(-1)].reshape(NPAR, PCOUP_PER * RANK, NRHS)
    parent_out = jnp.einsum('irk,ikn->irn', par_rows.astype(jnp.float32), par_picked.astype(jnp.float32)).astype(jnp.bfloat16)

    blocks = jnp.arange(N_LEAF, dtype=jnp.int32)
    offset_ids = jnp.arange(2 * SPAN, dtype=jnp.int32)
    offsets = jnp.where(offset_ids < SPAN, offset_ids - SPAN, offset_ids - SPAN + 1)
    peer_id = blocks[:, None] + offsets[None, :]
    in_range = (peer_id >= 0) & (peer_id < N_LEAF)
    is_live = in_range[:, :, None] & (far_request < LEAVES_DEV)
    slot_index = jnp.where(is_live, peer_id[:, :, None] * LEAVES_DEV + far_request, NLEAVES).astype(jnp.int32)
    skel_pad = jnp.concatenate([skeleton, jnp.zeros((1, RANK, NRHS), jnp.bfloat16)], 0)
    remote = skel_pad[slot_index.reshape(N_LEAF, 2 * SPAN * CAP)]
    slot_rows = jnp.concatenate([skeleton.reshape(N_LEAF, LEAVES_DEV, RANK, NRHS), remote], 1)

    halo_zeros = jnp.zeros((HALO, LEAF, NRHS), jnp.bfloat16)
    padded_x = jnp.concatenate([halo_zeros, leaves_x, halo_zeros], 0)

    def per_block(pieces):
        block_id, block_slots, coup_src, coup_mat, near_src, near_mat = pieces
        picked = block_slots[coup_src.reshape(-1)].reshape(LEAVES_DEV, COUP_PER * RANK, NRHS)
        coupled = jnp.einsum('irk,ikn->irn', coup_mat.astype(jnp.float32), picked.astype(jnp.float32))
        near_index = (block_id * LEAVES_DEV + near_src).astype(jnp.int32)
        stacked = padded_x[near_index.reshape(-1)].reshape(LEAVES_DEV, NEAR_PER * LEAF, NRHS)
        near_part = jnp.einsum('ilk,ikn->iln', near_mat.astype(jnp.float32), stacked.astype(jnp.float32))
        return coupled, near_part

    coupled, near_part = lax.map(per_block, (
        blocks,
        slot_rows,
        coup_source.reshape(N_LEAF, LEAVES_DEV, COUP_PER),
        coup_rows.reshape(N_LEAF, LEAVES_DEV, RANK, COUP_PER * RANK),
        near_source.reshape(N_LEAF, LEAVES_DEV, NEAR_PER),
        near_rows.reshape(N_LEAF, LEAVES_DEV, LEAF, NEAR_PER * LEAF)))
    coupled = coupled.reshape(NLEAVES, RANK, NRHS)
    near_part = near_part.reshape(NLEAVES, LEAF, NRHS)
    downward = jnp.einsum('iab,ibn->ian', transfer.astype(jnp.float32), jnp.repeat(parent_out, 8, 0).astype(jnp.float32))
    leaf_out = (coupled + downward).astype(jnp.bfloat16)
    far_part = jnp.einsum('ilr,irn->iln', basis.astype(jnp.float32), leaf_out.astype(jnp.float32))
    return (near_part + far_part).reshape(NPOINTS, NRHS).astype(jnp.bfloat16)
```

```python
import functools

import jax
import jax.numpy as jnp
from jax import lax
from jax.experimental import pallas as pl
from jax.experimental.pallas import tpu as pltpu
from jax.sharding import PartitionSpec as P

HALO = 16
BF = jnp.bfloat16
F32 = jnp.float32
ROWS_NEXT = (0, 3, 5)
ROWS_PREV = (2, 4, 7)


def far_routes(count):
    by_source, by_target = [{}, {}], [{}, {}]

    def put(color, source, target):
        by_source[color][source] = target
        by_target[color][target] = source

    for i in range(count):
        if i + 3 < count:
            put(0, i, i + 3)
            put(1, i + 3, i)
    for source, target in ((2, 1), (count - 3, count - 2)):
        color = 0 if target not in by_target[0] else 1
        moving = [(color, source, target)]
        while moving:
            color, source, target = moving.pop()
            old_target = by_source[color].get(source)
            if old_target is not None:
                del by_target[color][old_target]
            old_source = by_target[color].get(target)
            if old_source is not None:
                del by_source[color][old_source]
            put(color, source, target)
            if old_target is not None:
                moving.append((1 - color, source, old_target))
            if old_source is not None:
                moving.append((1 - color, old_source, target))
    swaps = [
        i
        for i in range(count)
        if by_target[1].get(i, i) < i and i != count - 2 or by_target[0].get(i, i) > i and i != 1
    ]
    return [sorted(routes.items()) for routes in by_source], swaps


def is_any(value, numbers):
    found = value < 0
    for number in numbers:
        found = found | (value == number)
    return found
VMEM = pltpu.VMEM
SMEM = pltpu.SMEM


def low_half(rows):
    return lax.broadcasted_iota(jnp.int32, (rows, 128), 1) < 64


def swapped(value):
    return pltpu.roll(value, 64, 1)


def matmul(a, b):
    return jnp.dot(a, b, preferred_element_type=F32)


def matmul_nt(a, b):
    return lax.dot_general(a, b, (((1,), (1,)), ((), ())), preferred_element_type=F32)


def matmul_tn(a, b):
    return lax.dot_general(a, b, (((0,), (0,)), ((), ())), preferred_element_type=F32)


def fill_block_diagonal(basis_ref, diag):
    leaf_count, rank, leaf = basis_ref.shape
    blank = jnp.zeros((rank, leaf), BF)
    empty = jnp.zeros((rank, 2 * leaf), BF)
    for i in range(leaf_count):
        rows = slice(rank * i, rank * (i + 1))
        block = basis_ref[i]
        pair = [block, blank] if i % 2 == 0 else [blank, block]
        place = i % 4 // 2
        diag[rows, 128 * place : 128 * place + 128] = jnp.concatenate(pair, 1)
        diag[rows, 128 * (1 - place) : 128 * (1 - place) + 128] = empty


def up_kernel(x_ref, basis_ref, trans_ref, req_ref, tail_ref, head_ref, skel_ref, tst_ref, diag, flat, req):
    rhs_count, points = x_ref.shape
    leaf_count, rank, leaf = basis_ref.shape
    width = tail_ref.shape[1] - 128
    req[...] = jnp.zeros(req.shape, F32)
    req[0:8, 0:8] = req_ref[...].astype(F32)
    asked = req[...].astype(BF)
    tail_ref[:, :width] = x_ref[:, points - width :]
    tail_ref[:, width:] = asked
    head_ref[:, :width] = x_ref[:, :width]
    head_ref[:, width:] = asked

    fill_block_diagonal(basis_ref, diag)
    for step in range(rank // 4):
        block = trans_ref[128 * step : 128 * step + 128, :].astype(F32).T
        for q in range(4):
            piece = block if q == 0 else pltpu.roll(block, 128 - 32 * q, 1)
            flat[pl.ds(4 * step + q, leaf_count, stride=rank), :] = piece
    tst_ref[...] = flat[:, 0:rank].astype(BF)

    low = low_half(2 * rank)
    low_one = low_half(rank)
    parents = []
    for p in range(leaf_count // 8):
        halves = []
        for quad in (2 * p, 2 * p + 1):
            x = x_ref[:, 256 * quad : 256 * quad + 256]
            skel = matmul_nt(
                diag[128 * quad : 128 * quad + 128, :], jnp.concatenate([x, x], 0)
            ).astype(BF)
            skel_ref[64 * quad : 64 * quad + 64, :] = jnp.where(low, skel[:64], skel[64:])
            halves.append(skel)
        parents.append(
            matmul_tn(tst_ref[256 * p : 256 * p + 256, :], jnp.concatenate(halves, 0)).astype(BF)
        )
    base = 16 * leaf_count
    for m in range((len(parents) + 1) // 2):
        left, right = parents[2 * m], parents[min(2 * m + 1, len(parents) - 1)]
        skel_ref[base + 32 * m : base + 32 * m + 32, :] = jnp.where(low_one, left, right)


def pick(ref, r, leaf_count, want_high):
    safe = jnp.minimum(r, leaf_count - 1)
    row = pl.multiple_of((safe >> 2) * 64 + (safe & 1) * 32, 32)
    value = ref[pl.ds(row, 32), :]
    moved = ((safe >> 1) & 1) != want_high
    value = jnp.where(moved, swapped(value), value)
    return jnp.where(r < leaf_count, value, jnp.zeros_like(value))


def reply_kernel(
    count,
    swaps,
    leaf_count,
    prev_ref,
    next_ref,
    own_ref,
    first_ref,
    second_ref,
    to_next,
    to_prev,
    before_ref,
    after_ref,
    ints,
    nums,
    sem,
):
    me = lax.axis_index("leaf")
    swap = is_any(me, swaps)
    width = prev_ref.shape[1] - 128
    ints[0:16, :] = next_ref[0:16, width:].astype(F32).astype(jnp.int32)
    ints[16:32, :] = prev_ref[0:16, width:].astype(F32).astype(jnp.int32)
    copy = pltpu.make_async_copy(ints, nums, sem)
    copy.start()
    first, second = first_ref[...], second_ref[...]
    before_ref[...] = jnp.where(swap, second, first)
    after_ref[...] = jnp.where(swap, first, second)
    blocks = (before_ref, own_ref, after_ref)
    stride = to_next.shape[0] // 3
    base = 16 * leaf_count
    for out in (to_next, to_prev):
        for b, ref in enumerate(blocks):
            out[stride * b + 128 : stride * (b + 1), :] = ref[base:, :]
    copy.wait()
    low = low_half(32)
    rows_next = ROWS_NEXT[:2] + (jnp.where(me == count - 2, 2, 5),)
    rows_prev = (jnp.where(me == 1, 5, 2),) + ROWS_PREV[1:]
    for out, first, rows in ((to_next, 0, rows_next), (to_prev, 16, rows_prev)):
        for b, ref in enumerate(blocks):
            for m in range(4):
                left = pick(ref, nums[first + rows[b], 2 * m], leaf_count, 0)
                right = pick(ref, nums[first + rows[b], 2 * m + 1], leaf_count, 1)
                at = stride * b + 32 * m
                out[at : at + 32, :] = jnp.where(low, left, right)


def near_kernel(
    x_ref, prev_ref, next_ref, near_ref, source_ref, out_ref, held, twice, stacked, sems
):
    leaf_count, leaf, depth = near_ref.shape
    count = source_ref.shape[0]
    width = prev_ref.shape[1] - 128
    quads = leaf_count // 4

    def copy(quad):
        part = pl.ds(4 * quad, 4)
        return pltpu.make_async_copy(near_ref.at[part], held.at[part], sems.at[quad])

    for quad in range(quads):
        copy(quad).start()

    low = low_half(leaf)
    halo = width // leaf

    def spread(ref, tile, at):
        value = ref[:, 128 * tile : 128 * tile + 128]
        other = swapped(value)
        twice[at] = jnp.where(low, value, other)
        twice[at + 1] = jnp.where(low, other, value)

    for tile in range(width // 128):
        spread(prev_ref, tile, 2 * tile)
        spread(next_ref, tile, halo + leaf_count + 2 * tile)
    for tile in range(x_ref.shape[1] // 128):
        spread(x_ref, tile, halo + 2 * tile)

    def body(quad, carry):
        copy(quad).wait()
        slot = lax.rem(quad, 2)
        for u in range(4):
            i = 4 * quad + u
            for m in range(count // 2):
                stacked[slot, 64 * u : 64 * u + 64, 128 * m : 128 * m + 128] = jnp.where(
                    low, twice[source_ref[2 * m, i]], twice[source_ref[2 * m + 1, i]]
                )
            if count % 2:
                m = count // 2
                stacked[slot, 64 * u : 64 * u + 64, 128 * m : 128 * m + 128] = twice[
                    source_ref[count - 1, i]
                ]
        rows = held[pl.ds(4 * quad, 4)].reshape(4 * leaf, depth)
        total = matmul_nt(stacked[slot, :, :depth], rows)
        for t in range(2):
            lanes = pl.ds(pl.multiple_of(256 * quad + 128 * t, 128), 128)
            out_ref[:, lanes] = jnp.where(
                low,
                total[128 * t : 128 * t + 64, 128 * t : 128 * t + 128],
                total[128 * t + 64 : 128 * t + 128, 128 * t : 128 * t + 128],
            )
        return carry

    lax.fori_loop(0, quads, body, 0)


def down_kernel(
    count,
    own_ref,
    before_ref,
    after_ref,
    prev_ref,
    next_ref,
    req_ref,
    coup_source,
    par_source,
    coup_ref,
    par_ref,
    basis_ref,
    tst_ref,
    near_ref,
    out_ref,
    slots,
    window,
    diag,
    weights,
):
    leaf_count, rank, leaf = basis_ref.shape
    parent_count = par_ref.shape[0]
    base = 16 * leaf_count
    stride = prev_ref.shape[0] // 3
    low64 = low_half(64)
    low = low_half(rank)

    def split(value, mask):
        other = swapped(value)
        return jnp.where(mask, value, other), jnp.where(mask, other, value)

    for quad in range(leaf_count // 4):
        first, second = split(own_ref[64 * quad : 64 * quad + 64, :], low64)
        slots[4 * quad] = first[:32]
        slots[4 * quad + 1] = first[32:]
        slots[4 * quad + 2] = second[:32]
        slots[4 * quad + 3] = second[32:]
    me = lax.axis_index("leaf")
    edge = is_any(me, (0, count - 1))
    k_prev, k_next = jnp.where(edge, 2, 5), jnp.where(edge, 5, 2)
    for ref, rows in (
        (prev_ref, ROWS_NEXT[:2] + (k_prev,)),
        (next_ref, (k_next,) + ROWS_PREV[1:]),
    ):
        for b, k in enumerate(rows):
            for m in range(4):
                at = stride * b + 32 * m
                first, second = split(ref[at : at + 32, :], low)
                slots[leaf_count + 8 * k + 2 * m] = first
                slots[leaf_count + 8 * k + 2 * m + 1] = second
    for ref, k in ((before_ref, 1), (after_ref, 6)):
        for c in range(8):
            r = req_ref[k, c]
            safe = jnp.minimum(r, leaf_count - 1)
            row = pl.multiple_of((safe >> 2) * 64 + (safe & 1) * 32, 32)
            first, second = split(ref[pl.ds(row, 32), :], low)
            value = jnp.where(((safe >> 1) & 1) == 0, first, second)
            slots[leaf_count + 8 * k + c] = jnp.where(
                r < leaf_count, value, jnp.zeros_like(value)
            )

    def put_parents(ref, at, block):
        for m in range((parent_count + 1) // 2):
            first, second = split(ref[at + 32 * m : at + 32 * m + 32, :], low)
            window[parent_count * block + 2 * m] = first
            if 2 * m + 1 < parent_count:
                window[parent_count * block + 2 * m + 1] = second

    put_parents(own_ref, base, 4)
    put_parents(before_ref, base, 1)
    put_parents(after_ref, base, 7)
    spot_prev, spot_next = jnp.where(edge, 2, 6), jnp.where(edge, 6, 2)
    for ref, spots in ((prev_ref, (0, 3, spot_prev)), (next_ref, (spot_next, 5, 8))):
        for b, block in enumerate(spots):
            put_parents(ref, stride * b + 128, block)

    fill_block_diagonal(basis_ref, diag)
    per = par_source.shape[1]
    coup = coup_source.shape[0]
    for p in range(parent_count):
        stack = jnp.concatenate([window[par_source[p, j]] for j in range(per)], 0)
        parent_out = matmul(par_ref[p], stack).astype(BF)
        down = matmul(tst_ref[256 * p : 256 * p + 256, :], parent_out)
        for half in range(2):
            quad = 2 * p + half
            for j in range(coup):
                for t in range(2):
                    i = 4 * quad + 2 * t
                    weights[half, rank * j : rank * j + rank, 128 * t : 128 * t + 128] = jnp.where(
                        low, slots[coup_source[j, i]], slots[coup_source[j, i + 1]]
                    )
            rows = coup_ref[4 * quad : 4 * quad + 4].reshape(4 * rank, coup * rank)
            coupled = matmul(rows, weights[half])
            coupled = jnp.concatenate([coupled[:64, :128], coupled[64:, 128:]], 0)
            leaf_out = (coupled + down[128 * half : 128 * half + 128]).astype(BF)
            far = matmul_tn(leaf_out, diag[128 * quad : 128 * quad + 128, :])
            for t in range(2):
                lanes = slice(256 * quad + 128 * t, 256 * quad + 128 * t + 128)
                tile = jnp.where(
                    low64, far[:64, 128 * t : 128 * t + 128], far[64:, 128 * t : 128 * t + 128]
                )
                out_ref[:, lanes] = (near_ref[:, lanes] + tile).astype(BF)


def shift(block, distance):
    devices = range(lax.axis_size("leaf"))
    route = [(i, i + distance) for i in devices if i + distance in devices]
    return lax.ppermute(block, "leaf", route)


def params(mib):
    return pltpu.CompilerParams(vmem_limit_bytes=mib << 20)


def cost(flops, size):
    return pl.CostEstimate(flops=flops, bytes_accessed=size, transcendentals=0)


def shards(
    rhs,
    basis,
    transfer,
    near_rows,
    near_source,
    far_request,
    coup_rows,
    coup_source,
    par_rows,
    par_source,
):
    leaf_count, leaf, rank = basis.shape
    points, rhs_count = rhs.shape
    parent_count = par_rows.shape[0]
    near_count = near_source.shape[1]
    coup_count = coup_source.shape[1]
    width = HALO * leaf
    packed = 16 * leaf_count + rank * ((parent_count + 1) // 2)
    stride = 128 + rank * ((parent_count + 1) // 2)

    x = rhs.T
    basis_t = basis.transpose(0, 2, 1)
    trans = transfer.transpose(1, 2, 0).reshape(rank * rank, leaf_count)
    requests = far_request[0]

    shape = jax.ShapeDtypeStruct
    vmem, smem = pl.BlockSpec(memory_space=VMEM), pl.BlockSpec(memory_space=SMEM)
    tail, head, skel, tst = pl.pallas_call(
        up_kernel,
        out_shape=(
            shape((rhs_count, width + 128), BF),
            shape((rhs_count, width + 128), BF),
            shape((packed, 128), BF),
            shape((rank * leaf_count, rank), BF),
        ),
        in_specs=[vmem] * 4,
        out_specs=(vmem,) * 4,
        scratch_shapes=[
            VMEM((rank * leaf_count, 256), BF),
            VMEM((rank * leaf_count, 128), F32),
            VMEM((rhs_count, 128), F32),
        ],
        compiler_params=params(8),
        cost_estimate=cost(10**9, 2 * 10**6),
        name="upward",
    )(x, basis_t, trans, requests)

    count = lax.axis_size("leaf")
    routes, swaps = far_routes(count)
    first = lax.ppermute(skel, "leaf", routes[0])
    second = lax.ppermute(skel, "leaf", routes[1])
    from_prev = shift(tail, 1)
    from_next = shift(head, -1)

    to_next, to_prev, before, after = pl.pallas_call(
        functools.partial(reply_kernel, count, swaps, leaf_count),
        out_shape=(shape((3 * stride, 128), BF),) * 2 + (shape((packed, 128), BF),) * 2,
        in_specs=[vmem] * 5,
        out_specs=(vmem,) * 4,
        scratch_shapes=[
            VMEM((32, 128), jnp.int32),
            SMEM((32, 128), jnp.int32),
            pltpu.SemaphoreType.DMA,
        ],
        compiler_params=params(8),
        cost_estimate=cost(10**8, 2 * 10**6),
        name="reply",
    )(from_prev, from_next, skel, first, second)

    got_prev = shift(to_next, 1)
    got_next = shift(to_prev, -1)

    near = pl.pallas_call(
        near_kernel,
        out_shape=shape((rhs_count, points), F32),
        in_specs=[vmem, vmem, vmem, pl.BlockSpec(memory_space=pl.ANY), smem],
        out_specs=vmem,
        scratch_shapes=[
            VMEM(near_rows.shape, BF),
            VMEM((leaf_count + 2 * HALO, leaf, 128), BF),
            VMEM((2, 256, 128 * ((near_count + 1) // 2)), BF),
            pltpu.SemaphoreType.DMA((leaf_count // 4,)),
        ],
        compiler_params=params(20),
        cost_estimate=cost(8 * 10**9, 10**7),
        name="near",
    )(x, from_prev, from_next, near_rows, near_source.T)

    product = pl.pallas_call(
        functools.partial(down_kernel, count),
        out_shape=shape((rhs_count, points), BF),
        in_specs=[vmem] * 5 + [smem] * 3 + [vmem] * 5,
        out_specs=vmem,
        scratch_shapes=[
            VMEM((leaf_count + 64, rank, 128), BF),
            VMEM((9 * parent_count, rank, 128), BF),
            VMEM((rank * leaf_count, 256), BF),
            VMEM((2, coup_count * rank, 256), BF),
        ],
        compiler_params=params(12),
        cost_estimate=cost(10**9, 4 * 10**6),
        name="downward",
    )(
        skel,
        before,
        after,
        got_prev,
        got_next,
        requests,
        coup_source.T,
        par_source,
        coup_rows,
        par_rows,
        basis_t,
        tst,
        near,
    )
    return product.T


def solution(mesh):
    split = ("groups", "leaf")
    return jax.shard_map(
        shards,
        mesh=mesh,
        in_specs=(
            P(split, None),
            P(split, None, None),
            P(split, None, None),
            P(split, None, None),
            P(split, None),
            P(split, None, None),
            P(split, None, None),
            P(split, None),
            P(split, None, None),
            P(split, None),
        ),
        out_specs=P(split, None),
        check_vma=False,
    )
```

```python
import functools

import jax
import jax.numpy as jnp
from jax import lax
from jax.experimental import pallas as pl
from jax.experimental.pallas import tpu as pltpu
from jax.sharding import PartitionSpec as P

HALO = 16
BF = jnp.bfloat16
F32 = jnp.float32
VMEM = pltpu.VMEM
SMEM = pltpu.SMEM
DMA = pltpu.SemaphoreType.DMA


def far_routes(count):
    by_source, by_target = [{}, {}], [{}, {}]

    def put(color, source, target):
        by_source[color][source] = target
        by_target[color][target] = source

    for i in range(count - 3):
        put(0, i, i + 3)
        put(1, i + 3, i)
    for source, target in ((count - 2, count - 3), (1, 2)):
        moving = [(0 if target not in by_target[0] else 1, source, target)]
        while moving:
            color, source, target = moving.pop()
            old_target = by_source[color].get(source)
            if old_target is not None:
                del by_target[color][old_target]
            old_source = by_target[color].get(target)
            if old_source is not None:
                del by_source[color][old_source]
            put(color, source, target)
            if old_target is not None:
                moving.append((1 - color, source, old_target))
            if old_source is not None:
                moving.append((1 - color, old_source, target))
    sends, takes = [], []
    for i in range(count):
        up = count - 3 if i == count - 2 else i + 3
        if by_source[1].get(i) == up or by_source[0].get(i, up) != up:
            sends.append(i)
        below = 1 if i == 2 else i - 3
        if by_target[1].get(i) == below or by_target[0].get(i, below) != below:
            takes.append(i)
    return [sorted(routes.items()) for routes in by_source], sends, takes


def is_any(value, numbers):
    found = value < 0
    for number in numbers:
        found = found | (value == number)
    return found


def low_half(rows):
    return lax.broadcasted_iota(jnp.int32, (rows, 128), 1) < 64


def swapped(value):
    return pltpu.roll(value, 64, 1)


def matmul(a, b):
    return jnp.dot(a, b, preferred_element_type=F32)


def matmul_nt(a, b):
    return lax.dot_general(a, b, (((1,), (1,)), ((), ())), preferred_element_type=F32)


def matmul_tn(a, b):
    return lax.dot_general(a, b, (((0,), (0,)), ((), ())), preferred_element_type=F32)


def fill_block_diagonal(basis_ref, diag):
    leaf_count, rank, leaf = basis_ref.shape
    blank = jnp.zeros((rank, leaf), BF)
    empty = jnp.zeros((rank, 2 * leaf), BF)
    for i in range(leaf_count):
        rows = slice(rank * i, rank * (i + 1))
        block = basis_ref[i]
        pair = [block, blank] if i % 2 == 0 else [blank, block]
        place = i % 4 // 2
        diag[rows, 128 * place : 128 * place + 128] = jnp.concatenate(pair, 1)
        diag[rows, 128 * (1 - place) : 128 * (1 - place) + 128] = empty


def up_kernel(x_hbm, basis_hbm, trans_hbm, to_next, to_prev, tst_ref, diag, x_ref, basis_ref, trans_ref, flat, sems):
    points = x_hbm.shape[1]
    leaf_count, rank, leaf = basis_hbm.shape
    copies = [
        pltpu.make_async_copy(source, held, sems.at[n])
        for n, (source, held) in enumerate(
            ((trans_hbm, trans_ref), (basis_hbm, basis_ref), (x_hbm, x_ref))
        )
    ]
    for copy in copies:
        copy.start()
    copies[0].wait()
    for step in range(rank // 4):
        block = trans_ref[128 * step : 128 * step + 128, :].astype(F32).T
        for q in range(4):
            piece = block if q == 0 else pltpu.roll(block, 128 - 32 * q, 1)
            flat[pl.ds(4 * step + q, leaf_count, stride=rank), :] = piece
    tst_ref[...] = flat[:, 0:rank].astype(BF)
    copies[1].wait()
    fill_block_diagonal(basis_ref, diag)
    copies[2].wait()

    base = HALO * leaf // 128 * 64
    for t in range(HALO * leaf // 128):
        rows = slice(64 * t, 64 * t + 64)
        to_prev[rows, :] = x_ref[:, 128 * t : 128 * t + 128]
        at = points - HALO * leaf + 128 * t
        to_next[rows, :] = x_ref[:, at : at + 128]

    def put(at, left, right):
        rows = left.shape[0]
        both = jnp.where(low_half(rows), left, right)
        to_next[base + at : base + at + rows, :] = both
        to_prev[base + at : base + at + rows, :] = both

    parents = []
    for p in range(leaf_count // 8):
        halves = []
        for quad in (2 * p, 2 * p + 1):
            x = x_ref[:, 256 * quad : 256 * quad + 256]
            skel = matmul_nt(
                diag[128 * quad : 128 * quad + 128, :], jnp.concatenate([x, x], 0)
            ).astype(BF)
            put(64 * quad, skel[:64], skel[64:])
            halves.append(skel)
        parents.append(
            matmul_tn(tst_ref[256 * p : 256 * p + 256, :], jnp.concatenate(halves, 0)).astype(BF)
        )
    for m in range((len(parents) + 1) // 2):
        put(16 * leaf_count + 32 * m, parents[2 * m], parents[min(2 * m + 1, len(parents) - 1)])


def place(r, leaf_count):
    safe = jnp.minimum(r, leaf_count - 1)
    return pl.multiple_of((safe >> 2) * 64 + (safe & 1) * 32, 32), (safe >> 1) & 1


def pick(ref, base, r, leaf_count, want_high):
    row, high = place(r, leaf_count)
    value = ref[pl.ds(base + row, 32), :]
    value = jnp.where(high != want_high, swapped(value), value)
    return jnp.where(r < leaf_count, value, jnp.zeros_like(value))


def reply_kernel(
    count, sends, leaf_count, base, requests, prev_ref, own_ref, next_ref, first, second, nums, sems
):
    me = lax.axis_index("leaf")
    swap = is_any(me, sends)
    end, start = me == count - 2, me == 1
    up = (jnp.where(end, count - 3, jnp.minimum(me + 3, count - 1)), jnp.where(end, 3, 0))
    down = (jnp.where(start, 2, jnp.maximum(me - 3, 0)), jnp.where(start, 2, 5))
    ways = []
    for n in range(2):
        is_up = swap if n else jnp.logical_not(swap)
        target = jnp.where(is_up, up[0], down[0])
        ways.append((is_up, jnp.where(is_up, up[1], down[1])))
        pltpu.make_async_copy(requests.at[target], nums.at[n], sems.at[n]).start()
    blocks = (prev_ref, own_ref, next_ref)
    stride = first.shape[0] // 3
    for out in (first, second):
        for b, ref in enumerate(blocks):
            out[stride * b + 128 : stride * (b + 1), :] = ref[base + 16 * leaf_count :, :]
    low = low_half(32)
    for n, out in enumerate((first, second)):
        pltpu.make_async_copy(requests.at[0], nums.at[n], sems.at[n]).wait()
        is_up, row = ways[n]
        for b, ref in enumerate(blocks):
            none = (is_up & end & (b != 2)) | (jnp.logical_not(is_up) & start & (b != 0))
            for m in range(4):
                asked = [
                    jnp.where(none, leaf_count, nums[n, row + b, 2 * m + side]) for side in range(2)
                ]
                left = pick(ref, base, asked[0], leaf_count, 0)
                right = pick(ref, base, asked[1], leaf_count, 1)
                at = stride * b + 32 * m
                out[at : at + 32, :] = jnp.where(low, left, right)


def near_kernel(
    x_hbm,
    prev_ref,
    next_ref,
    near_ref,
    source_hbm,
    out_ref,
    x_ref,
    source_ref,
    held,
    twice,
    stacked,
    sems,
):
    leaf_count, leaf, depth = near_ref.shape
    count = source_hbm.shape[0]
    quads = leaf_count // 4
    copy_x = pltpu.make_async_copy(x_hbm, x_ref, sems.at[quads])
    copy_source = pltpu.make_async_copy(source_hbm, source_ref, sems.at[quads + 1])
    copy_x.start()
    copy_source.start()

    def copy(quad):
        part = pl.ds(4 * quad, 4)
        return pltpu.make_async_copy(near_ref.at[part], held.at[part], sems.at[quad])

    for quad in range(quads):
        copy(quad).start()

    low = low_half(leaf)

    def spread(value, at):
        other = swapped(value)
        twice[at] = jnp.where(low, value, other)
        twice[at + 1] = jnp.where(low, other, value)

    for tile in range(HALO // 2):
        rows = slice(64 * tile, 64 * tile + 64)
        spread(prev_ref[rows, :], 2 * tile)
        spread(next_ref[rows, :], HALO + leaf_count + 2 * tile)
    copy_x.wait()
    for tile in range(leaf_count // 2):
        spread(x_ref[:, 128 * tile : 128 * tile + 128], HALO + 2 * tile)
    copy_source.wait()

    def body(quad, carry):
        copy(quad).wait()
        slot = lax.rem(quad, 2)
        for u in range(4):
            i = 4 * quad + u
            for m in range(count // 2):
                stacked[slot, 64 * u : 64 * u + 64, 128 * m : 128 * m + 128] = jnp.where(
                    low, twice[source_ref[2 * m, i]], twice[source_ref[2 * m + 1, i]]
                )
            if count % 2:
                m = count // 2
                stacked[slot, 64 * u : 64 * u + 64, 128 * m : 128 * m + 128] = twice[
                    source_ref[count - 1, i]
                ]
        rows = held[pl.ds(4 * quad, 4)].reshape(4 * leaf, depth)
        total = matmul_nt(stacked[slot, :, :depth], rows)
        for t in range(2):
            lanes = pl.ds(pl.multiple_of(256 * quad + 128 * t, 128), 128)
            out_ref[:, lanes] = jnp.where(
                low,
                total[128 * t : 128 * t + 64, 128 * t : 128 * t + 128],
                total[128 * t + 64 : 128 * t + 128, 128 * t : 128 * t + 128],
            )
        return carry

    lax.fori_loop(0, quads, body, 0)


def down_kernel(
    count,
    takes,
    own_ref,
    prev_ref,
    next_ref,
    first_ref,
    second_ref,
    req_ref,
    coup_source,
    par_source,
    coup_ref,
    par_ref,
    diag,
    tst_ref,
    near_ref,
    out_ref,
    slots,
    window,
    weights,
):
    leaf_count, rank = coup_ref.shape[:2]
    parent_count = par_ref.shape[0]
    base = HALO // 2 * 64
    parent_base = base + 16 * leaf_count
    stride = first_ref.shape[0] // 3
    low64 = low_half(64)
    low = low_half(rank)
    me = lax.axis_index("leaf")
    swap = is_any(me, takes)

    def split(value, mask):
        other = swapped(value)
        return jnp.where(mask, value, other), jnp.where(mask, other, value)

    for quad in range(leaf_count // 4):
        at = base + 64 * quad
        first, second = split(own_ref[at : at + 64, :], low64)
        slots[4 * quad] = first[:32]
        slots[4 * quad + 1] = first[32:]
        slots[4 * quad + 2] = second[:32]
        slots[4 * quad + 3] = second[32:]
    for ref, k in ((prev_ref, 3), (next_ref, 4)):
        for c in range(8):
            r = req_ref[k, c]
            row, high = place(r, leaf_count)
            first, second = split(ref[pl.ds(base + row, 32), :], low)
            value = jnp.where(high == 0, first, second)
            slots[leaf_count + 8 * k + c] = jnp.where(
                r < leaf_count, value, jnp.zeros_like(value)
            )

    def put_parents(read, block):
        for m in range((parent_count + 1) // 2):
            first, second = split(read(m), low)
            window[parent_count * block + 2 * m] = first
            if 2 * m + 1 < parent_count:
                window[parent_count * block + 2 * m + 1] = second

    for ref, block in ((own_ref, 4), (prev_ref, 3), (next_ref, 5)):
        put_parents(lambda m: ref[parent_base + 32 * m : parent_base + 32 * m + 32, :], block)
    for way in range(2):
        def got(at):
            one, two = first_ref[at : at + 32, :], second_ref[at : at + 32, :]
            return jnp.where(swap, one, two) if way else jnp.where(swap, two, one)

        turned = me == (count - 3 if way else 2)
        for b in range(3):
            order = jnp.where(turned, 2 - b, b)
            for m in range(4):
                first, second = split(got(stride * b + 32 * m), low)
                at = leaf_count + 8 * (5 * way + order) + 2 * m
                slots[at] = first
                slots[at + 1] = second
            put_parents(lambda m: got(stride * b + 128 + 32 * m), 6 * way + order)

    per = par_source.shape[1]
    coup = coup_source.shape[0]
    for p in range(parent_count):
        stack = jnp.concatenate([window[par_source[p, j]] for j in range(per)], 0)
        parent_out = matmul(par_ref[p], stack).astype(BF)
        down = matmul(tst_ref[256 * p : 256 * p + 256, :], parent_out)
        for half in range(2):
            quad = 2 * p + half
            for j in range(coup):
                for t in range(2):
                    i = 4 * quad + 2 * t
                    weights[half, rank * j : rank * j + rank, 128 * t : 128 * t + 128] = jnp.where(
                        low, slots[coup_source[j, i]], slots[coup_source[j, i + 1]]
                    )
            rows = coup_ref[4 * quad : 4 * quad + 4].reshape(4 * rank, coup * rank)
            coupled = matmul(rows, weights[half])
            coupled = jnp.concatenate([coupled[:64, :128], coupled[64:, 128:]], 0)
            leaf_out = (coupled + down[128 * half : 128 * half + 128]).astype(BF)
            far = matmul_tn(leaf_out, diag[128 * quad : 128 * quad + 128, :])
            for t in range(2):
                lanes = slice(256 * quad + 128 * t, 256 * quad + 128 * t + 128)
                tile = jnp.where(
                    low64, far[:64, 128 * t : 128 * t + 128], far[64:, 128 * t : 128 * t + 128]
                )
                out_ref[:, lanes] = (near_ref[:, lanes] + tile).astype(BF)


def params(mib):
    return pltpu.CompilerParams(vmem_limit_bytes=mib << 20)


def cost(flops, size):
    return pl.CostEstimate(flops=flops, bytes_accessed=size, transcendentals=0)


def shards(
    rhs,
    basis,
    transfer,
    near_rows,
    near_source,
    far_request,
    coup_rows,
    coup_source,
    par_rows,
    par_source,
):
    leaf_count, leaf, rank = basis.shape
    points, rhs_count = rhs.shape
    parent_count = par_rows.shape[0]
    near_count = near_source.shape[1]
    coup_count = coup_source.shape[1]
    base = HALO // 2 * rhs_count
    parent_rows = rank * ((parent_count + 1) // 2)
    packed = base + 16 * leaf_count + parent_rows
    stride = 128 + parent_rows
    count = lax.axis_size("leaf")
    routes, sends, takes = far_routes(count)

    x = rhs.T
    trans = transfer.transpose(1, 2, 0).reshape(rank * rank, leaf_count)
    all_requests = lax.all_gather(far_request, "leaf", tiled=True)

    shape = jax.ShapeDtypeStruct
    vmem, smem, hbm = (pl.BlockSpec(memory_space=kind) for kind in (VMEM, SMEM, pltpu.HBM))
    to_next, to_prev, tst, diag = pl.pallas_call(
        up_kernel,
        out_shape=(
            shape((packed, 128), BF),
            shape((packed, 128), BF),
            shape((rank * leaf_count, rank), BF),
            shape((rank * leaf_count, 256), BF),
        ),
        in_specs=[hbm] * 3,
        out_specs=(vmem,) * 4,
        scratch_shapes=[
            VMEM(x.shape, BF),
            VMEM((leaf_count, rank, leaf), BF),
            VMEM(trans.shape, BF),
            VMEM((rank * leaf_count, 128), F32),
            DMA((3,)),
        ],
        compiler_params=params(8),
        cost_estimate=cost(10**9, 2 * 10**6),
        name="upward",
    )(x, basis.transpose(0, 2, 1), trans)

    steps = range(count - 1)
    from_prev = lax.ppermute(to_next, "leaf", [(i, i + 1) for i in steps])
    from_next = lax.ppermute(to_prev, "leaf", [(i + 1, i) for i in steps])

    replies = pl.pallas_call(
        functools.partial(reply_kernel, count, sends, leaf_count, base),
        out_shape=(shape((3 * stride, 128), BF),) * 2,
        in_specs=[hbm] + [vmem] * 3,
        out_specs=(vmem,) * 2,
        scratch_shapes=[SMEM((2, 8, 8), jnp.int32), DMA((2,))],
        compiler_params=params(8),
        cost_estimate=cost(10**8, 2 * 10**6),
        name="reply",
    )(all_requests, from_prev, to_next, from_next)

    first = lax.ppermute(replies[0], "leaf", routes[0])
    second = lax.ppermute(replies[1], "leaf", routes[1])

    near = pl.pallas_call(
        near_kernel,
        out_shape=shape((rhs_count, points), F32),
        in_specs=[hbm, vmem, vmem, hbm, hbm],
        out_specs=vmem,
        scratch_shapes=[
            VMEM(x.shape, BF),
            SMEM((near_count, leaf_count), jnp.int32),
            VMEM(near_rows.shape, BF),
            VMEM((leaf_count + 2 * HALO, leaf, 128), BF),
            VMEM((2, 256, 128 * ((near_count + 1) // 2)), BF),
            DMA((leaf_count // 4 + 2,)),
        ],
        compiler_params=params(20),
        cost_estimate=cost(8 * 10**9, 10**7),
        name="near",
    )(x, from_prev, from_next, near_rows, near_source.T)

    product = pl.pallas_call(
        functools.partial(down_kernel, count, takes),
        out_shape=shape((rhs_count, points), BF),
        in_specs=[vmem] * 5 + [smem] * 3 + [vmem] * 5,
        out_specs=vmem,
        scratch_shapes=[
            VMEM((leaf_count + 64, rank, 128), BF),
            VMEM((9 * parent_count, rank, 128), BF),
            VMEM((2, coup_count * rank, 256), BF),
        ],
        compiler_params=params(12),
        cost_estimate=cost(10**9, 4 * 10**6),
        name="downward",
    )(
        to_next,
        from_prev,
        from_next,
        first,
        second,
        far_request[0],
        coup_source.T,
        par_source,
        coup_rows,
        par_rows,
        diag,
        tst,
        near,
    )
    return product.T


def solution(mesh):
    split = ("groups", "leaf")
    return jax.shard_map(
        shards,
        mesh=mesh,
        in_specs=(
            P(split, None),
            P(split, None, None),
            P(split, None, None),
            P(split, None, None),
            P(split, None),
            P(split, None, None),
            P(split, None, None),
            P(split, None),
            P(split, None, None),
            P(split, None),
        ),
        out_specs=P(split, None),
        check_vma=False,
    )
```

```python
import functools

import jax
import jax.numpy as jnp
from jax import lax
from jax.experimental import pallas as pl
from jax.experimental.pallas import tpu as pltpu
from jax.sharding import PartitionSpec as P

HALO = 16
BF = jnp.bfloat16
F32 = jnp.float32
VMEM = pltpu.VMEM
SMEM = pltpu.SMEM
DMA = pltpu.SemaphoreType.DMA


def far_routes(count):
    by_source, by_target = [{}, {}], [{}, {}]

    def put(color, source, target):
        by_source[color][source] = target
        by_target[color][target] = source

    for i in range(count - 3):
        put(0, i, i + 3)
        put(1, i + 3, i)
    for source, target in ((count - 2, count - 3), (1, 2)):
        moving = [(0 if target not in by_target[0] else 1, source, target)]
        while moving:
            color, source, target = moving.pop()
            old_target = by_source[color].get(source)
            if old_target is not None:
                del by_target[color][old_target]
            old_source = by_target[color].get(target)
            if old_source is not None:
                del by_source[color][old_source]
            put(color, source, target)
            if old_target is not None:
                moving.append((1 - color, source, old_target))
            if old_source is not None:
                moving.append((1 - color, old_source, target))
    sends, takes = [], []
    for i in range(count):
        up = count - 3 if i == count - 2 else i + 3
        if by_source[1].get(i) == up or by_source[0].get(i, up) != up:
            sends.append(i)
        below = 1 if i == 2 else i - 3
        if by_target[1].get(i) == below or by_target[0].get(i, below) != below:
            takes.append(i)
    return [sorted(routes.items()) for routes in by_source], sends, takes


def is_any(value, numbers):
    found = value < 0
    for number in numbers:
        found = found | (value == number)
    return found


def low_half(rows):
    return lax.broadcasted_iota(jnp.int32, (rows, 128), 1) < 64


def swapped(value):
    return pltpu.roll(value, 64, 1)


def matmul(a, b):
    return jnp.dot(a, b, preferred_element_type=F32)


def matmul_nt(a, b):
    return lax.dot_general(a, b, (((1,), (1,)), ((), ())), preferred_element_type=F32)


def matmul_tn(a, b):
    return lax.dot_general(a, b, (((0,), (0,)), ((), ())), preferred_element_type=F32)


def fill_block_diagonal(basis_ref, diag):
    leaf_count, rank, leaf = basis_ref.shape
    blank = jnp.zeros((rank, leaf), BF)
    empty = jnp.zeros((rank, 2 * leaf), BF)
    for i in range(leaf_count):
        rows = slice(rank * i, rank * (i + 1))
        block = basis_ref[i]
        pair = [block, blank] if i % 2 == 0 else [blank, block]
        place = i % 4 // 2
        diag[rows, 128 * place : 128 * place + 128] = jnp.concatenate(pair, 1)
        diag[rows, 128 * (1 - place) : 128 * (1 - place) + 128] = empty


def up_kernel(x_hbm, basis_hbm, trans_hbm, to_next, to_prev, tst_ref, diag, x_ref, basis_ref, trans_ref, flat, sems):
    points = x_hbm.shape[1]
    leaf_count, rank, leaf = basis_hbm.shape
    copies = [
        pltpu.make_async_copy(source, held, sems.at[n])
        for n, (source, held) in enumerate(
            ((trans_hbm, trans_ref), (basis_hbm, basis_ref), (x_hbm, x_ref))
        )
    ]
    for copy in copies:
        copy.start()
    copies[0].wait()
    for step in range(rank // 4):
        block = trans_ref[128 * step : 128 * step + 128, :].astype(F32).T
        for q in range(4):
            piece = block if q == 0 else pltpu.roll(block, 128 - 32 * q, 1)
            flat[pl.ds(4 * step + q, leaf_count, stride=rank), :] = piece
    tst_ref[...] = flat[:, 0:rank].astype(BF)
    copies[1].wait()
    fill_block_diagonal(basis_ref, diag)
    copies[2].wait()

    base = HALO * leaf // 128 * 64
    for t in range(HALO * leaf // 128):
        rows = slice(64 * t, 64 * t + 64)
        to_prev[rows, :] = x_ref[:, 128 * t : 128 * t + 128]
        at = points - HALO * leaf + 128 * t
        to_next[rows, :] = x_ref[:, at : at + 128]

    def put(at, left, right):
        rows = left.shape[0]
        both = jnp.where(low_half(rows), left, right)
        to_next[base + at : base + at + rows, :] = both
        to_prev[base + at : base + at + rows, :] = both

    parents = []
    for p in range(leaf_count // 8):
        halves = []
        for quad in (2 * p, 2 * p + 1):
            x = x_ref[:, 256 * quad : 256 * quad + 256]
            skel = matmul_nt(
                diag[128 * quad : 128 * quad + 128, :], jnp.concatenate([x, x], 0)
            ).astype(BF)
            put(64 * quad, skel[:64], skel[64:])
            halves.append(skel)
        parents.append(
            matmul_tn(tst_ref[256 * p : 256 * p + 256, :], jnp.concatenate(halves, 0)).astype(BF)
        )
    for m in range((len(parents) + 1) // 2):
        put(16 * leaf_count + 32 * m, parents[2 * m], parents[min(2 * m + 1, len(parents) - 1)])


def place(r, leaf_count):
    safe = jnp.minimum(r, leaf_count - 1)
    return pl.multiple_of((safe >> 2) * 64 + (safe & 1) * 32, 32), (safe >> 1) & 1


def pick(ref, base, r, leaf_count, want_high):
    row, high = place(r, leaf_count)
    value = ref[pl.ds(base + row, 32), :]
    value = jnp.where(high != want_high, swapped(value), value)
    return jnp.where(r < leaf_count, value, jnp.zeros_like(value))


def reply_kernel(
    count, sends, leaf_count, base, one_ref, two_ref, prev_ref, own_ref, next_ref, first, second
):
    me = lax.axis_index("leaf")
    swap = is_any(me, sends)
    end, start = me == count - 2, me == 1
    up, down = jnp.where(end, 3, 0), jnp.where(start, 2, 5)
    blocks = (prev_ref, own_ref, next_ref)
    stride = first.shape[0] // 3
    for out in (first, second):
        for b, ref in enumerate(blocks):
            out[stride * b + 128 : stride * (b + 1), :] = ref[base + 16 * leaf_count :, :]
    low = low_half(32)
    for out, nums, is_up in ((first, one_ref, jnp.logical_not(swap)), (second, two_ref, swap)):
        row = jnp.where(is_up, up, down)
        for b, ref in enumerate(blocks):
            none = (is_up & end & (b != 2)) | (jnp.logical_not(is_up) & start & (b != 0))
            for m in range(4):
                asked = [
                    jnp.where(none, leaf_count, nums[row + b, 2 * m + side]) for side in range(2)
                ]
                left = pick(ref, base, asked[0], leaf_count, 0)
                right = pick(ref, base, asked[1], leaf_count, 1)
                at = stride * b + 32 * m
                out[at : at + 32, :] = jnp.where(low, left, right)


def near_kernel(
    x_hbm,
    prev_ref,
    next_ref,
    near_ref,
    source_hbm,
    out_ref,
    x_ref,
    source_ref,
    held,
    twice,
    even,
    odd,
    sems,
):
    leaf_count, leaf, depth = near_ref.shape
    count = source_hbm.shape[0]
    quads = leaf_count // 4
    copy_x = pltpu.make_async_copy(x_hbm, x_ref, sems.at[quads])
    copy_source = pltpu.make_async_copy(source_hbm, source_ref, sems.at[quads + 1])
    copy_x.start()
    copy_source.start()

    def copy(quad):
        part = pl.ds(4 * quad, 4)
        return pltpu.make_async_copy(near_ref.at[part], held.at[part], sems.at[quad])

    for quad in range(quads):
        copy(quad).start()

    low = low_half(leaf)

    def spread(value, at):
        other = swapped(value)
        twice[at] = jnp.where(low, value, other)
        twice[at + 1] = jnp.where(low, other, value)

    for tile in range(HALO // 2):
        rows = slice(64 * tile, 64 * tile + 64)
        spread(prev_ref[rows, :], 2 * tile)
        spread(next_ref[rows, :], HALO + leaf_count + 2 * tile)
    copy_x.wait()
    for tile in range(leaf_count // 2):
        spread(x_ref[:, 128 * tile : 128 * tile + 128], HALO + 2 * tile)
    copy_source.wait()

    def build(quad, stacked):
        for u in range(4):
            i = 4 * quad + u
            rows = slice(64 * u, 64 * u + 64)
            for m in range(count // 2):
                stacked[rows, 128 * m : 128 * m + 128] = jnp.where(
                    low, twice[source_ref[2 * m, i]], twice[source_ref[2 * m + 1, i]]
                )
            if count % 2:
                m = count // 2
                stacked[rows, 128 * m : 128 * m + 128] = twice[source_ref[count - 1, i]]

    def multiply(quad, stacked):
        rows = held[pl.ds(4 * quad, 4)].reshape(4 * leaf, depth)
        total = matmul_nt(stacked[:, :depth], rows)
        for t in range(2):
            lanes = pl.ds(pl.multiple_of(256 * quad + 128 * t, 128), 128)
            out_ref[:, lanes] = jnp.where(
                low,
                total[128 * t : 128 * t + 64, 128 * t : 128 * t + 128],
                total[128 * t + 64 : 128 * t + 128, 128 * t : 128 * t + 128],
            )

    build(0, even)

    def body(step, carry):
        quad = 2 * step
        copy(quad).wait()
        copy(quad + 1).wait()
        build(quad + 1, odd)
        multiply(quad, even)
        build(jnp.minimum(quad + 2, quads - 1), even)
        multiply(quad + 1, odd)
        return carry

    lax.fori_loop(0, quads // 2, body, 0)


def down_kernel(
    count,
    takes,
    own_ref,
    prev_ref,
    next_ref,
    first_ref,
    second_ref,
    req_ref,
    coup_source,
    par_source,
    coup_ref,
    par_ref,
    diag,
    tst_ref,
    near_ref,
    out_ref,
    slots,
    window,
    weights,
):
    leaf_count, rank = coup_ref.shape[:2]
    parent_count = par_ref.shape[0]
    base = HALO // 2 * 64
    parent_base = base + 16 * leaf_count
    stride = first_ref.shape[0] // 3
    low64 = low_half(64)
    low = low_half(rank)
    me = lax.axis_index("leaf")
    swap = is_any(me, takes)

    def split(value, mask):
        other = swapped(value)
        return jnp.where(mask, value, other), jnp.where(mask, other, value)

    for quad in range(leaf_count // 4):
        at = base + 64 * quad
        first, second = split(own_ref[at : at + 64, :], low64)
        slots[4 * quad] = first[:32]
        slots[4 * quad + 1] = first[32:]
        slots[4 * quad + 2] = second[:32]
        slots[4 * quad + 3] = second[32:]
    for ref, k in ((prev_ref, 3), (next_ref, 4)):
        for c in range(8):
            r = req_ref[k, c]
            row, high = place(r, leaf_count)
            first, second = split(ref[pl.ds(base + row, 32), :], low)
            value = jnp.where(high == 0, first, second)
            slots[leaf_count + 8 * k + c] = jnp.where(
                r < leaf_count, value, jnp.zeros_like(value)
            )

    def put_parents(read, block):
        for m in range((parent_count + 1) // 2):
            first, second = split(read(m), low)
            window[parent_count * block + 2 * m] = first
            if 2 * m + 1 < parent_count:
                window[parent_count * block + 2 * m + 1] = second

    for ref, block in ((own_ref, 4), (prev_ref, 3), (next_ref, 5)):
        put_parents(lambda m: ref[parent_base + 32 * m : parent_base + 32 * m + 32, :], block)
    for way in range(2):
        def got(at):
            one, two = first_ref[at : at + 32, :], second_ref[at : at + 32, :]
            return jnp.where(swap, one, two) if way else jnp.where(swap, two, one)

        turned = me == (count - 3 if way else 2)
        for b in range(3):
            order = jnp.where(turned, 2 - b, b)
            for m in range(4):
                first, second = split(got(stride * b + 32 * m), low)
                at = leaf_count + 8 * (5 * way + order) + 2 * m
                slots[at] = first
                slots[at + 1] = second
            put_parents(lambda m: got(stride * b + 128 + 32 * m), 6 * way + order)

    per = par_source.shape[1]
    coup = coup_source.shape[0]
    for p in range(parent_count):
        stack = jnp.concatenate([window[par_source[p, j]] for j in range(per)], 0)
        parent_out = matmul(par_ref[p], stack).astype(BF)
        down = matmul(tst_ref[256 * p : 256 * p + 256, :], parent_out)
        for half in range(2):
            quad = 2 * p + half
            for j in range(coup):
                for t in range(2):
                    i = 4 * quad + 2 * t
                    weights[half, rank * j : rank * j + rank, 128 * t : 128 * t + 128] = jnp.where(
                        low, slots[coup_source[j, i]], slots[coup_source[j, i + 1]]
                    )
            rows = coup_ref[4 * quad : 4 * quad + 4].reshape(4 * rank, coup * rank)
            coupled = matmul(rows, weights[half])
            coupled = jnp.concatenate([coupled[:64, :128], coupled[64:, 128:]], 0)
            leaf_out = (coupled + down[128 * half : 128 * half + 128]).astype(BF)
            far = matmul_tn(leaf_out, diag[128 * quad : 128 * quad + 128, :])
            for t in range(2):
                lanes = slice(256 * quad + 128 * t, 256 * quad + 128 * t + 128)
                tile = jnp.where(
                    low64, far[:64, 128 * t : 128 * t + 128], far[64:, 128 * t : 128 * t + 128]
                )
                out_ref[:, lanes] = (near_ref[:, lanes] + tile).astype(BF)


def in_hbm(array):
    return pltpu.with_memory_space_constraint(array, pltpu.HBM)


def params(mib):
    return pltpu.CompilerParams(vmem_limit_bytes=mib << 20)


def cost(flops, size):
    return pl.CostEstimate(flops=flops, bytes_accessed=size, transcendentals=0)


def shards(
    rhs,
    basis,
    transfer,
    near_rows,
    near_source,
    far_request,
    coup_rows,
    coup_source,
    par_rows,
    par_source,
):
    leaf_count, leaf, rank = basis.shape
    points, rhs_count = rhs.shape
    parent_count = par_rows.shape[0]
    near_count = near_source.shape[1]
    coup_count = coup_source.shape[1]
    base = HALO // 2 * rhs_count
    parent_rows = rank * ((parent_count + 1) // 2)
    packed = base + 16 * leaf_count + parent_rows
    stride = 128 + parent_rows
    count = lax.axis_size("leaf")
    routes, sends, takes = far_routes(count)

    x = rhs.T
    trans = transfer.transpose(1, 2, 0).reshape(rank * rank, leaf_count)
    requests = far_request[0]
    asked = [lax.ppermute(requests, "leaf", [(b, a) for a, b in route]) for route in routes]

    shape = jax.ShapeDtypeStruct
    vmem, smem, hbm = (pl.BlockSpec(memory_space=kind) for kind in (VMEM, SMEM, pltpu.HBM))
    to_next, to_prev, tst, diag = pl.pallas_call(
        up_kernel,
        out_shape=(
            shape((packed, 128), BF),
            shape((packed, 128), BF),
            shape((rank * leaf_count, rank), BF),
            shape((rank * leaf_count, 256), BF),
        ),
        in_specs=[hbm] * 3,
        out_specs=(vmem,) * 4,
        scratch_shapes=[
            VMEM(x.shape, BF),
            VMEM((leaf_count, rank, leaf), BF),
            VMEM(trans.shape, BF),
            VMEM((rank * leaf_count, 128), F32),
            DMA((3,)),
        ],
        compiler_params=params(8),
        cost_estimate=cost(10**9, 2 * 10**6),
        name="upward",
    )(in_hbm(x), in_hbm(basis.transpose(0, 2, 1)), in_hbm(trans))

    steps = range(count - 1)
    from_prev = lax.ppermute(to_next, "leaf", [(i, i + 1) for i in steps])
    from_next = lax.ppermute(to_prev, "leaf", [(i + 1, i) for i in steps])

    replies = pl.pallas_call(
        functools.partial(reply_kernel, count, sends, leaf_count, base),
        out_shape=(shape((3 * stride, 128), BF),) * 2,
        in_specs=[smem] * 2 + [vmem] * 3,
        out_specs=(vmem,) * 2,
        compiler_params=params(8),
        cost_estimate=cost(10**8, 2 * 10**6),
        name="reply",
    )(*asked, from_prev, to_next, from_next)

    first = lax.ppermute(replies[0], "leaf", routes[0])
    second = lax.ppermute(replies[1], "leaf", routes[1])

    near = pl.pallas_call(
        near_kernel,
        out_shape=shape((rhs_count, points), F32),
        in_specs=[hbm, vmem, vmem, hbm, hbm],
        out_specs=vmem,
        scratch_shapes=[
            VMEM(x.shape, BF),
            SMEM((near_count, leaf_count), jnp.int32),
            VMEM(near_rows.shape, BF),
            VMEM((leaf_count + 2 * HALO, leaf, 128), BF),
            VMEM((256, 128 * ((near_count + 1) // 2)), BF),
            VMEM((256, 128 * ((near_count + 1) // 2)), BF),
            DMA((leaf_count // 4 + 2,)),
        ],
        compiler_params=params(20),
        cost_estimate=cost(8 * 10**9, 10**7),
        name="near",
    )(in_hbm(x), from_prev, from_next, in_hbm(near_rows), in_hbm(near_source.T))

    product = pl.pallas_call(
        functools.partial(down_kernel, count, takes),
        out_shape=shape((rhs_count, points), BF),
        in_specs=[vmem] * 5 + [smem] * 3 + [vmem] * 5,
        out_specs=vmem,
        scratch_shapes=[
            VMEM((leaf_count + 64, rank, 128), BF),
            VMEM((9 * parent_count, rank, 128), BF),
            VMEM((2, coup_count * rank, 256), BF),
        ],
        compiler_params=params(12),
        cost_estimate=cost(10**9, 4 * 10**6),
        name="downward",
    )(
        to_next,
        from_prev,
        from_next,
        first,
        second,
        requests,
        coup_source.T,
        par_source,
        coup_rows,
        par_rows,
        diag,
        tst,
        near,
    )
    return product.T


def solution(mesh):
    split = ("groups", "leaf")
    return jax.shard_map(
        shards,
        mesh=mesh,
        in_specs=(
            P(split, None),
            P(split, None, None),
            P(split, None, None),
            P(split, None, None),
            P(split, None),
            P(split, None, None),
            P(split, None, None),
            P(split, None),
            P(split, None, None),
            P(split, None),
        ),
        out_specs=P(split, None),
        check_vma=False,
    )
```

```python
import functools

import jax
import jax.numpy as jnp
from jax import lax
from jax.experimental import pallas as pl
from jax.experimental.pallas import tpu as pltpu
from jax.sharding import PartitionSpec as P

HALO = 16
BF = jnp.bfloat16
F32 = jnp.float32
VMEM = pltpu.VMEM
SMEM = pltpu.SMEM
DMA = pltpu.SemaphoreType.DMA


def low_half(rows):
    return lax.broadcasted_iota(jnp.int32, (rows, 128), 1) < 64


def swapped(value):
    return pltpu.roll(value, 64, 1)


def matmul(a, b):
    return jnp.dot(a, b, preferred_element_type=F32)


def matmul_nt(a, b):
    return lax.dot_general(a, b, (((1,), (1,)), ((), ())), preferred_element_type=F32)


def matmul_tn(a, b):
    return lax.dot_general(a, b, (((0,), (0,)), ((), ())), preferred_element_type=F32)


def fill_block_diagonal(basis_ref, diag):
    leaf_count, rank, leaf = basis_ref.shape
    blank = jnp.zeros((rank, leaf), BF)
    empty = jnp.zeros((rank, 2 * leaf), BF)
    for i in range(leaf_count):
        rows = slice(rank * i, rank * (i + 1))
        block = basis_ref[i]
        pair = [block, blank] if i % 2 == 0 else [blank, block]
        place = i % 4 // 2
        diag[rows, 128 * place : 128 * place + 128] = jnp.concatenate(pair, 1)
        diag[rows, 128 * (1 - place) : 128 * (1 - place) + 128] = empty


def up_kernel(x_hbm, basis_hbm, trans_hbm, one, two, tst_ref, diag, x_ref, basis_ref, trans_ref, flat, sems):
    points = x_hbm.shape[1]
    leaf_count, rank, leaf = basis_hbm.shape
    copies = [
        pltpu.make_async_copy(source, held, sems.at[n])
        for n, (source, held) in enumerate(
            ((trans_hbm, trans_ref), (basis_hbm, basis_ref), (x_hbm, x_ref))
        )
    ]
    for copy in copies:
        copy.start()
    copies[0].wait()
    for step in range(rank // 4):
        block = trans_ref[128 * step : 128 * step + 128, :].astype(F32).T
        for q in range(4):
            piece = block if q == 0 else pltpu.roll(block, 128 - 32 * q, 1)
            flat[pl.ds(4 * step + q, leaf_count, stride=rank), :] = piece
    tst_ref[...] = flat[:, 0:rank].astype(BF)
    copies[1].wait()
    fill_block_diagonal(basis_ref, diag)
    copies[2].wait()

    odd = lax.rem(lax.axis_index("leaf"), 2) == 1
    base = HALO * leaf // 128 * 64
    for t in range(HALO * leaf // 128):
        rows = slice(64 * t, 64 * t + 64)
        at = points - HALO * leaf + 128 * t
        head, tail = x_ref[:, 128 * t : 128 * t + 128], x_ref[:, at : at + 128]
        one[rows, :] = jnp.where(odd, head, tail)
        two[rows, :] = jnp.where(odd, tail, head)

    def put(at, left, right):
        rows = left.shape[0]
        both = jnp.where(low_half(rows), left, right)
        one[base + at : base + at + rows, :] = both
        two[base + at : base + at + rows, :] = both

    parents = []
    for p in range(leaf_count // 8):
        halves = []
        for quad in (2 * p, 2 * p + 1):
            x = x_ref[:, 256 * quad : 256 * quad + 256]
            skel = matmul_nt(
                diag[128 * quad : 128 * quad + 128, :], jnp.concatenate([x, x], 0)
            ).astype(BF)
            put(64 * quad, skel[:64], skel[64:])
            halves.append(skel)
        parents.append(
            matmul_tn(tst_ref[256 * p : 256 * p + 256, :], jnp.concatenate(halves, 0)).astype(BF)
        )
    for m in range((len(parents) + 1) // 2):
        put(16 * leaf_count + 32 * m, parents[2 * m], parents[min(2 * m + 1, len(parents) - 1)])


def place(r, leaf_count):
    safe = jnp.minimum(r, leaf_count - 1)
    return pl.multiple_of((safe >> 2) * 64 + (safe & 1) * 32, 32), (safe >> 1) & 1


def relay_kernel(count, base, one_ref, own_ref, two_ref, out_ref):
    size = out_ref.shape[0] // 3
    me = lax.axis_index("leaf")
    edge = (me == 0) | (me == count - 1)
    out_ref[:size, :] = one_ref[base:, :]
    out_ref[size : 2 * size, :] = own_ref[base:, :]
    out_ref[2 * size :, :] = jnp.where(edge, own_ref[base:, :], two_ref[base:, :])


def near_kernel(
    x_hbm,
    one_ref,
    two_ref,
    near_ref,
    source_hbm,
    out_ref,
    x_ref,
    source_ref,
    held,
    twice,
    pair_a,
    pair_b,
    sems,
):
    leaf_count, leaf, depth = near_ref.shape
    count = source_hbm.shape[0]
    quads = leaf_count // 4
    copy_x = pltpu.make_async_copy(x_hbm, x_ref, sems.at[quads])
    copy_source = pltpu.make_async_copy(source_hbm, source_ref, sems.at[quads + 1])
    copy_x.start()
    copy_source.start()

    def copy(quad):
        part = pl.ds(4 * quad, 4)
        return pltpu.make_async_copy(near_ref.at[part], held.at[part], sems.at[quad])

    for quad in range(quads):
        copy(quad).start()

    low = low_half(leaf)

    def spread(value, at):
        other = swapped(value)
        twice[at] = jnp.where(low, value, other)
        twice[at + 1] = jnp.where(low, other, value)

    odd = lax.rem(lax.axis_index("leaf"), 2) == 1
    after = HALO + leaf_count
    at_one, at_two = jnp.where(odd, 0, after), jnp.where(odd, after, 0)
    for tile in range(HALO // 2):
        rows = slice(64 * tile, 64 * tile + 64)
        spread(one_ref[rows, :], at_one + 2 * tile)
        spread(two_ref[rows, :], at_two + 2 * tile)
    copy_x.wait()
    for tile in range(leaf_count // 2):
        spread(x_ref[:, 128 * tile : 128 * tile + 128], HALO + 2 * tile)
    copy_source.wait()

    def build(quad, stacked):
        for u in range(4):
            i = 4 * quad + u
            rows = slice(64 * u, 64 * u + 64)
            for m in range(count // 2):
                stacked[rows, 128 * m : 128 * m + 128] = jnp.where(
                    low, twice[source_ref[2 * m, i]], twice[source_ref[2 * m + 1, i]]
                )
            if count % 2:
                m = count // 2
                stacked[rows, 128 * m : 128 * m + 128] = twice[source_ref[count - 1, i]]

    def multiply(quad, stacked):
        rows = held[pl.ds(4 * quad, 4)].reshape(4 * leaf, depth)
        total = matmul_nt(stacked[:, :depth], rows)
        for t in range(2):
            lanes = pl.ds(pl.multiple_of(256 * quad + 128 * t, 128), 128)
            out_ref[:, lanes] = jnp.where(
                low,
                total[128 * t : 128 * t + 64, 128 * t : 128 * t + 128],
                total[128 * t + 64 : 128 * t + 128, 128 * t : 128 * t + 128],
            )

    build(0, pair_a)

    def body(step, carry):
        quad = 2 * step
        copy(quad).wait()
        copy(quad + 1).wait()
        build(quad + 1, pair_b)
        multiply(quad, pair_a)
        build(jnp.minimum(quad + 2, quads - 1), pair_a)
        multiply(quad + 1, pair_b)
        return carry

    lax.fori_loop(0, quads // 2, body, 0)


def down_kernel(
    own_ref,
    one_ref,
    two_ref,
    far_ref,
    over_ref,
    far_over_ref,
    req_ref,
    coup_source,
    par_source,
    coup_ref,
    par_ref,
    diag,
    tst_ref,
    near_ref,
    out_ref,
    slots,
    window,
    weights,
    stack,
    outs,
):
    leaf_count, rank = coup_ref.shape[:2]
    parent_count = par_ref.shape[0]
    base = HALO // 2 * 64
    size = far_ref.shape[0] // 3
    low64 = low_half(64)
    low = low_half(rank)
    odd = lax.rem(lax.axis_index("leaf"), 2) == 1

    def split(value, mask):
        other = swapped(value)
        return jnp.where(mask, value, other), jnp.where(mask, other, value)

    for quad in range(leaf_count // 4):
        at = base + 64 * quad
        first, second = split(own_ref[at : at + 64, :], low64)
        slots[4 * quad] = first[:32]
        slots[4 * quad + 1] = first[32:]
        slots[4 * quad + 2] = second[:32]
        slots[4 * quad + 3] = second[32:]

    def put_parents(ref, at, block):
        for m in range((parent_count + 1) // 2):
            first, second = split(ref[at + 32 * m : at + 32 * m + 32, :], low)
            window[parent_count * block + 2 * m] = first
            if 2 * m + 1 < parent_count:
                window[parent_count * block + 2 * m + 1] = second

    put_parents(own_ref, base + 16 * leaf_count, 4)
    outer = ((two_ref, base), (far_ref, 2 * size), (far_ref, size), (far_ref, 0))
    inner = ((one_ref, base), (over_ref, base), (far_over_ref, 2 * size), (far_over_ref, size))
    for side, up in ((outer, odd), (inner, jnp.logical_not(odd))):
        for n, (ref, at) in enumerate(side):
            k = jnp.where(up, 4 + n, 3 - n)
            for c in range(8):
                r = req_ref[k, c]
                row, high = place(r, leaf_count)
                value = ref[pl.ds(at + row, 32), :]
                other = swapped(value)
                value = jnp.where(low == (high == 0), value, other)
                slots[leaf_count + 8 * k + c] = jnp.where(
                    r < leaf_count, value, jnp.zeros_like(value)
                )
            put_parents(ref, at + 16 * leaf_count, jnp.where(up, 5 + n, 3 - n))

    per = par_source.shape[1]
    coup = coup_source.shape[0]
    for j in range(per):
        for m in range((parent_count + 1) // 2):
            p, q = 2 * m, min(2 * m + 1, parent_count - 1)
            stack[rank * j : rank * j + rank, 128 * m : 128 * m + 128] = jnp.where(
                low, window[par_source[p, j]], window[par_source[q, j]]
            )
    rows = par_ref[...].reshape(parent_count * rank, per * rank)
    parent_outs = matmul(rows, stack[...]).astype(BF)
    for p in range(parent_count):
        tile = parent_outs[rank * p : rank * p + rank, 128 * (p // 2) : 128 * (p // 2) + 128]
        outs[p] = split(tile, low)[p % 2]

    def body(p, carry):
        down = matmul(tst_ref[pl.ds(pl.multiple_of(256 * p, 256), 256), :], outs[p])
        for half in range(2):
            quad = 2 * p + half
            for j in range(coup):
                for t in range(2):
                    i = 4 * quad + 2 * t
                    weights[half, rank * j : rank * j + rank, 128 * t : 128 * t + 128] = jnp.where(
                        low, slots[coup_source[j, i]], slots[coup_source[j, i + 1]]
                    )
        for half in range(2):
            quad = 2 * p + half
            rows = coup_ref[pl.ds(4 * quad, 4)].reshape(4 * rank, coup * rank)
            coupled = matmul(rows, weights[half])
            coupled = jnp.concatenate([coupled[:64, :128], coupled[64:, 128:]], 0)
            leaf_out = (coupled + down[128 * half : 128 * half + 128]).astype(BF)
            far = matmul_tn(leaf_out, diag[pl.ds(pl.multiple_of(128 * quad, 128), 128), :])
            for t in range(2):
                lanes = pl.ds(pl.multiple_of(256 * quad + 128 * t, 128), 128)
                tile = jnp.where(
                    low64, far[:64, 128 * t : 128 * t + 128], far[64:, 128 * t : 128 * t + 128]
                )
                out_ref[:, lanes] = (near_ref[:, lanes] + tile).astype(BF)
        return carry

    lax.fori_loop(0, parent_count, body, 0)


def in_hbm(array):
    return pltpu.with_memory_space_constraint(array, pltpu.HBM)


def params(mib):
    return pltpu.CompilerParams(vmem_limit_bytes=mib << 20)


def cost(flops, size):
    return pl.CostEstimate(flops=flops, bytes_accessed=size, transcendentals=0)


def shards(
    rhs,
    basis,
    transfer,
    near_rows,
    near_source,
    far_request,
    coup_rows,
    coup_source,
    par_rows,
    par_source,
):
    leaf_count, leaf, rank = basis.shape
    points, rhs_count = rhs.shape
    parent_count = par_rows.shape[0]
    near_count = near_source.shape[1]
    coup_count = coup_source.shape[1]
    base = HALO // 2 * rhs_count
    parent_rows = rank * ((parent_count + 1) // 2)
    packed = base + 16 * leaf_count + parent_rows
    count = lax.axis_size("leaf")

    x = rhs.T
    trans = transfer.transpose(1, 2, 0).reshape(rank * rank, leaf_count)
    shape = jax.ShapeDtypeStruct
    vmem, smem, hbm = (pl.BlockSpec(memory_space=kind) for kind in (VMEM, SMEM, pltpu.HBM))
    own_one, own_two, tst, diag = pl.pallas_call(
        up_kernel,
        out_shape=(
            shape((packed, 128), BF),
            shape((packed, 128), BF),
            shape((rank * leaf_count, rank), BF),
            shape((rank * leaf_count, 256), BF),
        ),
        in_specs=[hbm] * 3,
        out_specs=(vmem,) * 4,
        scratch_shapes=[
            VMEM(x.shape, BF),
            VMEM((leaf_count, rank, leaf), BF),
            VMEM(trans.shape, BF),
            VMEM((rank * leaf_count, 128), F32),
            DMA((3,)),
        ],
        compiler_params=params(8),
        cost_estimate=cost(10**9, 2 * 10**6),
        name="upward",
    )(in_hbm(x), in_hbm(basis.transpose(0, 2, 1)), in_hbm(trans))

    def exchange(block, begin, distance=1, more=()):
        pairs = [(i, i + distance) for i in range(begin, count - distance, 2)]
        return lax.ppermute(block, "leaf", pairs + [(b, a) for a, b in pairs] + list(more))

    one = exchange(own_one, 0)
    two = exchange(own_two, 1)
    bundle = pl.pallas_call(
        functools.partial(relay_kernel, count, base),
        out_shape=shape((3 * (packed - base), 128), BF),
        in_specs=[vmem] * 3,
        out_specs=vmem,
        compiler_params=params(8),
        cost_estimate=cost(10**6, 2 * 10**6),
        name="relay",
    )(one, own_one, two)
    far = exchange(bundle, 1, 3, ((0, 2), (count - 1, count - 3)))
    over = exchange(two, 0)
    near = pl.pallas_call(
        near_kernel,
        out_shape=shape((rhs_count, points), F32),
        in_specs=[hbm, vmem, vmem, hbm, hbm],
        out_specs=vmem,
        scratch_shapes=[
            VMEM(x.shape, BF),
            SMEM((near_count, leaf_count), jnp.int32),
            VMEM(near_rows.shape, BF),
            VMEM((leaf_count + 2 * HALO, leaf, 128), BF),
            VMEM((256, 128 * ((near_count + 1) // 2)), BF),
            VMEM((256, 128 * ((near_count + 1) // 2)), BF),
            DMA((leaf_count // 4 + 2,)),
        ],
        compiler_params=params(20),
        cost_estimate=cost(8 * 10**9, 10**7),
        name="near",
    )(in_hbm(x), one, two, in_hbm(near_rows), in_hbm(near_source.T))

    far, near = lax.optimization_barrier((far, near))
    far_over = exchange(far, 0)

    product = pl.pallas_call(
        down_kernel,
        out_shape=shape((rhs_count, points), BF),
        in_specs=[vmem] * 6 + [smem] * 3 + [vmem] * 5,
        out_specs=vmem,
        scratch_shapes=[
            VMEM((leaf_count + 64, rank, 128), BF),
            VMEM((9 * parent_count, rank, 128), BF),
            VMEM((2, coup_count * rank, 256), BF),
            VMEM((par_source.shape[1] * rank, 128 * ((parent_count + 1) // 2)), BF),
            VMEM((parent_count, rank, 128), BF),
        ],
        compiler_params=params(12),
        cost_estimate=cost(10**9, 4 * 10**6),
        name="downward",
    )(
        own_one,
        one,
        two,
        far,
        over,
        far_over,
        far_request[0],
        coup_source.T,
        par_source,
        coup_rows,
        par_rows,
        diag,
        tst,
        near,
    )
    return product.T


def solution(mesh):
    split = ("groups", "leaf")
    return jax.shard_map(
        shards,
        mesh=mesh,
        in_specs=(
            P(split, None),
            P(split, None, None),
            P(split, None, None),
            P(split, None, None),
            P(split, None),
            P(split, None, None),
            P(split, None, None),
            P(split, None),
            P(split, None, None),
            P(split, None),
        ),
        out_specs=P(split, None),
        check_vma=False,
    )
```

```python
import functools

import jax
import jax.numpy as jnp
from jax import lax
from jax.experimental import pallas as pl
from jax.experimental.pallas import tpu as pltpu
from jax.sharding import PartitionSpec as P

HALO = 16
BF = jnp.bfloat16
F32 = jnp.float32
VMEM = pltpu.VMEM
SMEM = pltpu.SMEM
DMA = pltpu.SemaphoreType.DMA


def low_half(rows):
    return lax.broadcasted_iota(jnp.int32, (rows, 128), 1) < 64


def swapped(value):
    return pltpu.roll(value, 64, 1)


def matmul(a, b):
    return jnp.dot(a, b, preferred_element_type=F32)


def matmul_nt(a, b):
    return lax.dot_general(a, b, (((1,), (1,)), ((), ())), preferred_element_type=F32)


def matmul_tn(a, b):
    return lax.dot_general(a, b, (((0,), (0,)), ((), ())), preferred_element_type=F32)


def fill_block_diagonal(basis_ref, diag):
    leaf_count, rank, leaf = basis_ref.shape
    blank = jnp.zeros((rank, leaf), BF)
    empty = jnp.zeros((rank, 2 * leaf), BF)
    for i in range(leaf_count):
        at = 128 * (1 - i % 4 // 2)
        diag[rank * i : rank * (i + 1), at : at + 128] = empty
    for first in range(0, leaf_count, 8):
        tiles = []
        for i in range(first, first + 8):
            block = basis_ref[i]
            tiles.append(jnp.concatenate([blank, block] if i % 2 else [block, blank], 1))
        for i, tile in enumerate(tiles, first):
            at = 128 * (i % 4 // 2)
            diag[rank * i : rank * (i + 1), at : at + 128] = tile


def up_kernel(x_hbm, basis_hbm, trans_hbm, one, two, tst_ref, diag, x_ref, basis_ref, trans_ref, flat, sems):
    points = x_hbm.shape[1]
    leaf_count, rank, leaf = basis_hbm.shape
    copies = [
        pltpu.make_async_copy(source, held, sems.at[n])
        for n, (source, held) in enumerate(
            ((trans_hbm, trans_ref), (basis_hbm, basis_ref), (x_hbm, x_ref))
        )
    ]
    for copy in copies:
        copy.start()
    copies[0].wait()
    for first in range(0, rank // 4, 4):
        blocks = [
            trans_ref[128 * step : 128 * step + 128, :].astype(F32).T
            for step in range(first, first + 4)
        ]
        for q in range(4):
            pieces = [block if q == 0 else pltpu.roll(block, 128 - 32 * q, 1) for block in blocks]
            for step, piece in enumerate(pieces, first):
                flat[pl.ds(4 * step + q, leaf_count, stride=rank), :] = piece
    tst_ref[...] = flat[:, 0:rank].astype(BF)
    copies[1].wait()
    fill_block_diagonal(basis_ref, diag)
    copies[2].wait()

    odd = lax.rem(lax.axis_index("leaf"), 2) == 1
    base = HALO * leaf // 128 * 64
    for t in range(HALO * leaf // 128):
        rows = slice(64 * t, 64 * t + 64)
        at = points - HALO * leaf + 128 * t
        head, tail = x_ref[:, 128 * t : 128 * t + 128], x_ref[:, at : at + 128]
        one[rows, :] = jnp.where(odd, head, tail)
        two[rows, :] = jnp.where(odd, tail, head)

    def put(at, left, right):
        rows = left.shape[0]
        both = jnp.where(low_half(rows), left, right)
        one[base + at : base + at + rows, :] = both
        two[base + at : base + at + rows, :] = both

    parent_count = leaf_count // 8
    skels = []
    for quad in range(leaf_count // 4):
        x = x_ref[:, 256 * quad : 256 * quad + 256]
        skels.append(
            matmul_nt(
                diag[128 * quad : 128 * quad + 128, :], jnp.concatenate([x, x], 0)
            ).astype(BF)
        )
    parents = [
        matmul_tn(
            tst_ref[256 * p : 256 * p + 256, :], jnp.concatenate(skels[2 * p : 2 * p + 2], 0)
        ).astype(BF)
        for p in range(parent_count)
    ]
    for quad, skel in enumerate(skels):
        put(64 * quad, skel[:64], skel[64:])
    for m in range((parent_count + 1) // 2):
        put(16 * leaf_count + 32 * m, parents[2 * m], parents[min(2 * m + 1, parent_count - 1)])


def place(r, leaf_count):
    safe = jnp.minimum(r, leaf_count - 1)
    return pl.multiple_of((safe >> 2) * 64 + (safe & 1) * 32, 32), (safe >> 1) & 1


def relay_kernel(count, base, one_ref, own_ref, two_ref, out_ref):
    size = out_ref.shape[0] // 3
    me = lax.axis_index("leaf")
    edge = (me == 0) | (me == count - 1)
    out_ref[:size, :] = one_ref[base:, :]
    out_ref[size : 2 * size, :] = own_ref[base:, :]
    out_ref[2 * size :, :] = jnp.where(edge, own_ref[base:, :], two_ref[base:, :])


def near_kernel(
    x_hbm,
    one_ref,
    two_ref,
    near_ref,
    source_hbm,
    out_ref,
    x_ref,
    source_ref,
    held,
    twice,
    pair_a,
    pair_b,
    sems,
):
    leaf_count, leaf, depth = near_ref.shape
    count = source_hbm.shape[0]
    quads = leaf_count // 4
    copy_x = pltpu.make_async_copy(x_hbm, x_ref, sems.at[quads])
    copy_source = pltpu.make_async_copy(source_hbm, source_ref, sems.at[quads + 1])
    copy_x.start()
    copy_source.start()

    def copy(quad):
        part = pl.ds(4 * quad, 4)
        return pltpu.make_async_copy(near_ref.at[part], held.at[part], sems.at[quad])

    for quad in range(quads):
        copy(quad).start()

    low = low_half(leaf)

    def spread(parts):
        others = [swapped(value) for value, _ in parts]
        for (value, at), other in zip(parts, others):
            twice[at] = jnp.where(low, value, other)
            twice[at + 1] = jnp.where(low, other, value)

    odd = lax.rem(lax.axis_index("leaf"), 2) == 1
    after = HALO + leaf_count
    at_one, at_two = jnp.where(odd, 0, after), jnp.where(odd, after, 0)
    for ref, at in ((one_ref, at_one), (two_ref, at_two)):
        spread([(ref[64 * n : 64 * n + 64, :], at + 2 * n) for n in range(HALO // 2)])
    copy_x.wait()
    for first in range(0, leaf_count // 2, 5):
        spread(
            [(x_ref[:, 128 * n : 128 * n + 128], HALO + 2 * n) for n in range(first, first + 5)]
        )
    copy_source.wait()

    def build(quad, stacked):
        for u in range(4):
            i = 4 * quad + u
            rows = slice(64 * u, 64 * u + 64)
            pairs = [(2 * m, min(2 * m + 1, count - 1)) for m in range((count + 1) // 2)]
            for first in range(0, len(pairs), 5):
                some = pairs[first : first + 5]
                loaded = [(twice[source_ref[a, i]], twice[source_ref[b, i]]) for a, b in some]
                for m, (left, right) in enumerate(loaded, first):
                    stacked[rows, 128 * m : 128 * m + 128] = jnp.where(low, left, right)

    def multiply(quad, stacked):
        rows = held[pl.ds(4 * quad, 4)].reshape(4 * leaf, depth)
        total = matmul_nt(stacked[:, :depth], rows)
        for t in range(2):
            lanes = pl.ds(pl.multiple_of(256 * quad + 128 * t, 128), 128)
            out_ref[:, lanes] = jnp.where(
                low,
                total[128 * t : 128 * t + 64, 128 * t : 128 * t + 128],
                total[128 * t + 64 : 128 * t + 128, 128 * t : 128 * t + 128],
            )

    build(0, pair_a)

    def body(step, carry):
        quad = 2 * step
        copy(quad).wait()
        copy(quad + 1).wait()
        build(quad + 1, pair_b)
        multiply(quad, pair_a)
        build(jnp.minimum(quad + 2, quads - 1), pair_a)
        multiply(quad + 1, pair_b)
        return carry

    lax.fori_loop(0, quads // 2, body, 0)


def down_kernel(
    own_ref,
    one_ref,
    two_ref,
    far_ref,
    over_ref,
    far_over_ref,
    req_ref,
    coup_source,
    par_source,
    coup_ref,
    par_ref,
    diag,
    tst_ref,
    near_ref,
    out_ref,
    slots,
    window,
    weights,
    stack,
    outs,
    leaf_outs,
):
    leaf_count, rank = coup_ref.shape[:2]
    parent_count = par_ref.shape[0]
    base = HALO // 2 * 64
    size = far_ref.shape[0] // 3
    low64 = low_half(64)
    low = low_half(rank)
    odd = lax.rem(lax.axis_index("leaf"), 2) == 1

    def split(value, mask):
        other = swapped(value)
        return jnp.where(mask, value, other), jnp.where(mask, other, value)

    for first in range(0, leaf_count // 4, 5):
        quads = range(first, first + 5)
        values = [own_ref[base + 64 * quad : base + 64 * quad + 64, :] for quad in quads]
        for quad, (left, right) in zip(quads, [split(value, low64) for value in values]):
            slots[4 * quad] = left[:32]
            slots[4 * quad + 1] = left[32:]
            slots[4 * quad + 2] = right[:32]
            slots[4 * quad + 3] = right[32:]

    def put_parents(ref, at, block):
        tiles = range((parent_count + 1) // 2)
        values = [ref[at + 32 * m : at + 32 * m + 32, :] for m in tiles]
        for m, (left, right) in zip(tiles, [split(value, low) for value in values]):
            window[parent_count * block + 2 * m] = left
            if 2 * m + 1 < parent_count:
                window[parent_count * block + 2 * m + 1] = right

    put_parents(own_ref, base + 16 * leaf_count, 4)
    outer = ((two_ref, base), (far_ref, 2 * size), (far_ref, size), (far_ref, 0))
    inner = ((one_ref, base), (over_ref, base), (far_over_ref, 2 * size), (far_over_ref, size))
    for side, up in ((outer, odd), (inner, jnp.logical_not(odd))):
        for n, (ref, at) in enumerate(side):
            k = jnp.where(up, 4 + n, 3 - n)
            asked = [req_ref[k, c] for c in range(8)]
            places = [place(r, leaf_count) for r in asked]
            values = [ref[pl.ds(at + row, 32), :] for row, _ in places]
            others = [swapped(value) for value in values]
            for c, r in enumerate(asked):
                value = jnp.where(low == (places[c][1] == 0), values[c], others[c])
                slots[leaf_count + 8 * k + c] = jnp.where(
                    r < leaf_count, value, jnp.zeros_like(value)
                )
            put_parents(ref, at + 16 * leaf_count, jnp.where(up, 5 + n, 3 - n))

    per = par_source.shape[1]
    coup = coup_source.shape[0]
    pairs = [(2 * m, min(2 * m + 1, parent_count - 1)) for m in range((parent_count + 1) // 2)]
    for first in range(0, per, 4):
        loaded = [
            [(window[par_source[p, j]], window[par_source[q, j]]) for p, q in pairs]
            for j in range(first, first + 4)
        ]
        for j, tiles in enumerate(loaded, first):
            for m, (left, right) in enumerate(tiles):
                stack[rank * j : rank * j + rank, 128 * m : 128 * m + 128] = jnp.where(
                    low, left, right
                )
    rows = par_ref[...].reshape(parent_count * rank, per * rank)
    parent_outs = matmul(rows, stack[...]).astype(BF)
    for p in range(parent_count):
        tile = parent_outs[rank * p : rank * p + rank, 128 * (p // 2) : 128 * (p // 2) + 128]
        outs[p] = split(tile, low)[p % 2]

    def build(quad, carry):
        for first in range(0, coup, 4):
            loaded = [
                [
                    (slots[coup_source[j, 4 * quad + t]], slots[coup_source[j, 4 * quad + t + 1]])
                    for t in (0, 2)
                ]
                for j in range(first, first + 4)
            ]
            for j, tiles in enumerate(loaded, first):
                for t, (left, right) in enumerate(tiles):
                    weights[quad, rank * j : rank * j + rank, 128 * t : 128 * t + 128] = jnp.where(
                        low, left, right
                    )
        return carry

    quads = leaf_count // 4
    lax.fori_loop(0, quads, build, 0)
    downs = [
        matmul(tst_ref[256 * p : 256 * p + 256, :], outs[p]) for p in range(parent_count)
    ]
    for first in range(0, quads, 2):
        outs_of = []
        for quad in range(first, first + 2):
            rows = coup_ref[4 * quad : 4 * quad + 4].reshape(4 * rank, coup * rank)
            coupled = matmul(rows, weights[quad])
            coupled = jnp.concatenate([coupled[:64, :128], coupled[64:, 128:]], 0)
            down = downs[quad // 2][128 * (quad % 2) : 128 * (quad % 2) + 128]
            outs_of.append((coupled + down).astype(BF))
        for quad, leaf_out in enumerate(outs_of, first):
            leaf_outs[128 * quad : 128 * quad + 128, :] = leaf_out
    for first in range(0, quads, 2):
        tiles = []
        for quad in range(first, first + 2):
            rows = slice(128 * quad, 128 * quad + 128)
            far = matmul_tn(leaf_outs[rows, :], diag[rows, :])
            for t in range(2):
                lanes = slice(256 * quad + 128 * t, 256 * quad + 128 * t + 128)
                tile = jnp.where(
                    low64, far[:64, 128 * t : 128 * t + 128], far[64:, 128 * t : 128 * t + 128]
                )
                tiles.append((lanes, (near_ref[:, lanes] + tile).astype(BF)))
        for lanes, tile in tiles:
            out_ref[:, lanes] = tile


def in_hbm(array):
    return pltpu.with_memory_space_constraint(array, pltpu.HBM)


def params(mib):
    return pltpu.CompilerParams(vmem_limit_bytes=mib << 20)


def cost(flops, size):
    return pl.CostEstimate(flops=flops, bytes_accessed=size, transcendentals=0)


def shards(
    rhs,
    basis,
    transfer,
    near_rows,
    near_source,
    far_request,
    coup_rows,
    coup_source,
    par_rows,
    par_source,
):
    leaf_count, leaf, rank = basis.shape
    points, rhs_count = rhs.shape
    parent_count = par_rows.shape[0]
    near_count = near_source.shape[1]
    coup_count = coup_source.shape[1]
    base = HALO // 2 * rhs_count
    parent_rows = rank * ((parent_count + 1) // 2)
    packed = base + 16 * leaf_count + parent_rows
    count = lax.axis_size("leaf")

    x = rhs.T
    trans = transfer.transpose(1, 2, 0).reshape(rank * rank, leaf_count)
    shape = jax.ShapeDtypeStruct
    vmem, smem, hbm = (pl.BlockSpec(memory_space=kind) for kind in (VMEM, SMEM, pltpu.HBM))
    own_one, own_two, tst, diag = pl.pallas_call(
        up_kernel,
        out_shape=(
            shape((packed, 128), BF),
            shape((packed, 128), BF),
            shape((rank * leaf_count, rank), BF),
            shape((rank * leaf_count, 256), BF),
        ),
        in_specs=[hbm] * 3,
        out_specs=(vmem,) * 4,
        scratch_shapes=[
            VMEM(x.shape, BF),
            VMEM((leaf_count, rank, leaf), BF),
            VMEM(trans.shape, BF),
            VMEM((rank * leaf_count, 128), F32),
            DMA((3,)),
        ],
        compiler_params=params(8),
        cost_estimate=cost(10**9, 2 * 10**6),
        name="upward",
    )(in_hbm(x), in_hbm(basis.transpose(0, 2, 1)), in_hbm(trans))

    def exchange(block, begin, distance=1, more=()):
        pairs = [(i, i + distance) for i in range(begin, count - distance, 2)]
        return lax.ppermute(block, "leaf", pairs + [(b, a) for a, b in pairs] + list(more))

    one = exchange(own_one, 0)
    two = exchange(own_two, 1)
    bundle = pl.pallas_call(
        functools.partial(relay_kernel, count, base),
        out_shape=shape((3 * (packed - base), 128), BF),
        in_specs=[vmem] * 3,
        out_specs=vmem,
        compiler_params=params(8),
        cost_estimate=cost(10**6, 2 * 10**6),
        name="relay",
    )(one, own_one, two)
    far = exchange(bundle, 1, 3, ((0, 2), (count - 1, count - 3)))
    over = exchange(two, 0)
    near = pl.pallas_call(
        near_kernel,
        out_shape=shape((rhs_count, points), F32),
        in_specs=[hbm, vmem, vmem, hbm, hbm],
        out_specs=vmem,
        scratch_shapes=[
            VMEM(x.shape, BF),
            SMEM((near_count, leaf_count), jnp.int32),
            VMEM(near_rows.shape, BF),
            VMEM((leaf_count + 2 * HALO, leaf, 128), BF),
            VMEM((256, 128 * ((near_count + 1) // 2)), BF),
            VMEM((256, 128 * ((near_count + 1) // 2)), BF),
            DMA((leaf_count // 4 + 2,)),
        ],
        compiler_params=params(20),
        cost_estimate=cost(8 * 10**9, 10**7),
        name="near",
    )(in_hbm(x), one, two, in_hbm(near_rows), in_hbm(near_source.T))

    far, near = lax.optimization_barrier((far, near))
    far_over = exchange(far, 0)

    product = pl.pallas_call(
        down_kernel,
        out_shape=shape((rhs_count, points), BF),
        in_specs=[vmem] * 6 + [smem] * 3 + [vmem] * 5,
        out_specs=vmem,
        scratch_shapes=[
            VMEM((leaf_count + 64, rank, 128), BF),
            VMEM((9 * parent_count, rank, 128), BF),
            VMEM((leaf_count // 4, coup_count * rank, 256), BF),
            VMEM((par_source.shape[1] * rank, 128 * ((parent_count + 1) // 2)), BF),
            VMEM((parent_count, rank, 128), BF),
            VMEM((rank * leaf_count, 128), BF),
        ],
        compiler_params=params(12),
        cost_estimate=cost(10**9, 4 * 10**6),
        name="downward",
    )(
        own_one,
        one,
        two,
        far,
        over,
        far_over,
        far_request[0],
        coup_source.T,
        par_source,
        coup_rows,
        par_rows,
        diag,
        tst,
        near,
    )
    return product.T


def solution(mesh):
    split = ("groups", "leaf")
    return jax.shard_map(
        shards,
        mesh=mesh,
        in_specs=(
            P(split, None),
            P(split, None, None),
            P(split, None, None),
            P(split, None, None),
            P(split, None),
            P(split, None, None),
            P(split, None, None),
            P(split, None),
            P(split, None, None),
            P(split, None),
        ),
        out_specs=P(split, None),
        check_vma=False,
    )
```

```python
import jax
import jax.numpy as jnp
from jax import lax
from jax.experimental import pallas as pl
from jax.experimental.pallas import tpu as pltpu
from jax.sharding import PartitionSpec as P

HALO = 16
BF = jnp.bfloat16
F32 = jnp.float32
VMEM = pltpu.VMEM
SMEM = pltpu.SMEM
DMA = pltpu.SemaphoreType.DMA


def low_half(rows):
    return lax.broadcasted_iota(jnp.int32, (rows, 128), 1) < 64


def swapped(value):
    return pltpu.roll(value, 64, 1)


def matmul(a, b):
    return jnp.dot(a, b, preferred_element_type=F32)


def matmul_nt(a, b):
    return lax.dot_general(a, b, (((1,), (1,)), ((), ())), preferred_element_type=F32)


def matmul_tn(a, b):
    return lax.dot_general(a, b, (((0,), (0,)), ((), ())), preferred_element_type=F32)


def fill_block_diagonal(basis_ref, diag):
    leaf_count, rank, leaf = basis_ref.shape
    blank = jnp.zeros((rank, leaf), BF)
    empty = jnp.zeros((rank, 2 * leaf), BF)
    for i in range(leaf_count):
        at = 128 * (1 - i % 4 // 2)
        diag[rank * i : rank * (i + 1), at : at + 128] = empty
    for first in range(0, leaf_count, 8):
        tiles = []
        for i in range(first, first + 8):
            block = basis_ref[i]
            tiles.append(jnp.concatenate([blank, block] if i % 2 else [block, blank], 1))
        for i, tile in enumerate(tiles, first):
            at = 128 * (i % 4 // 2)
            diag[rank * i : rank * (i + 1), at : at + 128] = tile


def up_kernel(x_hbm, basis_hbm, trans_hbm, one, two, own, tst_ref, diag, x_ref, basis_ref, trans_ref, flat, sems):
    points = x_hbm.shape[1]
    leaf_count, rank, leaf = basis_hbm.shape
    copies = [
        pltpu.make_async_copy(source, held, sems.at[n])
        for n, (source, held) in enumerate(
            ((trans_hbm, trans_ref), (basis_hbm, basis_ref), (x_hbm, x_ref))
        )
    ]
    for copy in copies:
        copy.start()
    copies[0].wait()
    for first in range(0, rank // 4, 4):
        blocks = [
            trans_ref[128 * step : 128 * step + 128, :].astype(F32).T
            for step in range(first, first + 4)
        ]
        for q in range(4):
            pieces = [block if q == 0 else pltpu.roll(block, 128 - 32 * q, 1) for block in blocks]
            for step, piece in enumerate(pieces, first):
                flat[pl.ds(4 * step + q, leaf_count, stride=rank), :] = piece
    tst_ref[...] = flat[:, 0:rank].astype(BF)
    copies[1].wait()
    fill_block_diagonal(basis_ref, diag)
    copies[2].wait()

    odd = lax.rem(lax.axis_index("leaf"), 2) == 1
    base = HALO * leaf // 128 * 64
    for t in range(HALO * leaf // 128):
        rows = slice(64 * t, 64 * t + 64)
        at = points - HALO * leaf + 128 * t
        head, tail = x_ref[:, 128 * t : 128 * t + 128], x_ref[:, at : at + 128]
        one[rows, :] = jnp.where(odd, head, tail)
        two[rows, :] = jnp.where(odd, tail, head)

    def put(at, left, right):
        rows = left.shape[0]
        both = jnp.where(low_half(rows), left, right)
        own[at : at + rows, :] = both
        one[base + at : base + at + rows, :] = both
        two[base + at : base + at + rows, :] = both

    parent_count = leaf_count // 8
    skels = []
    for quad in range(leaf_count // 4):
        x = x_ref[:, 256 * quad : 256 * quad + 256]
        skels.append(
            matmul_nt(
                diag[128 * quad : 128 * quad + 128, :], jnp.concatenate([x, x], 0)
            ).astype(BF)
        )
    parents = [
        matmul_tn(
            tst_ref[256 * p : 256 * p + 256, :], jnp.concatenate(skels[2 * p : 2 * p + 2], 0)
        ).astype(BF)
        for p in range(parent_count)
    ]
    for quad, skel in enumerate(skels):
        put(64 * quad, skel[:64], skel[64:])
    for m in range((parent_count + 1) // 2):
        put(16 * leaf_count + 32 * m, parents[2 * m], parents[min(2 * m + 1, parent_count - 1)])


def place(r, leaf_count):
    safe = jnp.minimum(r, leaf_count - 1)
    return pl.multiple_of((safe >> 2) * 64 + (safe & 1) * 32, 32), (safe >> 1) & 1


def near_kernel(
    x_hbm,
    one_ref,
    two_ref,
    near_ref,
    source_hbm,
    out_ref,
    x_ref,
    source_ref,
    held,
    twice,
    pair_a,
    pair_b,
    sems,
):
    leaf_count, leaf, depth = near_ref.shape
    count = source_hbm.shape[0]
    quads = leaf_count // 4
    copy_x = pltpu.make_async_copy(x_hbm, x_ref, sems.at[quads])
    copy_source = pltpu.make_async_copy(source_hbm, source_ref, sems.at[quads + 1])
    copy_x.start()
    copy_source.start()

    def copy(quad):
        part = pl.ds(4 * quad, 4)
        return pltpu.make_async_copy(near_ref.at[part], held.at[part], sems.at[quad])

    for quad in range(quads):
        copy(quad).start()

    low = low_half(leaf)

    def spread(parts):
        others = [swapped(value) for value, _ in parts]
        for (value, at), other in zip(parts, others):
            twice[at] = jnp.where(low, value, other)
            twice[at + 1] = jnp.where(low, other, value)

    odd = lax.rem(lax.axis_index("leaf"), 2) == 1
    after = HALO + leaf_count
    at_one, at_two = jnp.where(odd, 0, after), jnp.where(odd, after, 0)
    for ref, at in ((one_ref, at_one), (two_ref, at_two)):
        spread([(ref[64 * n : 64 * n + 64, :], at + 2 * n) for n in range(HALO // 2)])
    copy_x.wait()
    for first in range(0, leaf_count // 2, 5):
        spread(
            [(x_ref[:, 128 * n : 128 * n + 128], HALO + 2 * n) for n in range(first, first + 5)]
        )
    copy_source.wait()

    def build(quad, stacked):
        for u in range(4):
            i = 4 * quad + u
            rows = slice(64 * u, 64 * u + 64)
            pairs = [(2 * m, min(2 * m + 1, count - 1)) for m in range((count + 1) // 2)]
            for first in range(0, len(pairs), 5):
                some = pairs[first : first + 5]
                loaded = [(twice[source_ref[a, i]], twice[source_ref[b, i]]) for a, b in some]
                for m, (left, right) in enumerate(loaded, first):
                    stacked[rows, 128 * m : 128 * m + 128] = jnp.where(low, left, right)

    def multiply(quad, stacked):
        rows = held[pl.ds(4 * quad, 4)].reshape(4 * leaf, depth)
        total = matmul_nt(stacked[:, :depth], rows)
        for t in range(2):
            lanes = pl.ds(pl.multiple_of(256 * quad + 128 * t, 128), 128)
            out_ref[:, lanes] = jnp.where(
                low,
                total[128 * t : 128 * t + 64, 128 * t : 128 * t + 128],
                total[128 * t + 64 : 128 * t + 128, 128 * t : 128 * t + 128],
            )

    build(0, pair_a)

    def body(step, carry):
        quad = 2 * step
        copy(quad).wait()
        copy(quad + 1).wait()
        build(quad + 1, pair_b)
        multiply(quad, pair_a)
        build(jnp.minimum(quad + 2, quads - 1), pair_a)
        multiply(quad + 1, pair_b)
        return carry

    lax.fori_loop(0, quads // 2, body, 0)


def down_kernel(
    own_ref,
    one_ref,
    two_ref,
    three_ref,
    four_ref,
    five_ref,
    two_over,
    three_over,
    four_over,
    req_ref,
    coup_source,
    par_source,
    coup_ref,
    par_ref,
    diag,
    tst_ref,
    near_ref,
    out_ref,
    slots,
    window,
    weights,
    stack,
    outs,
    leaf_outs,
):
    leaf_count, rank = coup_ref.shape[:2]
    parent_count = par_ref.shape[0]
    base = HALO // 2 * 64
    low64 = low_half(64)
    low = low_half(rank)
    odd = lax.rem(lax.axis_index("leaf"), 2) == 1

    def split(value, mask):
        other = swapped(value)
        return jnp.where(mask, value, other), jnp.where(mask, other, value)

    for first in range(0, leaf_count // 4, 5):
        quads = range(first, first + 5)
        values = [own_ref[64 * quad : 64 * quad + 64, :] for quad in quads]
        for quad, (left, right) in zip(quads, [split(value, low64) for value in values]):
            slots[4 * quad] = left[:32]
            slots[4 * quad + 1] = left[32:]
            slots[4 * quad + 2] = right[:32]
            slots[4 * quad + 3] = right[32:]

    def put_parents(ref, at, block):
        tiles = range((parent_count + 1) // 2)
        values = [ref[at + 32 * m : at + 32 * m + 32, :] for m in tiles]
        for m, (left, right) in zip(tiles, [split(value, low) for value in values]):
            window[parent_count * block + 2 * m] = left
            if 2 * m + 1 < parent_count:
                window[parent_count * block + 2 * m + 1] = right

    put_parents(own_ref, 16 * leaf_count, 4)
    outer = ((two_ref, base), (three_over, 0), (four_ref, 0), (five_ref, 0))
    inner = ((one_ref, base), (two_over, base), (three_ref, 0), (four_over, 0))
    for side, up in ((outer, odd), (inner, jnp.logical_not(odd))):
        for n, (ref, at) in enumerate(side):
            k = jnp.where(up, 4 + n, 3 - n)
            asked = [req_ref[k, c] for c in range(8)]
            places = [place(r, leaf_count) for r in asked]
            values = [ref[pl.ds(at + row, 32), :] for row, _ in places]
            others = [swapped(value) for value in values]
            for c, r in enumerate(asked):
                value = jnp.where(low == (places[c][1] == 0), values[c], others[c])
                slots[leaf_count + 8 * k + c] = jnp.where(
                    r < leaf_count, value, jnp.zeros_like(value)
                )
            put_parents(ref, at + 16 * leaf_count, jnp.where(up, 5 + n, 3 - n))

    per = par_source.shape[1]
    coup = coup_source.shape[0]
    pairs = [(2 * m, min(2 * m + 1, parent_count - 1)) for m in range((parent_count + 1) // 2)]
    for first in range(0, per, 4):
        loaded = [
            [(window[par_source[p, j]], window[par_source[q, j]]) for p, q in pairs]
            for j in range(first, first + 4)
        ]
        for j, tiles in enumerate(loaded, first):
            for m, (left, right) in enumerate(tiles):
                stack[rank * j : rank * j + rank, 128 * m : 128 * m + 128] = jnp.where(
                    low, left, right
                )
    rows = par_ref[...].reshape(parent_count * rank, per * rank)
    parent_outs = matmul(rows, stack[...]).astype(BF)
    for p in range(parent_count):
        tile = parent_outs[rank * p : rank * p + rank, 128 * (p // 2) : 128 * (p // 2) + 128]
        outs[p] = split(tile, low)[p % 2]

    def build(quad, carry):
        for first in range(0, coup, 4):
            loaded = [
                [
                    (slots[coup_source[j, 4 * quad + t]], slots[coup_source[j, 4 * quad + t + 1]])
                    for t in (0, 2)
                ]
                for j in range(first, first + 4)
            ]
            for j, tiles in enumerate(loaded, first):
                for t, (left, right) in enumerate(tiles):
                    weights[quad, rank * j : rank * j + rank, 128 * t : 128 * t + 128] = jnp.where(
                        low, left, right
                    )
        return carry

    quads = leaf_count // 4
    lax.fori_loop(0, quads, build, 0)
    downs = [
        matmul(tst_ref[256 * p : 256 * p + 256, :], outs[p]) for p in range(parent_count)
    ]
    for first in range(0, quads, 2):
        outs_of = []
        for quad in range(first, first + 2):
            rows = coup_ref[4 * quad : 4 * quad + 4].reshape(4 * rank, coup * rank)
            coupled = matmul(rows, weights[quad])
            coupled = jnp.concatenate([coupled[:64, :128], coupled[64:, 128:]], 0)
            down = downs[quad // 2][128 * (quad % 2) : 128 * (quad % 2) + 128]
            outs_of.append((coupled + down).astype(BF))
        for quad, leaf_out in enumerate(outs_of, first):
            leaf_outs[128 * quad : 128 * quad + 128, :] = leaf_out
    for first in range(0, quads, 2):
        tiles = []
        for quad in range(first, first + 2):
            rows = slice(128 * quad, 128 * quad + 128)
            far = matmul_tn(leaf_outs[rows, :], diag[rows, :])
            for t in range(2):
                lanes = slice(256 * quad + 128 * t, 256 * quad + 128 * t + 128)
                tile = jnp.where(
                    low64, far[:64, 128 * t : 128 * t + 128], far[64:, 128 * t : 128 * t + 128]
                )
                tiles.append((lanes, (near_ref[:, lanes] + tile).astype(BF)))
        for lanes, tile in tiles:
            out_ref[:, lanes] = tile


def in_hbm(array):
    return pltpu.with_memory_space_constraint(array, pltpu.HBM)


def params(mib):
    return pltpu.CompilerParams(vmem_limit_bytes=mib << 20)


def cost(flops, size):
    return pl.CostEstimate(flops=flops, bytes_accessed=size, transcendentals=0)


def shards(
    rhs,
    basis,
    transfer,
    near_rows,
    near_source,
    far_request,
    coup_rows,
    coup_source,
    par_rows,
    par_source,
):
    leaf_count, leaf, rank = basis.shape
    points, rhs_count = rhs.shape
    parent_count = par_rows.shape[0]
    near_count = near_source.shape[1]
    coup_count = coup_source.shape[1]
    base = HALO // 2 * rhs_count
    parent_rows = rank * ((parent_count + 1) // 2)
    packed = base + 16 * leaf_count + parent_rows
    count = lax.axis_size("leaf")

    x = rhs.T
    trans = transfer.transpose(1, 2, 0).reshape(rank * rank, leaf_count)
    shape = jax.ShapeDtypeStruct
    vmem, smem, hbm = (pl.BlockSpec(memory_space=kind) for kind in (VMEM, SMEM, pltpu.HBM))
    own_one, own_two, own, tst, diag = pl.pallas_call(
        up_kernel,
        out_shape=(
            shape((packed, 128), BF),
            shape((packed, 128), BF),
            shape((packed - base, 128), BF),
            shape((rank * leaf_count, rank), BF),
            shape((rank * leaf_count, 256), BF),
        ),
        in_specs=[hbm] * 3,
        out_specs=(vmem,) * 5,
        scratch_shapes=[
            VMEM(x.shape, BF),
            VMEM((leaf_count, rank, leaf), BF),
            VMEM(trans.shape, BF),
            VMEM((rank * leaf_count, 128), F32),
            DMA((3,)),
        ],
        compiler_params=params(8),
        cost_estimate=cost(10**9, 2 * 10**6),
        name="upward",
    )(in_hbm(x), in_hbm(basis.transpose(0, 2, 1)), in_hbm(trans))

    def exchange(block, begin, distance=1):
        pairs = [(i, i + distance) for i in range(begin, count - distance, 2)]
        return lax.ppermute(block, "leaf", pairs + [(b, a) for a, b in pairs])

    one = exchange(own_one, 0)
    two = exchange(own_two, 1)
    three = exchange(own, 0, 3)
    four = exchange(own, 1, 3)
    crossing = [(i, i + 4) for i in range(0, count - 4, 2)]
    crossing += [(i, i - 4) for i in range(5, count, 2)]
    five = lax.ppermute(own, "leaf", crossing)
    two_over = exchange(two, 0)

    near = pl.pallas_call(
        near_kernel,
        out_shape=shape((rhs_count, points), F32),
        in_specs=[hbm, vmem, vmem, hbm, hbm],
        out_specs=vmem,
        scratch_shapes=[
            VMEM(x.shape, BF),
            SMEM((near_count, leaf_count), jnp.int32),
            VMEM(near_rows.shape, BF),
            VMEM((leaf_count + 2 * HALO, leaf, 128), BF),
            VMEM((256, 128 * ((near_count + 1) // 2)), BF),
            VMEM((256, 128 * ((near_count + 1) // 2)), BF),
            DMA((leaf_count // 4 + 2,)),
        ],
        compiler_params=params(20),
        cost_estimate=cost(8 * 10**9, 10**7),
        name="near",
    )(in_hbm(x), one, two, in_hbm(near_rows), in_hbm(near_source.T))

    three, four, near = lax.optimization_barrier((three, four, near))
    three_over = exchange(three, 0)
    four_over = exchange(four, 0)

    product = pl.pallas_call(
        down_kernel,
        out_shape=shape((rhs_count, points), BF),
        in_specs=[vmem] * 9 + [smem] * 3 + [vmem] * 5,
        out_specs=vmem,
        scratch_shapes=[
            VMEM((leaf_count + 64, rank, 128), BF),
            VMEM((9 * parent_count, rank, 128), BF),
            VMEM((leaf_count // 4, coup_count * rank, 256), BF),
            VMEM((par_source.shape[1] * rank, 128 * ((parent_count + 1) // 2)), BF),
            VMEM((parent_count, rank, 128), BF),
            VMEM((rank * leaf_count, 128), BF),
        ],
        compiler_params=params(12),
        cost_estimate=cost(10**9, 4 * 10**6),
        name="downward",
    )(
        own,
        one,
        two,
        three,
        four,
        five,
        two_over,
        three_over,
        four_over,
        far_request[0],
        coup_source.T,
        par_source,
        coup_rows,
        par_rows,
        diag,
        tst,
        near,
    )
    return product.T


def solution(mesh):
    split = ("groups", "leaf")
    return jax.shard_map(
        shards,
        mesh=mesh,
        in_specs=(
            P(split, None),
            P(split, None, None),
            P(split, None, None),
            P(split, None, None),
            P(split, None),
            P(split, None, None),
            P(split, None, None),
            P(split, None),
            P(split, None, None),
            P(split, None),
        ),
        out_specs=P(split, None),
        check_vma=False,
    )
```

```python
import functools

import jax
import jax.numpy as jnp
from jax import lax
from jax.experimental import pallas as pl
from jax.experimental.pallas import tpu as pltpu
from jax.sharding import PartitionSpec as P

HALO = 16
BF = jnp.bfloat16
F32 = jnp.float32
VMEM = pltpu.VMEM
SMEM = pltpu.SMEM
DMA = pltpu.SemaphoreType.DMA


def low_half(rows):
    return lax.broadcasted_iota(jnp.int32, (rows, 128), 1) < 64


def swapped(value):
    return pltpu.roll(value, 64, 1)


def matmul(a, b):
    return jnp.dot(a, b, preferred_element_type=F32)


def matmul_nt(a, b):
    return lax.dot_general(a, b, (((1,), (1,)), ((), ())), preferred_element_type=F32)


def matmul_tn(a, b):
    return lax.dot_general(a, b, (((0,), (0,)), ((), ())), preferred_element_type=F32)


def fill_block_diagonal(basis_ref, diag):
    leaf_count, rank, leaf = basis_ref.shape
    blank = jnp.zeros((rank, leaf), BF)
    empty = jnp.zeros((rank, 2 * leaf), BF)
    for i in range(leaf_count):
        at = 128 * (1 - i % 4 // 2)
        diag[rank * i : rank * (i + 1), at : at + 128] = empty
    for first in range(0, leaf_count, 8):
        tiles = []
        for i in range(first, first + 8):
            block = basis_ref[i]
            tiles.append(jnp.concatenate([blank, block] if i % 2 else [block, blank], 1))
        for i, tile in enumerate(tiles, first):
            at = 128 * (i % 4 // 2)
            diag[rank * i : rank * (i + 1), at : at + 128] = tile


def up_kernel(x_hbm, basis_hbm, trans_hbm, one, two, own, tst_ref, diag, x_ref, basis_ref, trans_ref, flat, sems):
    points = x_hbm.shape[1]
    leaf_count, rank, leaf = basis_hbm.shape
    copies = [
        pltpu.make_async_copy(source, held, sems.at[n])
        for n, (source, held) in enumerate(
            ((trans_hbm, trans_ref), (basis_hbm, basis_ref), (x_hbm, x_ref))
        )
    ]
    for copy in copies:
        copy.start()
    copies[0].wait()
    for first in range(0, rank // 4, 4):
        blocks = [
            trans_ref[128 * step : 128 * step + 128, :].astype(F32).T
            for step in range(first, first + 4)
        ]
        for q in range(4):
            pieces = [block if q == 0 else pltpu.roll(block, 128 - 32 * q, 1) for block in blocks]
            for step, piece in enumerate(pieces, first):
                flat[pl.ds(4 * step + q, leaf_count, stride=rank), :] = piece
    tst_ref[...] = flat[:, 0:rank].astype(BF)
    copies[1].wait()
    fill_block_diagonal(basis_ref, diag)
    copies[2].wait()

    odd = lax.rem(lax.axis_index("leaf"), 2) == 1
    base = HALO * leaf // 128 * 64
    for t in range(HALO * leaf // 128):
        rows = slice(64 * t, 64 * t + 64)
        at = points - HALO * leaf + 128 * t
        head, tail = x_ref[:, 128 * t : 128 * t + 128], x_ref[:, at : at + 128]
        one[rows, :] = jnp.where(odd, head, tail)
        two[rows, :] = jnp.where(odd, tail, head)

    def put(at, left, right):
        rows = left.shape[0]
        both = jnp.where(low_half(rows), left, right)
        own[at : at + rows, :] = both
        one[base + at : base + at + rows, :] = both
        two[base + at : base + at + rows, :] = both

    parent_count = leaf_count // 8
    skels = []
    for quad in range(leaf_count // 4):
        x = x_ref[:, 256 * quad : 256 * quad + 256]
        skels.append(
            matmul_nt(
                diag[128 * quad : 128 * quad + 128, :], jnp.concatenate([x, x], 0)
            ).astype(BF)
        )
    parents = [
        matmul_tn(
            tst_ref[256 * p : 256 * p + 256, :], jnp.concatenate(skels[2 * p : 2 * p + 2], 0)
        ).astype(BF)
        for p in range(parent_count)
    ]
    for quad, skel in enumerate(skels):
        put(64 * quad, skel[:64], skel[64:])
    for m in range((parent_count + 1) // 2):
        put(16 * leaf_count + 32 * m, parents[2 * m], parents[min(2 * m + 1, parent_count - 1)])


def place(r, leaf_count):
    safe = jnp.minimum(r, leaf_count - 1)
    return pl.multiple_of((safe >> 2) * 64 + (safe & 1) * 32, 32), (safe >> 1) & 1


def join_kernel(base, own_ref, one_ref, out_ref):
    size = own_ref.shape[0]
    out_ref[:size, :] = own_ref[...]
    out_ref[size:, :] = one_ref[base:, :]


def near_kernel(
    x_hbm,
    one_ref,
    two_ref,
    near_ref,
    source_hbm,
    out_ref,
    x_ref,
    source_ref,
    held,
    twice,
    pair_a,
    pair_b,
    sems,
):
    leaf_count, leaf, depth = near_ref.shape
    count = source_hbm.shape[0]
    quads = leaf_count // 4
    copy_x = pltpu.make_async_copy(x_hbm, x_ref, sems.at[quads])
    copy_source = pltpu.make_async_copy(source_hbm, source_ref, sems.at[quads + 1])
    copy_x.start()
    copy_source.start()

    def copy(quad):
        part = pl.ds(4 * quad, 4)
        return pltpu.make_async_copy(near_ref.at[part], held.at[part], sems.at[quad])

    for quad in range(quads):
        copy(quad).start()

    low = low_half(leaf)

    def spread(parts):
        others = [swapped(value) for value, _ in parts]
        for (value, at), other in zip(parts, others):
            twice[at] = jnp.where(low, value, other)
            twice[at + 1] = jnp.where(low, other, value)

    odd = lax.rem(lax.axis_index("leaf"), 2) == 1
    after = HALO + leaf_count
    at_one, at_two = jnp.where(odd, 0, after), jnp.where(odd, after, 0)
    for ref, at in ((one_ref, at_one), (two_ref, at_two)):
        spread([(ref[64 * n : 64 * n + 64, :], at + 2 * n) for n in range(HALO // 2)])
    copy_x.wait()
    for first in range(0, leaf_count // 2, 5):
        spread(
            [(x_ref[:, 128 * n : 128 * n + 128], HALO + 2 * n) for n in range(first, first + 5)]
        )
    copy_source.wait()

    def build(quad, stacked):
        for u in range(4):
            i = 4 * quad + u
            rows = slice(64 * u, 64 * u + 64)
            pairs = [(2 * m, min(2 * m + 1, count - 1)) for m in range((count + 1) // 2)]
            for first in range(0, len(pairs), 5):
                some = pairs[first : first + 5]
                loaded = [(twice[source_ref[a, i]], twice[source_ref[b, i]]) for a, b in some]
                for m, (left, right) in enumerate(loaded, first):
                    stacked[rows, 128 * m : 128 * m + 128] = jnp.where(low, left, right)

    def multiply(quad, stacked):
        rows = held[pl.ds(4 * quad, 4)].reshape(4 * leaf, depth)
        total = matmul_nt(stacked[:, :depth], rows)
        for t in range(2):
            lanes = pl.ds(pl.multiple_of(256 * quad + 128 * t, 128), 128)
            out_ref[:, lanes] = jnp.where(
                low,
                total[128 * t : 128 * t + 64, 128 * t : 128 * t + 128],
                total[128 * t + 64 : 128 * t + 128, 128 * t : 128 * t + 128],
            )

    build(0, pair_a)

    def body(step, carry):
        quad = 2 * step
        copy(quad).wait()
        copy(quad + 1).wait()
        build(quad + 1, pair_b)
        multiply(quad, pair_a)
        build(jnp.minimum(quad + 2, quads - 1), pair_a)
        multiply(quad + 1, pair_b)
        return carry

    lax.fori_loop(0, quads // 2, body, 0)


def down_kernel(
    own_ref,
    one_ref,
    two_ref,
    three_ref,
    far_ref,
    two_over,
    three_over,
    far_over,
    req_ref,
    coup_source,
    par_source,
    coup_ref,
    par_ref,
    diag,
    tst_ref,
    near_ref,
    out_ref,
    slots,
    window,
    weights,
    stack,
    outs,
    leaf_outs,
):
    leaf_count, rank = coup_ref.shape[:2]
    parent_count = par_ref.shape[0]
    base = HALO // 2 * 64
    low64 = low_half(64)
    low = low_half(rank)
    odd = lax.rem(lax.axis_index("leaf"), 2) == 1

    def split(value, mask):
        other = swapped(value)
        return jnp.where(mask, value, other), jnp.where(mask, other, value)

    for first in range(0, leaf_count // 4, 5):
        quads = range(first, first + 5)
        values = [own_ref[64 * quad : 64 * quad + 64, :] for quad in quads]
        for quad, (left, right) in zip(quads, [split(value, low64) for value in values]):
            slots[4 * quad] = left[:32]
            slots[4 * quad + 1] = left[32:]
            slots[4 * quad + 2] = right[:32]
            slots[4 * quad + 3] = right[32:]

    def put_parents(ref, at, block):
        tiles = range((parent_count + 1) // 2)
        values = [ref[at + 32 * m : at + 32 * m + 32, :] for m in tiles]
        for m, (left, right) in zip(tiles, [split(value, low) for value in values]):
            window[parent_count * block + 2 * m] = left
            if 2 * m + 1 < parent_count:
                window[parent_count * block + 2 * m + 1] = right

    put_parents(own_ref, 16 * leaf_count, 4)
    outer = ((two_ref, base), (three_over, 0), (far_ref, 0), (far_ref, own_ref.shape[0]))
    inner = ((one_ref, base), (two_over, base), (three_ref, 0), (far_over, 0))
    for side, up in ((outer, odd), (inner, jnp.logical_not(odd))):
        for n, (ref, at) in enumerate(side):
            k = jnp.where(up, 4 + n, 3 - n)
            asked = [req_ref[k, c] for c in range(8)]
            places = [place(r, leaf_count) for r in asked]
            values = [ref[pl.ds(at + row, 32), :] for row, _ in places]
            others = [swapped(value) for value in values]
            for c, r in enumerate(asked):
                value = jnp.where(low == (places[c][1] == 0), values[c], others[c])
                slots[leaf_count + 8 * k + c] = jnp.where(
                    r < leaf_count, value, jnp.zeros_like(value)
                )
            put_parents(ref, at + 16 * leaf_count, jnp.where(up, 5 + n, 3 - n))

    per = par_source.shape[1]
    coup = coup_source.shape[0]
    pairs = [(2 * m, min(2 * m + 1, parent_count - 1)) for m in range((parent_count + 1) // 2)]
    for first in range(0, per, 4):
        loaded = [
            [(window[par_source[p, j]], window[par_source[q, j]]) for p, q in pairs]
            for j in range(first, first + 4)
        ]
        for j, tiles in enumerate(loaded, first):
            for m, (left, right) in enumerate(tiles):
                stack[rank * j : rank * j + rank, 128 * m : 128 * m + 128] = jnp.where(
                    low, left, right
                )
    rows = par_ref[...].reshape(parent_count * rank, per * rank)
    parent_outs = matmul(rows, stack[...]).astype(BF)
    for p in range(parent_count):
        tile = parent_outs[rank * p : rank * p + rank, 128 * (p // 2) : 128 * (p // 2) + 128]
        outs[p] = split(tile, low)[p % 2]

    def build(quad, carry):
        for first in range(0, coup, 4):
            loaded = [
                [
                    (slots[coup_source[j, 4 * quad + t]], slots[coup_source[j, 4 * quad + t + 1]])
                    for t in (0, 2)
                ]
                for j in range(first, first + 4)
            ]
            for j, tiles in enumerate(loaded, first):
                for t, (left, right) in enumerate(tiles):
                    weights[quad, rank * j : rank * j + rank, 128 * t : 128 * t + 128] = jnp.where(
                        low, left, right
                    )
        return carry

    quads = leaf_count // 4
    lax.fori_loop(0, quads, build, 0)
    downs = [
        matmul(tst_ref[256 * p : 256 * p + 256, :], outs[p]) for p in range(parent_count)
    ]
    for first in range(0, quads, 2):
        outs_of = []
        for quad in range(first, first + 2):
            rows = coup_ref[4 * quad : 4 * quad + 4].reshape(4 * rank, coup * rank)
            coupled = matmul(rows, weights[quad])
            coupled = jnp.concatenate([coupled[:64, :128], coupled[64:, 128:]], 0)
            down = downs[quad // 2][128 * (quad % 2) : 128 * (quad % 2) + 128]
            outs_of.append((coupled + down).astype(BF))
        for quad, leaf_out in enumerate(outs_of, first):
            leaf_outs[128 * quad : 128 * quad + 128, :] = leaf_out
    for first in range(0, quads, 2):
        tiles = []
        for quad in range(first, first + 2):
            rows = slice(128 * quad, 128 * quad + 128)
            far = matmul_tn(leaf_outs[rows, :], diag[rows, :])
            for t in range(2):
                lanes = slice(256 * quad + 128 * t, 256 * quad + 128 * t + 128)
                tile = jnp.where(
                    low64, far[:64, 128 * t : 128 * t + 128], far[64:, 128 * t : 128 * t + 128]
                )
                tiles.append((lanes, (near_ref[:, lanes] + tile).astype(BF)))
        for lanes, tile in tiles:
            out_ref[:, lanes] = tile


def in_hbm(array):
    return pltpu.with_memory_space_constraint(array, pltpu.HBM)


def params(mib):
    return pltpu.CompilerParams(vmem_limit_bytes=mib << 20)


def cost(flops, size):
    return pl.CostEstimate(flops=flops, bytes_accessed=size, transcendentals=0)


def shards(
    rhs,
    basis,
    transfer,
    near_rows,
    near_source,
    far_request,
    coup_rows,
    coup_source,
    par_rows,
    par_source,
):
    leaf_count, leaf, rank = basis.shape
    points, rhs_count = rhs.shape
    parent_count = par_rows.shape[0]
    near_count = near_source.shape[1]
    coup_count = coup_source.shape[1]
    base = HALO // 2 * rhs_count
    parent_rows = rank * ((parent_count + 1) // 2)
    packed = base + 16 * leaf_count + parent_rows
    count = lax.axis_size("leaf")

    x = rhs.T
    trans = transfer.transpose(1, 2, 0).reshape(rank * rank, leaf_count)
    shape = jax.ShapeDtypeStruct
    vmem, smem, hbm = (pl.BlockSpec(memory_space=kind) for kind in (VMEM, SMEM, pltpu.HBM))
    own_one, own_two, own, tst, diag = pl.pallas_call(
        up_kernel,
        out_shape=(
            shape((packed, 128), BF),
            shape((packed, 128), BF),
            shape((packed - base, 128), BF),
            shape((rank * leaf_count, rank), BF),
            shape((rank * leaf_count, 256), BF),
        ),
        in_specs=[hbm] * 3,
        out_specs=(vmem,) * 5,
        scratch_shapes=[
            VMEM(x.shape, BF),
            VMEM((leaf_count, rank, leaf), BF),
            VMEM(trans.shape, BF),
            VMEM((rank * leaf_count, 128), F32),
            DMA((3,)),
        ],
        compiler_params=params(8),
        cost_estimate=cost(10**9, 2 * 10**6),
        name="upward",
    )(in_hbm(x), in_hbm(basis.transpose(0, 2, 1)), in_hbm(trans))

    def exchange(block, begin, distance=1):
        pairs = [(i, i + distance) for i in range(begin, count - distance, 2)]
        return lax.ppermute(block, "leaf", pairs + [(b, a) for a, b in pairs])

    one = exchange(own_one, 0)
    two = exchange(own_two, 1)
    three = exchange(own, 0, 3)
    both = pl.pallas_call(
        functools.partial(join_kernel, base),
        out_shape=shape((2 * (packed - base), 128), BF),
        in_specs=[vmem] * 2,
        out_specs=vmem,
        compiler_params=params(8),
        cost_estimate=cost(10**6, 10**6),
        name="join",
    )(own, one)
    far = exchange(both, 1, 3)
    two_over = exchange(two, 0)

    near = pl.pallas_call(
        near_kernel,
        out_shape=shape((rhs_count, points), F32),
        in_specs=[hbm, vmem, vmem, hbm, hbm],
        out_specs=vmem,
        scratch_shapes=[
            VMEM(x.shape, BF),
            SMEM((near_count, leaf_count), jnp.int32),
            VMEM(near_rows.shape, BF),
            VMEM((leaf_count + 2 * HALO, leaf, 128), BF),
            VMEM((256, 128 * ((near_count + 1) // 2)), BF),
            VMEM((256, 128 * ((near_count + 1) // 2)), BF),
            DMA((leaf_count // 4 + 2,)),
        ],
        compiler_params=params(20),
        cost_estimate=cost(8 * 10**9, 10**7),
        name="near",
    )(in_hbm(x), one, two, in_hbm(near_rows), in_hbm(near_source.T))

    three, far, near = lax.optimization_barrier((three, far, near))
    three_over = exchange(three, 0)
    far_over = exchange(far, 0)

    product = pl.pallas_call(
        down_kernel,
        out_shape=shape((rhs_count, points), BF),
        in_specs=[vmem] * 8 + [smem] * 3 + [vmem] * 5,
        out_specs=vmem,
        scratch_shapes=[
            VMEM((leaf_count + 64, rank, 128), BF),
            VMEM((9 * parent_count, rank, 128), BF),
            VMEM((leaf_count // 4, coup_count * rank, 256), BF),
            VMEM((par_source.shape[1] * rank, 128 * ((parent_count + 1) // 2)), BF),
            VMEM((parent_count, rank, 128), BF),
            VMEM((rank * leaf_count, 128), BF),
        ],
        compiler_params=params(12),
        cost_estimate=cost(10**9, 4 * 10**6),
        name="downward",
    )(
        own,
        one,
        two,
        three,
        far,
        two_over,
        three_over,
        far_over,
        far_request[0],
        coup_source.T,
        par_source,
        coup_rows,
        par_rows,
        diag,
        tst,
        near,
    )
    return product.T


def solution(mesh):
    split = ("groups", "leaf")
    return jax.shard_map(
        shards,
        mesh=mesh,
        in_specs=(
            P(split, None),
            P(split, None, None),
            P(split, None, None),
            P(split, None, None),
            P(split, None),
            P(split, None, None),
            P(split, None, None),
            P(split, None),
            P(split, None, None),
            P(split, None),
        ),
        out_specs=P(split, None),
        check_vma=False,
    )
```

```python
import functools

import jax
import jax.numpy as jnp
from jax import lax
from jax.experimental import pallas as pl
from jax.experimental.pallas import tpu as pltpu
from jax.sharding import PartitionSpec as P

HALO = 16
BF = jnp.bfloat16
F32 = jnp.float32
VMEM = pltpu.VMEM
SMEM = pltpu.SMEM
DMA = pltpu.SemaphoreType.DMA


def low_half(rows):
    return lax.broadcasted_iota(jnp.int32, (rows, 128), 1) < 64


def swapped(value):
    return pltpu.roll(value, 64, 1)


def matmul(a, b):
    return jnp.dot(a, b, preferred_element_type=F32)


def matmul_nt(a, b):
    return lax.dot_general(a, b, (((1,), (1,)), ((), ())), preferred_element_type=F32)


def matmul_tn(a, b):
    return lax.dot_general(a, b, (((0,), (0,)), ((), ())), preferred_element_type=F32)


def fill_block_diagonal(basis_ref, diag):
    leaf_count, rank, leaf = basis_ref.shape
    blank = jnp.zeros((rank, leaf), BF)
    empty = jnp.zeros((rank, 2 * leaf), BF)
    for i in range(leaf_count):
        at = 128 * (1 - i % 4 // 2)
        diag[rank * i : rank * (i + 1), at : at + 128] = empty
    for first in range(0, leaf_count, 8):
        tiles = []
        for i in range(first, first + 8):
            block = basis_ref[i]
            tiles.append(jnp.concatenate([blank, block] if i % 2 else [block, blank], 1))
        for i, tile in enumerate(tiles, first):
            at = 128 * (i % 4 // 2)
            diag[rank * i : rank * (i + 1), at : at + 128] = tile


def up_kernel(x_hbm, basis_hbm, trans_hbm, one, two, own, tst_ref, diag, x_ref, basis_ref, trans_ref, flat, sems):
    points = x_hbm.shape[1]
    leaf_count, rank, leaf = basis_hbm.shape
    copies = [
        pltpu.make_async_copy(source, held, sems.at[n])
        for n, (source, held) in enumerate(
            ((trans_hbm, trans_ref), (basis_hbm, basis_ref), (x_hbm, x_ref))
        )
    ]
    for copy in copies:
        copy.start()
    copies[0].wait()
    for first in range(0, rank // 4, 4):
        blocks = [
            trans_ref[128 * step : 128 * step + 128, :].astype(F32).T
            for step in range(first, first + 4)
        ]
        for q in range(4):
            pieces = [block if q == 0 else pltpu.roll(block, 128 - 32 * q, 1) for block in blocks]
            for step, piece in enumerate(pieces, first):
                flat[pl.ds(4 * step + q, leaf_count, stride=rank), :] = piece
    tst_ref[...] = flat[:, 0:rank].astype(BF)
    copies[1].wait()
    fill_block_diagonal(basis_ref, diag)
    copies[2].wait()

    odd = lax.rem(lax.axis_index("leaf"), 2) == 1
    base = HALO * leaf // 128 * 64
    for t in range(HALO * leaf // 128):
        rows = slice(64 * t, 64 * t + 64)
        at = points - HALO * leaf + 128 * t
        head, tail = x_ref[:, 128 * t : 128 * t + 128], x_ref[:, at : at + 128]
        one[rows, :] = jnp.where(odd, head, tail)
        two[rows, :] = jnp.where(odd, tail, head)

    def put(at, left, right):
        rows = left.shape[0]
        both = jnp.where(low_half(rows), left, right)
        own[at : at + rows, :] = both
        one[base + at : base + at + rows, :] = both
        two[base + at : base + at + rows, :] = both

    parent_count = leaf_count // 8
    skels = []
    for quad in range(leaf_count // 4):
        x = x_ref[:, 256 * quad : 256 * quad + 256]
        skels.append(
            matmul_nt(
                diag[128 * quad : 128 * quad + 128, :], jnp.concatenate([x, x], 0)
            ).astype(BF)
        )
    parents = [
        matmul_tn(
            tst_ref[256 * p : 256 * p + 256, :], jnp.concatenate(skels[2 * p : 2 * p + 2], 0)
        ).astype(BF)
        for p in range(parent_count)
    ]
    for quad, skel in enumerate(skels):
        put(64 * quad, skel[:64], skel[64:])
    for m in range((parent_count + 1) // 2):
        put(16 * leaf_count + 32 * m, parents[2 * m], parents[min(2 * m + 1, parent_count - 1)])


def place(r, leaf_count):
    safe = jnp.minimum(r, leaf_count - 1)
    return pl.multiple_of((safe >> 2) * 64 + (safe & 1) * 32, 32), (safe >> 1) & 1


def join_kernel(base, own_ref, one_ref, out_ref):
    size = own_ref.shape[0]
    out_ref[:size, :] = own_ref[...]
    out_ref[size:, :] = one_ref[base:, :]


def near_kernel(
    x_hbm,
    one_ref,
    two_ref,
    near_ref,
    source_hbm,
    out_ref,
    x_ref,
    source_ref,
    held,
    twice,
    pair_a,
    pair_b,
    sems,
):
    leaf_count, leaf, depth = near_ref.shape
    count = source_hbm.shape[0]
    quads = leaf_count // 4
    copy_x = pltpu.make_async_copy(x_hbm, x_ref, sems.at[quads])
    copy_source = pltpu.make_async_copy(source_hbm, source_ref, sems.at[quads + 1])
    copy_x.start()
    copy_source.start()

    def copy(quad):
        part = pl.ds(4 * quad, 4)
        return pltpu.make_async_copy(near_ref.at[part], held.at[part], sems.at[quad])

    for quad in range(quads):
        copy(quad).start()

    low = low_half(leaf)

    def spread(parts):
        turned = [jnp.concatenate([value, value], 0).T for value, _ in parts]
        for (_, at), value in zip(parts, turned):
            twice[at] = value[:64]
            twice[at + 1] = value[64:]

    odd = lax.rem(lax.axis_index("leaf"), 2) == 1
    after = HALO + leaf_count
    at_one, at_two = jnp.where(odd, 0, after), jnp.where(odd, after, 0)
    for ref, at in ((one_ref, at_one), (two_ref, at_two)):
        spread([(ref[64 * n : 64 * n + 64, :], at + 2 * n) for n in range(HALO // 2)])
    copy_x.wait()
    for first in range(0, leaf_count // 2, 5):
        spread(
            [(x_ref[:, 128 * n : 128 * n + 128], HALO + 2 * n) for n in range(first, first + 5)]
        )
    copy_source.wait()

    def build(quad, stacked):
        for first in range(0, count, 3):
            some = range(first, min(first + 3, count))
            loaded = [
                [
                    (twice[source_ref[j, 4 * quad + t]], twice[source_ref[j, 4 * quad + t + 1]])
                    for t in (0, 2)
                ]
                for j in some
            ]
            for j, tiles in zip(some, loaded):
                for t, (left, right) in enumerate(tiles):
                    stacked[leaf * j : leaf * j + leaf, 128 * t : 128 * t + 128] = jnp.where(
                        low, left, right
                    )

    def multiply(quad, stacked):
        rows = held[pl.ds(4 * quad, 4)].reshape(4 * leaf, depth)
        total = matmul(rows, stacked[...])
        for t in range(2):
            tile = slice(128 * t, 128 * t + 128)
            upper, lower = total[128 * t : 128 * t + 64, tile], total[128 * t + 64 : 128 * t + 128, tile]
            lanes = pl.ds(pl.multiple_of(256 * quad + 128 * t, 128), 128)
            out_ref[:, lanes] = jnp.concatenate([upper, swapped(lower)], 0).T[:64]

    build(0, pair_a)

    def body(step, carry):
        quad = 2 * step
        copy(quad).wait()
        copy(quad + 1).wait()
        build(quad + 1, pair_b)
        multiply(quad, pair_a)
        build(jnp.minimum(quad + 2, quads - 1), pair_a)
        multiply(quad + 1, pair_b)
        return carry

    lax.fori_loop(0, quads // 2, body, 0)


def down_kernel(
    own_ref,
    one_ref,
    two_ref,
    three_ref,
    far_ref,
    two_over,
    three_over,
    far_over,
    req_ref,
    coup_source,
    par_source,
    coup_ref,
    par_ref,
    diag,
    tst_ref,
    near_ref,
    out_ref,
    slots,
    window,
    weights,
    stack,
    outs,
    leaf_outs,
):
    leaf_count, rank = coup_ref.shape[:2]
    parent_count = par_ref.shape[0]
    base = HALO // 2 * 64
    low64 = low_half(64)
    low = low_half(rank)
    odd = lax.rem(lax.axis_index("leaf"), 2) == 1

    def split(value, mask):
        other = swapped(value)
        return jnp.where(mask, value, other), jnp.where(mask, other, value)

    for first in range(0, leaf_count // 4, 5):
        quads = range(first, first + 5)
        values = [own_ref[64 * quad : 64 * quad + 64, :] for quad in quads]
        for quad, (left, right) in zip(quads, [split(value, low64) for value in values]):
            slots[4 * quad] = left[:32]
            slots[4 * quad + 1] = left[32:]
            slots[4 * quad + 2] = right[:32]
            slots[4 * quad + 3] = right[32:]

    def put_parents(ref, at, block):
        tiles = range((parent_count + 1) // 2)
        values = [ref[at + 32 * m : at + 32 * m + 32, :] for m in tiles]
        for m, (left, right) in zip(tiles, [split(value, low) for value in values]):
            window[parent_count * block + 2 * m] = left
            if 2 * m + 1 < parent_count:
                window[parent_count * block + 2 * m + 1] = right

    put_parents(own_ref, 16 * leaf_count, 4)
    outer = ((two_ref, base), (three_over, 0), (far_ref, 0), (far_ref, own_ref.shape[0]))
    inner = ((one_ref, base), (two_over, base), (three_ref, 0), (far_over, 0))
    for side, up in ((outer, odd), (inner, jnp.logical_not(odd))):
        for n, (ref, at) in enumerate(side):
            k = jnp.where(up, 4 + n, 3 - n)
            asked = [req_ref[k, c] for c in range(8)]
            places = [place(r, leaf_count) for r in asked]
            values = [ref[pl.ds(at + row, 32), :] for row, _ in places]
            others = [swapped(value) for value in values]
            for c, r in enumerate(asked):
                value = jnp.where(low == (places[c][1] == 0), values[c], others[c])
                slots[leaf_count + 8 * k + c] = jnp.where(
                    r < leaf_count, value, jnp.zeros_like(value)
                )
            put_parents(ref, at + 16 * leaf_count, jnp.where(up, 5 + n, 3 - n))

    per = par_source.shape[1]
    coup = coup_source.shape[0]
    pairs = [(2 * m, min(2 * m + 1, parent_count - 1)) for m in range((parent_count + 1) // 2)]
    for first in range(0, per, 4):
        loaded = [
            [(window[par_source[p, j]], window[par_source[q, j]]) for p, q in pairs]
            for j in range(first, first + 4)
        ]
        for j, tiles in enumerate(loaded, first):
            for m, (left, right) in enumerate(tiles):
                stack[rank * j : rank * j + rank, 128 * m : 128 * m + 128] = jnp.where(
                    low, left, right
                )
    rows = par_ref[...].reshape(parent_count * rank, per * rank)
    parent_outs = matmul(rows, stack[...]).astype(BF)
    for p in range(parent_count):
        tile = parent_outs[rank * p : rank * p + rank, 128 * (p // 2) : 128 * (p // 2) + 128]
        outs[p] = split(tile, low)[p % 2]

    def build(quad, carry):
        for first in range(0, coup, 4):
            loaded = [
                [
                    (slots[coup_source[j, 4 * quad + t]], slots[coup_source[j, 4 * quad + t + 1]])
                    for t in (0, 2)
                ]
                for j in range(first, first + 4)
            ]
            for j, tiles in enumerate(loaded, first):
                for t, (left, right) in enumerate(tiles):
                    weights[quad, rank * j : rank * j + rank, 128 * t : 128 * t + 128] = jnp.where(
                        low, left, right
                    )
        return carry

    quads = leaf_count // 4
    lax.fori_loop(0, quads, build, 0)
    downs = [
        matmul(tst_ref[256 * p : 256 * p + 256, :], outs[p]) for p in range(parent_count)
    ]
    for first in range(0, quads, 2):
        outs_of = []
        for quad in range(first, first + 2):
            rows = coup_ref[4 * quad : 4 * quad + 4].reshape(4 * rank, coup * rank)
            coupled = matmul(rows, weights[quad])
            coupled = jnp.concatenate([coupled[:64, :128], coupled[64:, 128:]], 0)
            down = downs[quad // 2][128 * (quad % 2) : 128 * (quad % 2) + 128]
            outs_of.append((coupled + down).astype(BF))
        for quad, leaf_out in enumerate(outs_of, first):
            leaf_outs[128 * quad : 128 * quad + 128, :] = leaf_out
    for first in range(0, quads, 2):
        tiles = []
        for quad in range(first, first + 2):
            rows = slice(128 * quad, 128 * quad + 128)
            far = matmul_tn(leaf_outs[rows, :], diag[rows, :])
            for t in range(2):
                lanes = slice(256 * quad + 128 * t, 256 * quad + 128 * t + 128)
                tile = jnp.where(
                    low64, far[:64, 128 * t : 128 * t + 128], far[64:, 128 * t : 128 * t + 128]
                )
                tiles.append((lanes, (near_ref[:, lanes] + tile).astype(BF)))
        for lanes, tile in tiles:
            out_ref[:, lanes] = tile


def in_hbm(array):
    return pltpu.with_memory_space_constraint(array, pltpu.HBM)


def params(mib):
    return pltpu.CompilerParams(vmem_limit_bytes=mib << 20)


def cost(flops, size):
    return pl.CostEstimate(flops=flops, bytes_accessed=size, transcendentals=0)


def shards(
    rhs,
    basis,
    transfer,
    near_rows,
    near_source,
    far_request,
    coup_rows,
    coup_source,
    par_rows,
    par_source,
):
    leaf_count, leaf, rank = basis.shape
    points, rhs_count = rhs.shape
    parent_count = par_rows.shape[0]
    near_count = near_source.shape[1]
    coup_count = coup_source.shape[1]
    base = HALO // 2 * rhs_count
    parent_rows = rank * ((parent_count + 1) // 2)
    packed = base + 16 * leaf_count + parent_rows
    count = lax.axis_size("leaf")

    x = rhs.T
    trans = transfer.transpose(1, 2, 0).reshape(rank * rank, leaf_count)
    shape = jax.ShapeDtypeStruct
    vmem, smem, hbm = (pl.BlockSpec(memory_space=kind) for kind in (VMEM, SMEM, pltpu.HBM))
    own_one, own_two, own, tst, diag = pl.pallas_call(
        up_kernel,
        out_shape=(
            shape((packed, 128), BF),
            shape((packed, 128), BF),
            shape((packed - base, 128), BF),
            shape((rank * leaf_count, rank), BF),
            shape((rank * leaf_count, 256), BF),
        ),
        in_specs=[hbm] * 3,
        out_specs=(vmem,) * 5,
        scratch_shapes=[
            VMEM(x.shape, BF),
            VMEM((leaf_count, rank, leaf), BF),
            VMEM(trans.shape, BF),
            VMEM((rank * leaf_count, 128), F32),
            DMA((3,)),
        ],
        compiler_params=params(8),
        cost_estimate=cost(10**9, 2 * 10**6),
        name="upward",
    )(in_hbm(x), in_hbm(basis.transpose(0, 2, 1)), in_hbm(trans))

    def exchange(block, begin, distance=1):
        pairs = [(i, i + distance) for i in range(begin, count - distance, 2)]
        return lax.ppermute(block, "leaf", pairs + [(b, a) for a, b in pairs])

    one = exchange(own_one, 0)
    two = exchange(own_two, 1)
    both = pl.pallas_call(
        functools.partial(join_kernel, base),
        out_shape=shape((2 * (packed - base), 128), BF),
        in_specs=[vmem] * 2,
        out_specs=vmem,
        compiler_params=params(8),
        cost_estimate=cost(10**6, 10**6),
        name="join",
    )(own, one)
    far = exchange(both, 1, 3)
    own, _ = lax.optimization_barrier((own, both))
    three = exchange(own, 0, 3)
    two_over = exchange(two, 0)

    near = pl.pallas_call(
        near_kernel,
        out_shape=shape((rhs_count, points), F32),
        in_specs=[hbm, vmem, vmem, hbm, hbm],
        out_specs=vmem,
        scratch_shapes=[
            VMEM(x.shape, BF),
            SMEM((near_count, leaf_count), jnp.int32),
            VMEM(near_rows.shape, BF),
            VMEM((leaf_count + 2 * HALO, leaf, 128), BF),
            VMEM((near_count * leaf, 256), BF),
            VMEM((near_count * leaf, 256), BF),
            DMA((leaf_count // 4 + 2,)),
        ],
        compiler_params=params(20),
        cost_estimate=cost(8 * 10**9, 10**7),
        name="near",
    )(in_hbm(x), one, two, in_hbm(near_rows), in_hbm(near_source.T))

    three, far, near = lax.optimization_barrier((three, far, near))
    three_over = exchange(three, 0)
    far_over = exchange(far, 0)

    product = pl.pallas_call(
        down_kernel,
        out_shape=shape((rhs_count, points), BF),
        in_specs=[vmem] * 8 + [smem] * 3 + [vmem] * 5,
        out_specs=vmem,
        scratch_shapes=[
            VMEM((leaf_count + 64, rank, 128), BF),
            VMEM((9 * parent_count, rank, 128), BF),
            VMEM((leaf_count // 4, coup_count * rank, 256), BF),
            VMEM((par_source.shape[1] * rank, 128 * ((parent_count + 1) // 2)), BF),
            VMEM((parent_count, rank, 128), BF),
            VMEM((rank * leaf_count, 128), BF),
        ],
        compiler_params=params(12),
        cost_estimate=cost(10**9, 4 * 10**6),
        name="downward",
    )(
        own,
        one,
        two,
        three,
        far,
        two_over,
        three_over,
        far_over,
        far_request[0],
        coup_source.T,
        par_source,
        coup_rows,
        par_rows,
        diag,
        tst,
        near,
    )
    return product.T


def solution(mesh):
    split = ("groups", "leaf")
    return jax.shard_map(
        shards,
        mesh=mesh,
        in_specs=(
            P(split, None),
            P(split, None, None),
            P(split, None, None),
            P(split, None, None),
            P(split, None),
            P(split, None, None),
            P(split, None, None),
            P(split, None),
            P(split, None, None),
            P(split, None),
        ),
        out_specs=P(split, None),
        check_vma=False,
    )
```

```python
import functools

import jax
import jax.numpy as jnp
from jax import lax
from jax.experimental import pallas as pl
from jax.experimental.pallas import tpu as pltpu
from jax.sharding import PartitionSpec as P

HALO = 16
BF = jnp.bfloat16
F32 = jnp.float32
VMEM = pltpu.VMEM
SMEM = pltpu.SMEM
DMA = pltpu.SemaphoreType.DMA


def low_half(rows):
    return lax.broadcasted_iota(jnp.int32, (rows, 128), 1) < 64


def swapped(value):
    return pltpu.roll(value, 64, 1)


def matmul(a, b):
    return jnp.dot(a, b, preferred_element_type=F32)


def matmul_nt(a, b):
    return lax.dot_general(a, b, (((1,), (1,)), ((), ())), preferred_element_type=F32)


def matmul_tn(a, b):
    return lax.dot_general(a, b, (((0,), (0,)), ((), ())), preferred_element_type=F32)


def fill_block_diagonal(basis_ref, diag):
    leaf_count, rank, leaf = basis_ref.shape
    blank = jnp.zeros((rank, leaf), BF)
    empty = jnp.zeros((rank, 2 * leaf), BF)
    for i in range(leaf_count):
        at = 128 * (1 - i % 4 // 2)
        diag[rank * i : rank * (i + 1), at : at + 128] = empty
    for first in range(0, leaf_count, 8):
        tiles = []
        for i in range(first, first + 8):
            block = basis_ref[i]
            tiles.append(jnp.concatenate([blank, block] if i % 2 else [block, blank], 1))
        for i, tile in enumerate(tiles, first):
            at = 128 * (i % 4 // 2)
            diag[rank * i : rank * (i + 1), at : at + 128] = tile


def load_kernel(x_hbm, basis_hbm, trans_hbm, x_ref, basis_ref, trans_ref, halo_ref, sems):
    odd = lax.rem(lax.axis_index("leaf"), 2) == 1
    width = halo_ref.shape[1]
    at = pl.multiple_of(jnp.where(odd, x_hbm.shape[1] - width, 0), 128)
    copies = [
        pltpu.make_async_copy(source, held, sems.at[n])
        for n, (source, held) in enumerate(
            (
                (x_hbm.at[:, pl.ds(at, width)], halo_ref),
                (x_hbm, x_ref),
                (basis_hbm, basis_ref),
                (trans_hbm, trans_ref),
            )
        )
    ]
    for copy in copies:
        copy.start()
    for copy in copies:
        copy.wait()


def up_kernel(x_ref, basis_ref, trans_ref, side, own, tst_ref, diag, flat):
    points = x_ref.shape[1]
    leaf_count, rank, leaf = basis_ref.shape
    for first in range(0, rank // 4, 4):
        blocks = [
            trans_ref[128 * step : 128 * step + 128, :].astype(F32).T
            for step in range(first, first + 4)
        ]
        for q in range(4):
            pieces = [block if q == 0 else pltpu.roll(block, 128 - 32 * q, 1) for block in blocks]
            for step, piece in enumerate(pieces, first):
                flat[pl.ds(4 * step + q, leaf_count, stride=rank), :] = piece
    tst_ref[...] = flat[:, 0:rank].astype(BF)
    fill_block_diagonal(basis_ref, diag)

    odd = lax.rem(lax.axis_index("leaf"), 2) == 1
    base = HALO * leaf // 128 * 64
    for t in range(HALO * leaf // 128):
        rows = slice(64 * t, 64 * t + 64)
        at = points - HALO * leaf + 128 * t
        head, tail = x_ref[:, 128 * t : 128 * t + 128], x_ref[:, at : at + 128]
        side[rows, :] = jnp.where(odd, head, tail)

    def put(at, left, right):
        rows = left.shape[0]
        both = jnp.where(low_half(rows), left, right)
        own[at : at + rows, :] = both
        side[base + at : base + at + rows, :] = both

    parent_count = leaf_count // 8
    skels = []
    for quad in range(leaf_count // 4):
        x = x_ref[:, 256 * quad : 256 * quad + 256]
        skels.append(
            matmul_nt(
                diag[128 * quad : 128 * quad + 128, :], jnp.concatenate([x, x], 0)
            ).astype(BF)
        )
    parents = [
        matmul_tn(
            tst_ref[256 * p : 256 * p + 256, :], jnp.concatenate(skels[2 * p : 2 * p + 2], 0)
        ).astype(BF)
        for p in range(parent_count)
    ]
    for quad, skel in enumerate(skels):
        put(64 * quad, skel[:64], skel[64:])
    for m in range((parent_count + 1) // 2):
        put(16 * leaf_count + 32 * m, parents[2 * m], parents[min(2 * m + 1, parent_count - 1)])


def place(r, leaf_count):
    safe = jnp.minimum(r, leaf_count - 1)
    return pl.multiple_of((safe >> 2) * 64 + (safe & 1) * 32, 32), (safe >> 1) & 1


def join_kernel(base, own_ref, one_ref, out_ref):
    size = own_ref.shape[0]
    out_ref[:size, :] = own_ref[...]
    out_ref[size:, :] = one_ref[base:, :]


def near_kernel(
    x_ref,
    one_ref,
    two_ref,
    near_ref,
    source_hbm,
    out_ref,
    source_ref,
    held,
    twice,
    pair_a,
    pair_b,
    sems,
):
    leaf_count, leaf, depth = near_ref.shape
    count = source_hbm.shape[0]
    quads = leaf_count // 4
    copy_source = pltpu.make_async_copy(source_hbm, source_ref, sems.at[quads])
    copy_source.start()

    def copy(quad):
        part = pl.ds(4 * quad, 4)
        return pltpu.make_async_copy(near_ref.at[part], held.at[part], sems.at[quad])

    for quad in range(quads):
        copy(quad).start()

    low = low_half(leaf)

    def spread(parts):
        others = [swapped(value) for value, _ in parts]
        for (value, at), other in zip(parts, others):
            twice[at] = jnp.where(low, value, other)
            twice[at + 1] = jnp.where(low, other, value)

    odd = lax.rem(lax.axis_index("leaf"), 2) == 1
    after = HALO + leaf_count
    at_one, at_two = jnp.where(odd, 0, after), jnp.where(odd, after, 0)
    halos = range(HALO // 2)
    spread([(one_ref[64 * n : 64 * n + 64, :], at_one + 2 * n) for n in halos])
    spread([(two_ref[:, 128 * n : 128 * n + 128], at_two + 2 * n) for n in halos])
    for first in range(0, leaf_count // 2, 5):
        spread(
            [(x_ref[:, 128 * n : 128 * n + 128], HALO + 2 * n) for n in range(first, first + 5)]
        )
    copy_source.wait()

    def build(quad, stacked):
        for u in range(4):
            i = 4 * quad + u
            rows = slice(64 * u, 64 * u + 64)
            pairs = [(2 * m, min(2 * m + 1, count - 1)) for m in range((count + 1) // 2)]
            for first in range(0, len(pairs), 5):
                some = pairs[first : first + 5]
                loaded = [(twice[source_ref[a, i]], twice[source_ref[b, i]]) for a, b in some]
                for m, (left, right) in enumerate(loaded, first):
                    stacked[rows, 128 * m : 128 * m + 128] = jnp.where(low, left, right)

    def multiply(quad, stacked):
        rows = held[pl.ds(4 * quad, 4)].reshape(4 * leaf, depth)
        total = matmul_nt(stacked[:, :depth], rows)
        for t in range(2):
            lanes = pl.ds(pl.multiple_of(256 * quad + 128 * t, 128), 128)
            out_ref[:, lanes] = jnp.where(
                low,
                total[128 * t : 128 * t + 64, 128 * t : 128 * t + 128],
                total[128 * t + 64 : 128 * t + 128, 128 * t : 128 * t + 128],
            )

    build(0, pair_a)

    def body(step, carry):
        quad = 2 * step
        copy(quad).wait()
        copy(quad + 1).wait()
        build(quad + 1, pair_b)
        multiply(quad, pair_a)
        build(jnp.minimum(quad + 2, quads - 1), pair_a)
        multiply(quad + 1, pair_b)
        return carry

    lax.fori_loop(0, quads // 2, body, 0)


def down_kernel(
    own_ref,
    one_ref,
    three_ref,
    far_ref,
    three_over,
    far_over,
    req_ref,
    coup_source,
    par_source,
    coup_ref,
    par_ref,
    diag,
    tst_ref,
    near_ref,
    out_ref,
    slots,
    window,
    weights,
    stack,
    outs,
    leaf_outs,
):
    leaf_count, rank = coup_ref.shape[:2]
    parent_count = par_ref.shape[0]
    base = HALO // 2 * 64
    low64 = low_half(64)
    low = low_half(rank)
    odd = lax.rem(lax.axis_index("leaf"), 2) == 1

    def split(value, mask):
        other = swapped(value)
        return jnp.where(mask, value, other), jnp.where(mask, other, value)

    for first in range(0, leaf_count // 4, 5):
        quads = range(first, first + 5)
        values = [own_ref[64 * quad : 64 * quad + 64, :] for quad in quads]
        for quad, (left, right) in zip(quads, [split(value, low64) for value in values]):
            slots[4 * quad] = left[:32]
            slots[4 * quad + 1] = left[32:]
            slots[4 * quad + 2] = right[:32]
            slots[4 * quad + 3] = right[32:]

    def put_parents(ref, at, block):
        tiles = range((parent_count + 1) // 2)
        values = [ref[at + 32 * m : at + 32 * m + 32, :] for m in tiles]
        for m, (left, right) in zip(tiles, [split(value, low) for value in values]):
            window[parent_count * block + 2 * m] = left
            if 2 * m + 1 < parent_count:
                window[parent_count * block + 2 * m + 1] = right

    put_parents(own_ref, 16 * leaf_count, 4)
    size = own_ref.shape[0]
    outer = ((three_over, size), (three_over, 0), (far_ref, 0), (far_ref, size))
    inner = ((one_ref, base), (three_ref, size), (three_ref, 0), (far_over, 0))
    for side, up in ((outer, odd), (inner, jnp.logical_not(odd))):
        for n, (ref, at) in enumerate(side):
            k = jnp.where(up, 4 + n, 3 - n)
            asked = [req_ref[k, c] for c in range(8)]
            places = [place(r, leaf_count) for r in asked]
            values = [ref[pl.ds(at + row, 32), :] for row, _ in places]
            others = [swapped(value) for value in values]
            for c, r in enumerate(asked):
                value = jnp.where(low == (places[c][1] == 0), values[c], others[c])
                slots[leaf_count + 8 * k + c] = jnp.where(
                    r < leaf_count, value, jnp.zeros_like(value)
                )
            put_parents(ref, at + 16 * leaf_count, jnp.where(up, 5 + n, 3 - n))

    per = par_source.shape[1]
    coup = coup_source.shape[0]
    pairs = [(2 * m, min(2 * m + 1, parent_count - 1)) for m in range((parent_count + 1) // 2)]
    for first in range(0, per, 4):
        loaded = [
            [(window[par_source[p, j]], window[par_source[q, j]]) for p, q in pairs]
            for j in range(first, first + 4)
        ]
        for j, tiles in enumerate(loaded, first):
            for m, (left, right) in enumerate(tiles):
                stack[rank * j : rank * j + rank, 128 * m : 128 * m + 128] = jnp.where(
                    low, left, right
                )
    rows = par_ref[...].reshape(parent_count * rank, per * rank)
    parent_outs = matmul(rows, stack[...]).astype(BF)
    for p in range(parent_count):
        tile = parent_outs[rank * p : rank * p + rank, 128 * (p // 2) : 128 * (p // 2) + 128]
        outs[p] = split(tile, low)[p % 2]

    def build(quad, carry):
        for first in range(0, coup, 4):
            loaded = [
                [
                    (slots[coup_source[j, 4 * quad + t]], slots[coup_source[j, 4 * quad + t + 1]])
                    for t in (0, 2)
                ]
                for j in range(first, first + 4)
            ]
            for j, tiles in enumerate(loaded, first):
                for t, (left, right) in enumerate(tiles):
                    weights[quad, rank * j : rank * j + rank, 128 * t : 128 * t + 128] = jnp.where(
                        low, left, right
                    )
        return carry

    quads = leaf_count // 4
    lax.fori_loop(0, quads, build, 0)
    downs = [
        matmul(tst_ref[256 * p : 256 * p + 256, :], outs[p]) for p in range(parent_count)
    ]
    for first in range(0, quads, 2):
        outs_of = []
        for quad in range(first, first + 2):
            rows = coup_ref[4 * quad : 4 * quad + 4].reshape(4 * rank, coup * rank)
            coupled = matmul(rows, weights[quad])
            coupled = jnp.concatenate([coupled[:64, :128], coupled[64:, 128:]], 0)
            down = downs[quad // 2][128 * (quad % 2) : 128 * (quad % 2) + 128]
            outs_of.append((coupled + down).astype(BF))
        for quad, leaf_out in enumerate(outs_of, first):
            leaf_outs[128 * quad : 128 * quad + 128, :] = leaf_out
    for first in range(0, quads, 2):
        tiles = []
        for quad in range(first, first + 2):
            rows = slice(128 * quad, 128 * quad + 128)
            far = matmul_tn(leaf_outs[rows, :], diag[rows, :])
            for t in range(2):
                lanes = slice(256 * quad + 128 * t, 256 * quad + 128 * t + 128)
                tile = jnp.where(
                    low64, far[:64, 128 * t : 128 * t + 128], far[64:, 128 * t : 128 * t + 128]
                )
                tiles.append((lanes, (near_ref[:, lanes] + tile).astype(BF)))
        for lanes, tile in tiles:
            out_ref[:, lanes] = tile


def in_hbm(array):
    return pltpu.with_memory_space_constraint(array, pltpu.HBM)


def params(mib):
    return pltpu.CompilerParams(vmem_limit_bytes=mib << 20)


def cost(flops, size):
    return pl.CostEstimate(flops=flops, bytes_accessed=size, transcendentals=0)


def shards(
    rhs,
    basis,
    transfer,
    near_rows,
    near_source,
    far_request,
    coup_rows,
    coup_source,
    par_rows,
    par_source,
):
    leaf_count, leaf, rank = basis.shape
    points, rhs_count = rhs.shape
    parent_count = par_rows.shape[0]
    near_count = near_source.shape[1]
    coup_count = coup_source.shape[1]
    base = HALO // 2 * rhs_count
    parent_rows = rank * ((parent_count + 1) // 2)
    packed = base + 16 * leaf_count + parent_rows
    count = lax.axis_size("leaf")

    x = rhs.T
    trans = transfer.transpose(1, 2, 0).reshape(rank * rank, leaf_count)
    shape = jax.ShapeDtypeStruct
    vmem, smem, hbm = (pl.BlockSpec(memory_space=kind) for kind in (VMEM, SMEM, pltpu.HBM))
    basis_t = basis.transpose(0, 2, 1)
    x, basis_t, trans, halo = pl.pallas_call(
        load_kernel,
        out_shape=tuple(
            shape(dims, BF) for dims in (x.shape, basis_t.shape, trans.shape, (rhs_count, HALO * leaf))
        ),
        in_specs=[hbm] * 3,
        out_specs=(vmem,) * 4,
        scratch_shapes=[DMA((4,))],
        compiler_params=params(8),
        cost_estimate=cost(10**6, 2 * 10**6),
        name="load",
    )(in_hbm(x), in_hbm(basis_t), in_hbm(trans))

    def exchange(block, begin, distance=1):
        pairs = [(i, i + distance) for i in range(begin, count - distance, 2)]
        return lax.ppermute(block, "leaf", pairs + [(b, a) for a, b in pairs])

    two = exchange(halo, 1)
    side, own, tst, diag = pl.pallas_call(
        up_kernel,
        out_shape=(
            shape((packed, 128), BF),
            shape((packed - base, 128), BF),
            shape((rank * leaf_count, rank), BF),
            shape((rank * leaf_count, 256), BF),
        ),
        in_specs=[vmem] * 3,
        out_specs=(vmem,) * 4,
        scratch_shapes=[VMEM((rank * leaf_count, 128), F32)],
        compiler_params=params(8),
        cost_estimate=cost(10**9, 2 * 10**6),
        name="upward",
    )(x, basis_t, trans)
    one = exchange(side, 0)
    both = pl.pallas_call(
        functools.partial(join_kernel, base),
        out_shape=shape((2 * (packed - base), 128), BF),
        in_specs=[vmem] * 2,
        out_specs=vmem,
        compiler_params=params(8),
        cost_estimate=cost(10**6, 10**6),
        name="join",
    )(own, one)
    three = exchange(both, 0, 3)
    far = exchange(both, 1, 3)

    near = pl.pallas_call(
        near_kernel,
        out_shape=shape((rhs_count, points), F32),
        in_specs=[vmem, vmem, vmem, hbm, hbm],
        out_specs=vmem,
        scratch_shapes=[
            SMEM((near_count, leaf_count), jnp.int32),
            VMEM(near_rows.shape, BF),
            VMEM((leaf_count + 2 * HALO, leaf, 128), BF),
            VMEM((256, 128 * ((near_count + 1) // 2)), BF),
            VMEM((256, 128 * ((near_count + 1) // 2)), BF),
            DMA((leaf_count // 4 + 1,)),
        ],
        compiler_params=params(20),
        cost_estimate=cost(8 * 10**9, 10**7),
        name="near",
    )(x, one, two, in_hbm(near_rows), in_hbm(near_source.T))

    three, far, near = lax.optimization_barrier((three, far, near))
    three_over = exchange(three, 0)
    far_over = exchange(far, 0)

    product = pl.pallas_call(
        down_kernel,
        out_shape=shape((rhs_count, points), BF),
        in_specs=[vmem] * 6 + [smem] * 3 + [vmem] * 5,
        out_specs=vmem,
        scratch_shapes=[
            VMEM((leaf_count + 64, rank, 128), BF),
            VMEM((9 * parent_count, rank, 128), BF),
            VMEM((leaf_count // 4, coup_count * rank, 256), BF),
            VMEM((par_source.shape[1] * rank, 128 * ((parent_count + 1) // 2)), BF),
            VMEM((parent_count, rank, 128), BF),
            VMEM((rank * leaf_count, 128), BF),
        ],
        compiler_params=params(12),
        cost_estimate=cost(10**9, 4 * 10**6),
        name="downward",
    )(
        own,
        one,
        three,
        far,
        three_over,
        far_over,
        far_request[0],
        coup_source.T,
        par_source,
        coup_rows,
        par_rows,
        diag,
        tst,
        near,
    )
    return product.T


def solution(mesh):
    split = ("groups", "leaf")
    return jax.shard_map(
        shards,
        mesh=mesh,
        in_specs=(
            P(split, None),
            P(split, None, None),
            P(split, None, None),
            P(split, None, None),
            P(split, None),
            P(split, None, None),
            P(split, None, None),
            P(split, None),
            P(split, None, None),
            P(split, None),
        ),
        out_specs=P(split, None),
        check_vma=False,
    )
```

```python
import functools

import jax
import jax.numpy as jnp
from jax import lax
from jax.experimental import pallas as pl
from jax.experimental.pallas import tpu as pltpu
from jax.sharding import PartitionSpec as P

HALO = 16
BF = jnp.bfloat16
F32 = jnp.float32
VMEM = pltpu.VMEM
SMEM = pltpu.SMEM
DMA = pltpu.SemaphoreType.DMA


def low_half(rows):
    return lax.broadcasted_iota(jnp.int32, (rows, 128), 1) < 64


def swapped(value):
    return pltpu.roll(value, 64, 1)


def matmul(a, b):
    return jnp.dot(a, b, preferred_element_type=F32)


def matmul_nt(a, b):
    return lax.dot_general(a, b, (((1,), (1,)), ((), ())), preferred_element_type=F32)


def matmul_tn(a, b):
    return lax.dot_general(a, b, (((0,), (0,)), ((), ())), preferred_element_type=F32)


def fill_block_diagonal(basis_ref, diag):
    leaf_count, rank, leaf = basis_ref.shape
    blank = jnp.zeros((rank, leaf), BF)
    empty = jnp.zeros((rank, 2 * leaf), BF)
    for i in range(leaf_count):
        at = 128 * (1 - i % 4 // 2)
        diag[rank * i : rank * (i + 1), at : at + 128] = empty
    for first in range(0, leaf_count, 8):
        tiles = []
        for i in range(first, first + 8):
            block = basis_ref[i]
            tiles.append(jnp.concatenate([blank, block] if i % 2 else [block, blank], 1))
        for i, tile in enumerate(tiles, first):
            at = 128 * (i % 4 // 2)
            diag[rank * i : rank * (i + 1), at : at + 128] = tile


def load_kernel(*refs):
    count = len(refs) // 2
    sems = refs[-1]
    copies = [
        pltpu.make_async_copy(refs[n], refs[count + n], sems.at[n]) for n in range(count)
    ]
    for copy in copies:
        copy.start()
    for copy in copies:
        copy.wait()


def up_kernel(
    x_ref, basis_ref, trans_ref, own_ask, other_ask, side, halo_ref, own, tst_ref, diag, flat, ask
):
    points = x_ref.shape[1]
    leaf_count, rank, leaf = basis_ref.shape
    for first in range(0, rank // 4, 4):
        blocks = [
            trans_ref[128 * step : 128 * step + 128, :].astype(F32).T
            for step in range(first, first + 4)
        ]
        for q in range(4):
            pieces = [block if q == 0 else pltpu.roll(block, 128 - 32 * q, 1) for block in blocks]
            for step, piece in enumerate(pieces, first):
                flat[pl.ds(4 * step + q, leaf_count, stride=rank), :] = piece
    tst_ref[...] = flat[:, 0:rank].astype(BF)
    fill_block_diagonal(basis_ref, diag)

    odd = lax.rem(lax.axis_index("leaf"), 2) == 1
    base = HALO * leaf // 128 * 64
    for t in range(HALO * leaf // 128):
        rows = slice(64 * t, 64 * t + 64)
        at = points - HALO * leaf + 128 * t
        head, tail = x_ref[:, 128 * t : 128 * t + 128], x_ref[:, at : at + 128]
        side[rows, :] = jnp.where(odd, head, tail)
        halo_ref[:, 128 * t : 128 * t + 128] = jnp.where(odd, tail, head)
    ask[...] = jnp.zeros(ask.shape, F32)
    ask[0:8, 0:8] = own_ask[...].astype(F32)
    ask[16:24, 0:8] = other_ask[...].astype(F32)
    halo_ref[:, HALO * leaf :] = ask[...].astype(BF)

    def put(at, left, right):
        rows = left.shape[0]
        both = jnp.where(low_half(rows), left, right)
        own[at : at + rows, :] = both
        side[base + at : base + at + rows, :] = both

    parent_count = leaf_count // 8
    skels = []
    for quad in range(leaf_count // 4):
        x = x_ref[:, 256 * quad : 256 * quad + 256]
        skels.append(
            matmul_nt(
                diag[128 * quad : 128 * quad + 128, :], jnp.concatenate([x, x], 0)
            ).astype(BF)
        )
    parents = [
        matmul_tn(
            tst_ref[256 * p : 256 * p + 256, :], jnp.concatenate(skels[2 * p : 2 * p + 2], 0)
        ).astype(BF)
        for p in range(parent_count)
    ]
    for quad, skel in enumerate(skels):
        put(64 * quad, skel[:64], skel[64:])
    for m in range((parent_count + 1) // 2):
        put(16 * leaf_count + 32 * m, parents[2 * m], parents[min(2 * m + 1, parent_count - 1)])


def place(r, leaf_count):
    safe = jnp.minimum(r, leaf_count - 1)
    return pl.multiple_of((safe >> 2) * 64 + (safe & 1) * 32, 32), (safe >> 1) & 1


def pick(ref, base, r, leaf_count, want_high):
    row, high = place(r, leaf_count)
    value = ref[pl.ds(base + row, 32), :]
    value = jnp.where(high != want_high, swapped(value), value)
    return jnp.where(r < leaf_count, value, jnp.zeros_like(value))


def reply_kernel(leaf_count, base, got_ref, own_ref, one_ref, out_ref, ints, nums, sem):
    width = HALO // 2 * 128
    ints[...] = got_ref[0:32, width:].astype(F32).astype(jnp.int32)
    copy = pltpu.make_async_copy(ints, nums, sem)
    copy.start()
    parents = 16 * leaf_count
    size = own_ref.shape[0] - parents
    blocks = ((own_ref, 0), (one_ref, base))
    for n, (ref, at) in enumerate(blocks):
        out_ref[512 + size * n : 512 + size * (n + 1), :] = ref[at + parents : at + parents + size, :]
    odd = lax.rem(lax.axis_index("leaf"), 2) == 1
    low = low_half(32)
    copy.wait()
    for asker in range(2):
        for n, (ref, at) in enumerate(blocks):
            reach = 1 + asker + n
            k = jnp.where(odd, 4 - reach, 3 + reach)
            asked = [nums[16 * asker + k, c] for c in range(8)]
            values = [pick(ref, at, r, leaf_count, c % 2) for c, r in enumerate(asked)]
            for m in range(4):
                row = 256 * asker + 128 * n + 32 * m
                out_ref[row : row + 32, :] = jnp.where(low, values[2 * m], values[2 * m + 1])


def join_kernel(base, own_ref, one_ref, out_ref):
    size = own_ref.shape[0]
    out_ref[:size, :] = own_ref[...]
    out_ref[size:, :] = one_ref[base:, :]


def near_kernel(
    x_ref,
    one_ref,
    two_ref,
    near_ref,
    source_hbm,
    out_ref,
    source_ref,
    held,
    twice,
    pair_a,
    pair_b,
    sems,
):
    leaf_count, leaf, depth = near_ref.shape
    count = source_hbm.shape[0]
    quads = leaf_count // 4
    copy_source = pltpu.make_async_copy(source_hbm, source_ref, sems.at[quads])
    copy_source.start()

    def copy(quad):
        part = pl.ds(4 * quad, 4)
        return pltpu.make_async_copy(near_ref.at[part], held.at[part], sems.at[quad])

    for quad in range(quads):
        copy(quad).start()

    low = low_half(leaf)

    def spread(parts):
        others = [swapped(value) for value, _ in parts]
        for (value, at), other in zip(parts, others):
            twice[at] = jnp.where(low, value, other)
            twice[at + 1] = jnp.where(low, other, value)

    odd = lax.rem(lax.axis_index("leaf"), 2) == 1
    after = HALO + leaf_count
    at_one, at_two = jnp.where(odd, 0, after), jnp.where(odd, after, 0)
    halos = range(HALO // 2)
    spread([(one_ref[64 * n : 64 * n + 64, :], at_one + 2 * n) for n in halos])
    spread([(two_ref[:, 128 * n : 128 * n + 128], at_two + 2 * n) for n in halos])
    for first in range(0, leaf_count // 2, 5):
        spread(
            [(x_ref[:, 128 * n : 128 * n + 128], HALO + 2 * n) for n in range(first, first + 5)]
        )
    copy_source.wait()

    def build(quad, stacked):
        for u in range(4):
            i = 4 * quad + u
            rows = slice(64 * u, 64 * u + 64)
            pairs = [(2 * m, min(2 * m + 1, count - 1)) for m in range((count + 1) // 2)]
            for first in range(0, len(pairs), 5):
                some = pairs[first : first + 5]
                loaded = [(twice[source_ref[a, i]], twice[source_ref[b, i]]) for a, b in some]
                for m, (left, right) in enumerate(loaded, first):
                    stacked[rows, 128 * m : 128 * m + 128] = jnp.where(low, left, right)

    def multiply(quad, stacked):
        rows = held[pl.ds(4 * quad, 4)].reshape(4 * leaf, depth)
        total = matmul_nt(stacked[:, :depth], rows)
        for t in range(2):
            lanes = pl.ds(pl.multiple_of(256 * quad + 128 * t, 128), 128)
            out_ref[:, lanes] = jnp.where(
                low,
                total[128 * t : 128 * t + 64, 128 * t : 128 * t + 128],
                total[128 * t + 64 : 128 * t + 128, 128 * t : 128 * t + 128],
            )

    build(0, pair_a)

    def body(step, carry):
        quad = 2 * step
        copy(quad).wait()
        copy(quad + 1).wait()
        build(quad + 1, pair_b)
        multiply(quad, pair_a)
        build(jnp.minimum(quad + 2, quads - 1), pair_a)
        multiply(quad + 1, pair_b)
        return carry

    lax.fori_loop(0, quads // 2, body, 0)


def down_kernel(
    own_ref,
    one_ref,
    three_ref,
    far_ref,
    three_over,
    far_over,
    req_ref,
    coup_source,
    par_source,
    coup_ref,
    par_ref,
    diag,
    tst_ref,
    near_ref,
    out_ref,
    slots,
    window,
    weights,
    stack,
    outs,
    leaf_outs,
):
    leaf_count, rank = coup_ref.shape[:2]
    parent_count = par_ref.shape[0]
    base = HALO // 2 * 64
    low64 = low_half(64)
    low = low_half(rank)
    odd = lax.rem(lax.axis_index("leaf"), 2) == 1

    def split(value, mask):
        other = swapped(value)
        return jnp.where(mask, value, other), jnp.where(mask, other, value)

    for first in range(0, leaf_count // 4, 5):
        quads = range(first, first + 5)
        values = [own_ref[64 * quad : 64 * quad + 64, :] for quad in quads]
        for quad, (left, right) in zip(quads, [split(value, low64) for value in values]):
            slots[4 * quad] = left[:32]
            slots[4 * quad + 1] = left[32:]
            slots[4 * quad + 2] = right[:32]
            slots[4 * quad + 3] = right[32:]

    def put_parents(ref, at, block):
        tiles = range((parent_count + 1) // 2)
        values = [ref[at + 32 * m : at + 32 * m + 32, :] for m in tiles]
        for m, (left, right) in zip(tiles, [split(value, low) for value in values]):
            window[parent_count * block + 2 * m] = left
            if 2 * m + 1 < parent_count:
                window[parent_count * block + 2 * m + 1] = right

    put_parents(own_ref, 16 * leaf_count, 4)
    size = own_ref.shape[0]
    parents = 16 * leaf_count
    parent_size = size - parents
    inward = jnp.logical_not(odd)
    for ref, at, reach, up in (
        (one_ref, base, 1, inward),
        (far_ref, 0, 3, odd),
        (far_ref, size, 4, odd),
        (far_over, 0, 4, inward),
    ):
        k = jnp.where(up, 3 + reach, 4 - reach)
        asked = [req_ref[k, c] for c in range(8)]
        places = [place(r, leaf_count) for r in asked]
        values = [ref[pl.ds(at + row, 32), :] for row, _ in places]
        others = [swapped(value) for value in values]
        for c, r in enumerate(asked):
            value = jnp.where(low == (places[c][1] == 0), values[c], others[c])
            slots[leaf_count + 8 * k + c] = jnp.where(r < leaf_count, value, jnp.zeros_like(value))
        put_parents(ref, at + parents, jnp.where(up, 4 + reach, 4 - reach))
    for ref, up, first in ((three_ref, odd, 0), (three_over, inward, 1)):
        for n in range(2):
            reach = 1 + first + n
            at = leaf_count + 8 * jnp.where(up, 3 + reach, 4 - reach)
            rows = 256 * first + 128 * n
            values = [ref[rows + 32 * m : rows + 32 * m + 32, :] for m in range(4)]
            for m, (left, right) in enumerate([split(value, low) for value in values]):
                slots[at + 2 * m] = left
                slots[at + 2 * m + 1] = right
            put_parents(ref, 512 + parent_size * n, jnp.where(up, 4 + reach, 4 - reach))

    per = par_source.shape[1]
    coup = coup_source.shape[0]
    pairs = [(2 * m, min(2 * m + 1, parent_count - 1)) for m in range((parent_count + 1) // 2)]
    for first in range(0, per, 4):
        loaded = [
            [(window[par_source[p, j]], window[par_source[q, j]]) for p, q in pairs]
            for j in range(first, first + 4)
        ]
        for j, tiles in enumerate(loaded, first):
            for m, (left, right) in enumerate(tiles):
                stack[rank * j : rank * j + rank, 128 * m : 128 * m + 128] = jnp.where(
                    low, left, right
                )
    rows = par_ref[...].reshape(parent_count * rank, per * rank)
    parent_outs = matmul(rows, stack[...]).astype(BF)
    for p in range(parent_count):
        tile = parent_outs[rank * p : rank * p + rank, 128 * (p // 2) : 128 * (p // 2) + 128]
        outs[p] = split(tile, low)[p % 2]

    def build(quad, carry):
        for first in range(0, coup, 4):
            loaded = [
                [
                    (slots[coup_source[j, 4 * quad + t]], slots[coup_source[j, 4 * quad + t + 1]])
                    for t in (0, 2)
                ]
                for j in range(first, first + 4)
            ]
            for j, tiles in enumerate(loaded, first):
                for t, (left, right) in enumerate(tiles):
                    weights[quad, rank * j : rank * j + rank, 128 * t : 128 * t + 128] = jnp.where(
                        low, left, right
                    )
        return carry

    quads = leaf_count // 4
    lax.fori_loop(0, quads, build, 0)
    downs = [
        matmul(tst_ref[256 * p : 256 * p + 256, :], outs[p]) for p in range(parent_count)
    ]
    for first in range(0, quads, 2):
        outs_of = []
        for quad in range(first, first + 2):
            rows = coup_ref[4 * quad : 4 * quad + 4].reshape(4 * rank, coup * rank)
            coupled = matmul(rows, weights[quad])
            coupled = jnp.concatenate([coupled[:64, :128], coupled[64:, 128:]], 0)
            down = downs[quad // 2][128 * (quad % 2) : 128 * (quad % 2) + 128]
            outs_of.append((coupled + down).astype(BF))
        for quad, leaf_out in enumerate(outs_of, first):
            leaf_outs[128 * quad : 128 * quad + 128, :] = leaf_out
    for first in range(0, quads, 2):
        tiles = []
        for quad in range(first, first + 2):
            rows = slice(128 * quad, 128 * quad + 128)
            far = matmul_tn(leaf_outs[rows, :], diag[rows, :])
            for t in range(2):
                lanes = slice(256 * quad + 128 * t, 256 * quad + 128 * t + 128)
                tile = jnp.where(
                    low64, far[:64, 128 * t : 128 * t + 128], far[64:, 128 * t : 128 * t + 128]
                )
                tiles.append((lanes, (near_ref[:, lanes] + tile).astype(BF)))
        for lanes, tile in tiles:
            out_ref[:, lanes] = tile


def in_hbm(array):
    return pltpu.with_memory_space_constraint(array, pltpu.HBM)


def params(mib):
    return pltpu.CompilerParams(vmem_limit_bytes=mib << 20)


def cost(flops, size):
    return pl.CostEstimate(flops=flops, bytes_accessed=size, transcendentals=0)


def shards(
    rhs,
    basis,
    transfer,
    near_rows,
    near_source,
    far_request,
    coup_rows,
    coup_source,
    par_rows,
    par_source,
):
    leaf_count, leaf, rank = basis.shape
    points, rhs_count = rhs.shape
    parent_count = par_rows.shape[0]
    near_count = near_source.shape[1]
    coup_count = coup_source.shape[1]
    base = HALO // 2 * rhs_count
    parent_rows = rank * ((parent_count + 1) // 2)
    packed = base + 16 * leaf_count + parent_rows
    count = lax.axis_size("leaf")

    x = rhs.T
    trans = transfer.transpose(1, 2, 0).reshape(rank * rank, leaf_count)
    shape = jax.ShapeDtypeStruct
    vmem, smem, hbm = (pl.BlockSpec(memory_space=kind) for kind in (VMEM, SMEM, pltpu.HBM))
    basis_t = basis.transpose(0, 2, 1)
    requests = far_request[0]
    inputs = (x, basis_t, trans, requests)
    x, basis_t, trans, own_ask = pl.pallas_call(
        load_kernel,
        out_shape=tuple(shape(held.shape, held.dtype) for held in inputs),
        in_specs=[hbm] * 4,
        out_specs=(vmem,) * 4,
        scratch_shapes=[DMA((4,))],
        compiler_params=params(8),
        cost_estimate=cost(10**6, 2 * 10**6),
        name="load",
    )(*(in_hbm(held) for held in inputs))

    def exchange(block, begin, distance=1):
        pairs = [(i, i + distance) for i in range(begin, count - distance, 2)]
        return lax.ppermute(block, "leaf", pairs + [(b, a) for a, b in pairs])

    side, halo, own, tst, diag = pl.pallas_call(
        up_kernel,
        out_shape=(
            shape((packed, 128), BF),
            shape((rhs_count, HALO * leaf + 128), BF),
            shape((packed - base, 128), BF),
            shape((rank * leaf_count, rank), BF),
            shape((rank * leaf_count, 256), BF),
        ),
        in_specs=[vmem] * 5,
        out_specs=(vmem,) * 5,
        scratch_shapes=[VMEM((rank * leaf_count, 128), F32), VMEM((rhs_count, 128), F32)],
        compiler_params=params(8),
        cost_estimate=cost(10**9, 2 * 10**6),
        name="upward",
    )(x, basis_t, trans, own_ask, exchange(requests, 0))
    one = exchange(side, 0)
    two = exchange(halo, 1)
    both = pl.pallas_call(
        functools.partial(join_kernel, base),
        out_shape=shape((2 * (packed - base), 128), BF),
        in_specs=[vmem] * 2,
        out_specs=vmem,
        compiler_params=params(8),
        cost_estimate=cost(10**6, 10**6),
        name="join",
    )(own, one)
    far = exchange(both, 1, 3)
    reply = pl.pallas_call(
        functools.partial(reply_kernel, leaf_count, base),
        out_shape=shape((512 + 2 * parent_rows, 128), BF),
        in_specs=[vmem] * 3,
        out_specs=vmem,
        scratch_shapes=[
            VMEM((32, 128), jnp.int32),
            SMEM((32, 128), jnp.int32),
            pltpu.SemaphoreType.DMA,
        ],
        compiler_params=params(8),
        cost_estimate=cost(10**6, 10**6),
        name="reply",
    )(two, own, one)
    three = exchange(reply, 1)

    near = pl.pallas_call(
        near_kernel,
        out_shape=shape((rhs_count, points), F32),
        in_specs=[vmem, vmem, vmem, hbm, hbm],
        out_specs=vmem,
        scratch_shapes=[
            SMEM((near_count, leaf_count), jnp.int32),
            VMEM(near_rows.shape, BF),
            VMEM((leaf_count + 2 * HALO, leaf, 128), BF),
            VMEM((256, 128 * ((near_count + 1) // 2)), BF),
            VMEM((256, 128 * ((near_count + 1) // 2)), BF),
            DMA((leaf_count // 4 + 1,)),
        ],
        compiler_params=params(20),
        cost_estimate=cost(35 * 10**8, 9 * 10**5 * 5),
        name="near",
    )(x, one, two, in_hbm(near_rows), in_hbm(near_source.T))

    three, far, near = lax.optimization_barrier((three, far, near))
    three_over = exchange(three, 0)
    far_over = exchange(far, 0)

    product = pl.pallas_call(
        down_kernel,
        out_shape=shape((rhs_count, points), BF),
        in_specs=[vmem] * 6 + [smem] * 3 + [vmem] * 5,
        out_specs=vmem,
        scratch_shapes=[
            VMEM((leaf_count + 64, rank, 128), BF),
            VMEM((9 * parent_count, rank, 128), BF),
            VMEM((leaf_count // 4, coup_count * rank, 256), BF),
            VMEM((par_source.shape[1] * rank, 128 * ((parent_count + 1) // 2)), BF),
            VMEM((parent_count, rank, 128), BF),
            VMEM((rank * leaf_count, 128), BF),
        ],
        compiler_params=params(12),
        cost_estimate=cost(10**9, 4 * 10**6),
        name="downward",
    )(
        own,
        one,
        three,
        far,
        three_over,
        far_over,
        requests,
        coup_source.T,
        par_source,
        coup_rows,
        par_rows,
        diag,
        tst,
        near,
    )
    return product.T


def solution(mesh):
    split = ("groups", "leaf")
    return jax.shard_map(
        shards,
        mesh=mesh,
        in_specs=(
            P(split, None),
            P(split, None, None),
            P(split, None, None),
            P(split, None, None),
            P(split, None),
            P(split, None, None),
            P(split, None, None),
            P(split, None),
            P(split, None, None),
            P(split, None),
        ),
        out_specs=P(split, None),
        check_vma=False,
    )
```

```python
import functools

import jax
import jax.numpy as jnp
from jax import lax
from jax.experimental import pallas as pl
from jax.experimental.pallas import tpu as pltpu
from jax.sharding import PartitionSpec as P

HALO = 16
BF = jnp.bfloat16
F32 = jnp.float32
VMEM = pltpu.VMEM
SMEM = pltpu.SMEM
DMA = pltpu.SemaphoreType.DMA


def low_half(rows):
    return lax.broadcasted_iota(jnp.int32, (rows, 128), 1) < 64


def swapped(value):
    return pltpu.roll(value, 64, 1)


def matmul(a, b):
    return jnp.dot(a, b, preferred_element_type=F32)


def matmul_nt(a, b):
    return lax.dot_general(a, b, (((1,), (1,)), ((), ())), preferred_element_type=F32)


def matmul_tn(a, b):
    return lax.dot_general(a, b, (((0,), (0,)), ((), ())), preferred_element_type=F32)


def fill_block_diagonal(basis_ref, diag):
    leaf_count, rank, leaf = basis_ref.shape
    blank = jnp.zeros((rank, leaf), BF)
    empty = jnp.zeros((rank, 2 * leaf), BF)
    for i in range(leaf_count):
        at = 128 * (1 - i % 4 // 2)
        diag[rank * i : rank * (i + 1), at : at + 128] = empty
    for first in range(0, leaf_count, 8):
        tiles = []
        for i in range(first, first + 8):
            block = basis_ref[i]
            tiles.append(jnp.concatenate([blank, block] if i % 2 else [block, blank], 1))
        for i, tile in enumerate(tiles, first):
            at = 128 * (i % 4 // 2)
            diag[rank * i : rank * (i + 1), at : at + 128] = tile


def load_kernel(*refs):
    count = len(refs) // 2
    sems = refs[-1]
    copies = [
        pltpu.make_async_copy(refs[n], refs[count + n], sems.at[n]) for n in range(count)
    ]
    for copy in copies:
        copy.start()
    for copy in copies:
        copy.wait()


def up_kernel(
    x_ref, basis_ref, trans_ref, own_ask, other_ask, side, halo_ref, own, tst_ref, diag, flat, ask
):
    points = x_ref.shape[1]
    leaf_count, rank, leaf = basis_ref.shape
    for first in range(0, rank // 4, 4):
        blocks = [
            trans_ref[128 * step : 128 * step + 128, :].astype(F32).T
            for step in range(first, first + 4)
        ]
        for q in range(4):
            pieces = [block if q == 0 else pltpu.roll(block, 128 - 32 * q, 1) for block in blocks]
            for step, piece in enumerate(pieces, first):
                flat[pl.ds(4 * step + q, leaf_count, stride=rank), :] = piece
    tst_ref[...] = flat[:, 0:rank].astype(BF)
    fill_block_diagonal(basis_ref, diag)

    odd = lax.rem(lax.axis_index("leaf"), 2) == 1
    base = HALO * leaf // 128 * 64
    for t in range(HALO * leaf // 128):
        rows = slice(64 * t, 64 * t + 64)
        at = points - HALO * leaf + 128 * t
        head, tail = x_ref[:, 128 * t : 128 * t + 128], x_ref[:, at : at + 128]
        side[rows, :] = jnp.where(odd, head, tail)
        halo_ref[:, 128 * t : 128 * t + 128] = jnp.where(odd, tail, head)
    ask[...] = jnp.zeros(ask.shape, F32)
    ask[0:8, 0:8] = own_ask[...].astype(F32)
    ask[16:24, 0:8] = other_ask[...].astype(F32)
    halo_ref[:, HALO * leaf :] = ask[...].astype(BF)

    def put(at, left, right):
        rows = left.shape[0]
        both = jnp.where(low_half(rows), left, right)
        own[at : at + rows, :] = both
        side[base + at : base + at + rows, :] = both

    parent_count = leaf_count // 8
    skels = []
    for quad in range(leaf_count // 4):
        x = x_ref[:, 256 * quad : 256 * quad + 256]
        skels.append(
            matmul_nt(
                diag[128 * quad : 128 * quad + 128, :], jnp.concatenate([x, x], 0)
            ).astype(BF)
        )
    parents = [
        matmul_tn(
            tst_ref[256 * p : 256 * p + 256, :], jnp.concatenate(skels[2 * p : 2 * p + 2], 0)
        ).astype(BF)
        for p in range(parent_count)
    ]
    for quad, skel in enumerate(skels):
        put(64 * quad, skel[:64], skel[64:])
    for m in range((parent_count + 1) // 2):
        put(16 * leaf_count + 32 * m, parents[2 * m], parents[min(2 * m + 1, parent_count - 1)])


def place(r, leaf_count):
    safe = jnp.minimum(r, leaf_count - 1)
    return pl.multiple_of((safe >> 2) * 64 + (safe & 1) * 32, 32), (safe >> 1) & 1


def pick(ref, base, r, leaf_count, want_high):
    row, high = place(r, leaf_count)
    value = ref[pl.ds(base + row, 32), :]
    value = jnp.where(high != want_high, swapped(value), value)
    return jnp.where(r < leaf_count, value, jnp.zeros_like(value))


def reply_kernel(leaf_count, base, got_ref, own_ref, one_ref, out_ref, ints, nums, sem):
    width = HALO // 2 * 128
    ints[...] = got_ref[0:32, width:].astype(F32).astype(jnp.int32)
    copy = pltpu.make_async_copy(ints, nums, sem)
    copy.start()
    parents = 16 * leaf_count
    size = own_ref.shape[0] - parents
    blocks = ((own_ref, 0), (one_ref, base))
    for n, (ref, at) in enumerate(blocks):
        out_ref[512 + size * n : 512 + size * (n + 1), :] = ref[at + parents : at + parents + size, :]
    odd = lax.rem(lax.axis_index("leaf"), 2) == 1
    low = low_half(32)
    copy.wait()
    for asker in range(2):
        for n, (ref, at) in enumerate(blocks):
            reach = 1 + asker + n
            k = jnp.where(odd, 4 - reach, 3 + reach)
            asked = [nums[16 * asker + k, c] for c in range(8)]
            values = [pick(ref, at, r, leaf_count, c % 2) for c, r in enumerate(asked)]
            for m in range(4):
                row = 256 * asker + 128 * n + 32 * m
                out_ref[row : row + 32, :] = jnp.where(low, values[2 * m], values[2 * m + 1])


def join_kernel(base, own_ref, one_ref, out_ref):
    size = own_ref.shape[0]
    out_ref[:size, :] = own_ref[...]
    out_ref[size:, :] = one_ref[base:, :]


def near_kernel(
    x_ref,
    one_ref,
    two_ref,
    near_ref,
    source_hbm,
    out_ref,
    source_ref,
    held,
    twice,
    sems,
):
    leaf_count, leaf, depth = near_ref.shape
    count = source_hbm.shape[0]
    quads = leaf_count // 4
    copy_source = pltpu.make_async_copy(source_hbm, source_ref, sems.at[quads])
    copy_source.start()

    def copy(quad):
        part = pl.ds(4 * quad, 4)
        return pltpu.make_async_copy(near_ref.at[part], held.at[part], sems.at[quad])

    for quad in range(quads):
        copy(quad).start()

    low = low_half(leaf)

    def spread(parts):
        others = [swapped(value) for value, _ in parts]
        for (value, at), other in zip(parts, others):
            twice[at] = jnp.where(low, value, other)
            twice[at + 1] = jnp.where(low, other, value)

    odd = lax.rem(lax.axis_index("leaf"), 2) == 1
    after = HALO + leaf_count
    at_one, at_two = jnp.where(odd, 0, after), jnp.where(odd, after, 0)
    halos = range(HALO // 2)
    spread([(one_ref[64 * n : 64 * n + 64, :], at_one + 2 * n) for n in halos])
    spread([(two_ref[:, 128 * n : 128 * n + 128], at_two + 2 * n) for n in halos])
    for first in range(0, leaf_count // 2, 5):
        spread(
            [(x_ref[:, 128 * n : 128 * n + 128], HALO + 2 * n) for n in range(first, first + 5)]
        )
    copy_source.wait()

    def product(i):
        pieces = [
            jnp.where(low, twice[source_ref[2 * m, i]], twice[source_ref[2 * m + 1, i]])
            for m in range(count // 2)
        ]
        if count % 2:
            pieces.append(twice[source_ref[count - 1, i]][:, :leaf])
        return matmul_nt(jnp.concatenate(pieces, 1), held[i])

    def body(quad, carry):
        copy(quad).wait()
        parts = [product(4 * quad + u) for u in range(4)]
        for t in range(2):
            lanes = pl.ds(pl.multiple_of(256 * quad + 128 * t, 128), 128)
            out_ref[:, lanes] = jnp.concatenate(parts[2 * t : 2 * t + 2], 1)
        return carry

    lax.fori_loop(0, quads, body, 0)


def split(value):
    low = low_half(value.shape[0])
    other = swapped(value)
    return jnp.where(low, value, other), jnp.where(low, other, value)


class Tables:
    def __init__(self, leaf_count, slots, window, requests):
        self.leaf_count, self.slots, self.window, self.requests = leaf_count, slots, window, requests
        self.parent_count = leaf_count // 8

    def spot(self, reach, up):
        k = jnp.where(up, 3 + reach, 4 - reach)
        return k, jnp.where(up, 4 + reach, 4 - reach)

    def put_parents(self, ref, at, block):
        tiles = range((self.parent_count + 1) // 2)
        values = [ref[at + 32 * m : at + 32 * m + 32, :] for m in tiles]
        for m, (left, right) in zip(tiles, [split(value) for value in values]):
            self.window[self.parent_count * block + 2 * m] = left
            if 2 * m + 1 < self.parent_count:
                self.window[self.parent_count * block + 2 * m + 1] = right

    def put_own(self, ref):
        for first in range(0, self.leaf_count // 4, 5):
            quads = range(first, first + 5)
            values = [ref[64 * quad : 64 * quad + 64, :] for quad in quads]
            for quad, (left, right) in zip(quads, [split(value) for value in values]):
                self.slots[4 * quad] = left[:32]
                self.slots[4 * quad + 1] = left[32:]
                self.slots[4 * quad + 2] = right[:32]
                self.slots[4 * quad + 3] = right[32:]
        self.put_parents(ref, 16 * self.leaf_count, 4)

    def look_up(self, ref, at, reach, up):
        k, block = self.spot(reach, up)
        low = low_half(32)
        asked = [self.requests[k, c] for c in range(8)]
        places = [place(r, self.leaf_count) for r in asked]
        values = [ref[pl.ds(at + row, 32), :] for row, _ in places]
        others = [swapped(value) for value in values]
        for c, r in enumerate(asked):
            value = jnp.where(low == (places[c][1] == 0), values[c], others[c])
            self.slots[self.leaf_count + 8 * k + c] = jnp.where(
                r < self.leaf_count, value, jnp.zeros_like(value)
            )
        self.put_parents(ref, at + 16 * self.leaf_count, block)

    def put_reply(self, ref, at, parents_at, reach, up):
        k, block = self.spot(reach, up)
        values = [ref[at + 32 * m : at + 32 * m + 32, :] for m in range(4)]
        for m, (left, right) in enumerate([split(value) for value in values]):
            self.slots[self.leaf_count + 8 * k + 2 * m] = left
            self.slots[self.leaf_count + 8 * k + 2 * m + 1] = right
        self.put_parents(ref, parents_at, block)


def is_odd():
    return lax.rem(lax.axis_index("leaf"), 2) == 1


def first_kernel(leaf_count, base, own_ref, one_ref, requests, slots, window):
    tables = Tables(leaf_count, slots, window, requests)
    tables.put_own(own_ref)
    tables.look_up(one_ref, base, 1, jnp.logical_not(is_odd()))


def second_kernel(
    leaf_count, three_ref, far_ref, requests, slots_in, window_in, slots, window
):
    tables = Tables(leaf_count, slots, window, requests)
    odd = is_odd()
    size = far_ref.shape[0] // 2
    parent_size = size - 16 * leaf_count
    tables.look_up(far_ref, 0, 3, odd)
    tables.look_up(far_ref, size, 4, odd)
    tables.put_reply(three_ref, 0, 512, 1, odd)
    tables.put_reply(three_ref, 128, 512 + parent_size, 2, odd)


def down_kernel(
    three_over,
    far_over,
    requests,
    coup_source,
    par_source,
    coup_ref,
    par_ref,
    diag,
    tst_ref,
    near_ref,
    slots_in,
    window_in,
    out_ref,
    slots,
    window,
    weights,
    stack,
    outs,
    leaf_outs,
):
    leaf_count, rank = coup_ref.shape[:2]
    parent_count = par_ref.shape[0]
    low64 = low_half(64)
    low = low_half(rank)
    tables = Tables(leaf_count, slots, window, requests)
    inward = jnp.logical_not(is_odd())
    parent_size = far_over.shape[0] // 2 - 16 * leaf_count
    tables.look_up(far_over, 0, 4, inward)
    tables.put_reply(three_over, 256, 512, 2, inward)
    tables.put_reply(three_over, 384, 512 + parent_size, 3, inward)

    per = par_source.shape[1]
    coup = coup_source.shape[0]
    pairs = [(2 * m, min(2 * m + 1, parent_count - 1)) for m in range((parent_count + 1) // 2)]
    for first in range(0, per, 4):
        loaded = [
            [(window[par_source[p, j]], window[par_source[q, j]]) for p, q in pairs]
            for j in range(first, first + 4)
        ]
        for j, tiles in enumerate(loaded, first):
            for m, (left, right) in enumerate(tiles):
                stack[rank * j : rank * j + rank, 128 * m : 128 * m + 128] = jnp.where(
                    low, left, right
                )
    rows = par_ref[...].reshape(parent_count * rank, per * rank)
    parent_outs = matmul(rows, stack[...]).astype(BF)
    for p in range(parent_count):
        tile = parent_outs[rank * p : rank * p + rank, 128 * (p // 2) : 128 * (p // 2) + 128]
        outs[p] = split(tile)[p % 2]

    def build(quad, carry):
        for first in range(0, coup, 4):
            loaded = [
                [
                    (slots[coup_source[j, 4 * quad + t]], slots[coup_source[j, 4 * quad + t + 1]])
                    for t in (0, 2)
                ]
                for j in range(first, first + 4)
            ]
            for j, tiles in enumerate(loaded, first):
                for t, (left, right) in enumerate(tiles):
                    weights[quad, rank * j : rank * j + rank, 128 * t : 128 * t + 128] = jnp.where(
                        low, left, right
                    )
        return carry

    quads = leaf_count // 4
    lax.fori_loop(0, quads, build, 0)
    downs = [
        matmul(tst_ref[256 * p : 256 * p + 256, :], outs[p]) for p in range(parent_count)
    ]
    for first in range(0, quads, 2):
        outs_of = []
        for quad in range(first, first + 2):
            rows = coup_ref[4 * quad : 4 * quad + 4].reshape(4 * rank, coup * rank)
            coupled = matmul(rows, weights[quad])
            coupled = jnp.concatenate([coupled[:64, :128], coupled[64:, 128:]], 0)
            down = downs[quad // 2][128 * (quad % 2) : 128 * (quad % 2) + 128]
            outs_of.append((coupled + down).astype(BF))
        for quad, leaf_out in enumerate(outs_of, first):
            leaf_outs[128 * quad : 128 * quad + 128, :] = leaf_out
    for first in range(0, quads, 2):
        tiles = []
        for quad in range(first, first + 2):
            rows = slice(128 * quad, 128 * quad + 128)
            far = matmul_tn(leaf_outs[rows, :], diag[rows, :])
            for t in range(2):
                lanes = slice(256 * quad + 128 * t, 256 * quad + 128 * t + 128)
                tile = jnp.where(
                    low64, far[:64, 128 * t : 128 * t + 128], far[64:, 128 * t : 128 * t + 128]
                )
                tiles.append((lanes, (near_ref[:, lanes] + tile).astype(BF)))
        for lanes, tile in tiles:
            out_ref[:, lanes] = tile


def in_hbm(array):
    return pltpu.with_memory_space_constraint(array, pltpu.HBM)


def params(mib):
    return pltpu.CompilerParams(vmem_limit_bytes=mib << 20)


def cost(flops, size):
    return pl.CostEstimate(flops=flops, bytes_accessed=size, transcendentals=0)


def shards(
    rhs,
    basis,
    transfer,
    near_rows,
    near_source,
    far_request,
    coup_rows,
    coup_source,
    par_rows,
    par_source,
):
    leaf_count, leaf, rank = basis.shape
    points, rhs_count = rhs.shape
    parent_count = par_rows.shape[0]
    near_count = near_source.shape[1]
    coup_count = coup_source.shape[1]
    base = HALO // 2 * rhs_count
    parent_rows = rank * ((parent_count + 1) // 2)
    packed = base + 16 * leaf_count + parent_rows
    count = lax.axis_size("leaf")

    x = rhs.T
    trans = transfer.transpose(1, 2, 0).reshape(rank * rank, leaf_count)
    shape = jax.ShapeDtypeStruct
    vmem, smem, hbm = (pl.BlockSpec(memory_space=kind) for kind in (VMEM, SMEM, pltpu.HBM))
    basis_t = basis.transpose(0, 2, 1)
    requests = far_request[0]
    inputs = (x, basis_t, trans, requests)
    x, basis_t, trans, own_ask = pl.pallas_call(
        load_kernel,
        out_shape=tuple(shape(held.shape, held.dtype) for held in inputs),
        in_specs=[hbm] * 4,
        out_specs=(vmem,) * 4,
        scratch_shapes=[DMA((4,))],
        compiler_params=params(8),
        cost_estimate=cost(10**6, 2 * 10**6),
        name="load",
    )(*(in_hbm(held) for held in inputs))

    def exchange(block, begin, distance=1):
        pairs = [(i, i + distance) for i in range(begin, count - distance, 2)]
        return lax.ppermute(block, "leaf", pairs + [(b, a) for a, b in pairs])

    side, halo, own, tst, diag = pl.pallas_call(
        up_kernel,
        out_shape=(
            shape((packed, 128), BF),
            shape((rhs_count, HALO * leaf + 128), BF),
            shape((packed - base, 128), BF),
            shape((rank * leaf_count, rank), BF),
            shape((rank * leaf_count, 256), BF),
        ),
        in_specs=[vmem] * 5,
        out_specs=(vmem,) * 5,
        scratch_shapes=[VMEM((rank * leaf_count, 128), F32), VMEM((rhs_count, 128), F32)],
        compiler_params=params(8),
        cost_estimate=cost(10**9, 2 * 10**6),
        name="upward",
    )(x, basis_t, trans, own_ask, exchange(requests, 0))
    one = exchange(side, 0)
    two = exchange(halo, 1)
    both = pl.pallas_call(
        functools.partial(join_kernel, base),
        out_shape=shape((2 * (packed - base), 128), BF),
        in_specs=[vmem] * 2,
        out_specs=vmem,
        compiler_params=params(8),
        cost_estimate=cost(10**6, 10**6),
        name="join",
    )(own, one)
    far = exchange(both, 1, 3)
    table_shapes = (
        shape((leaf_count + 64, rank, 128), BF),
        shape((9 * parent_count, rank, 128), BF),
    )
    tables = pl.pallas_call(
        functools.partial(first_kernel, leaf_count, base),
        out_shape=table_shapes,
        in_specs=[vmem, vmem, smem],
        out_specs=(vmem,) * 2,
        compiler_params=params(8),
        cost_estimate=cost(10**6, 10**6),
        name="first_tables",
    )(own, one, own_ask)
    two, tables = lax.optimization_barrier((two, tables))
    reply = pl.pallas_call(
        functools.partial(reply_kernel, leaf_count, base),
        out_shape=shape((512 + 2 * parent_rows, 128), BF),
        in_specs=[vmem] * 3,
        out_specs=vmem,
        scratch_shapes=[
            VMEM((32, 128), jnp.int32),
            SMEM((32, 128), jnp.int32),
            pltpu.SemaphoreType.DMA,
        ],
        compiler_params=params(8),
        cost_estimate=cost(10**6, 10**6),
        name="reply",
    )(two, own, one)
    three = exchange(reply, 1)

    near = pl.pallas_call(
        near_kernel,
        out_shape=shape((rhs_count, points), F32),
        in_specs=[vmem, vmem, vmem, hbm, hbm],
        out_specs=vmem,
        scratch_shapes=[
            SMEM((near_count, leaf_count), jnp.int32),
            VMEM(near_rows.shape, BF),
            VMEM((leaf_count + 2 * HALO, leaf, 128), BF),
            DMA((leaf_count // 4 + 1,)),
        ],
        compiler_params=params(20),
        cost_estimate=cost(35 * 10**8, 9 * 10**5 * 5),
        name="near",
    )(x, one, two, in_hbm(near_rows), in_hbm(near_source.T))

    three, far, near = lax.optimization_barrier((three, far, near))
    three_over = exchange(three, 0)
    far_over = exchange(far, 0)

    tables = pl.pallas_call(
        functools.partial(second_kernel, leaf_count),
        out_shape=table_shapes,
        in_specs=[vmem, vmem, smem, vmem, vmem],
        out_specs=(vmem,) * 2,
        input_output_aliases={3: 0, 4: 1},
        compiler_params=params(8),
        cost_estimate=cost(10**6, 10**6),
        name="second_tables",
    )(three, far, own_ask, *tables)

    product, _, _ = pl.pallas_call(
        down_kernel,
        out_shape=(shape((rhs_count, points), BF),) + table_shapes,
        in_specs=[vmem] * 2 + [smem] * 3 + [vmem] * 7,
        out_specs=(vmem,) * 3,
        input_output_aliases={10: 1, 11: 2},
        scratch_shapes=[
            VMEM((leaf_count // 4, coup_count * rank, 256), BF),
            VMEM((par_source.shape[1] * rank, 128 * ((parent_count + 1) // 2)), BF),
            VMEM((parent_count, rank, 128), BF),
            VMEM((rank * leaf_count, 128), BF),
        ],
        compiler_params=params(12),
        cost_estimate=cost(10**9, 4 * 10**6),
        name="downward",
    )(
        three_over,
        far_over,
        own_ask,
        coup_source.T,
        par_source,
        coup_rows,
        par_rows,
        diag,
        tst,
        near,
        *tables,
    )
    return product.T


def solution(mesh):
    split = ("groups", "leaf")
    return jax.shard_map(
        shards,
        mesh=mesh,
        in_specs=(
            P(split, None),
            P(split, None, None),
            P(split, None, None),
            P(split, None, None),
            P(split, None),
            P(split, None, None),
            P(split, None, None),
            P(split, None),
            P(split, None, None),
            P(split, None),
        ),
        out_specs=P(split, None),
        check_vma=False,
    )
```

```python
import functools

import jax
import jax.numpy as jnp
from jax import lax
from jax.experimental import pallas as pl
from jax.experimental.pallas import tpu as pltpu
from jax.sharding import PartitionSpec as P

HALO = 16
BF = jnp.bfloat16
F32 = jnp.float32
VMEM = pltpu.VMEM
SMEM = pltpu.SMEM
DMA = pltpu.SemaphoreType.DMA


def low_half(rows):
    return lax.broadcasted_iota(jnp.int32, (rows, 128), 1) < 64


def swapped(value):
    return pltpu.roll(value, 64, 1)


def matmul(a, b):
    return jnp.dot(a, b, preferred_element_type=F32)


def matmul_nt(a, b):
    return lax.dot_general(a, b, (((1,), (1,)), ((), ())), preferred_element_type=F32)


def matmul_tn(a, b):
    return lax.dot_general(a, b, (((0,), (0,)), ((), ())), preferred_element_type=F32)


def fill_block_diagonal(basis_ref, diag):
    leaf_count, rank, leaf = basis_ref.shape
    blank = jnp.zeros((rank, leaf), BF)
    empty = jnp.zeros((rank, 2 * leaf), BF)
    for i in range(leaf_count):
        at = 128 * (1 - i % 4 // 2)
        diag[rank * i : rank * (i + 1), at : at + 128] = empty
    for first in range(0, leaf_count, 8):
        tiles = []
        for i in range(first, first + 8):
            block = basis_ref[i]
            tiles.append(jnp.concatenate([blank, block] if i % 2 else [block, blank], 1))
        for i, tile in enumerate(tiles, first):
            at = 128 * (i % 4 // 2)
            diag[rank * i : rank * (i + 1), at : at + 128] = tile


def load_kernel(*refs):
    count = len(refs) // 2
    sems = refs[-1]
    copies = [
        pltpu.make_async_copy(refs[n], refs[count + n], sems.at[n]) for n in range(count)
    ]
    for copy in copies:
        copy.start()
    for copy in copies:
        copy.wait()


def up_kernel(
    x_ref, basis_ref, trans_ref, side, halo_ref, own, tst_ref, diag, flat
):
    points = x_ref.shape[1]
    leaf_count, rank, leaf = basis_ref.shape
    for first in range(0, rank // 4, 4):
        blocks = [
            trans_ref[128 * step : 128 * step + 128, :].astype(F32).T
            for step in range(first, first + 4)
        ]
        for q in range(4):
            pieces = [block if q == 0 else pltpu.roll(block, 128 - 32 * q, 1) for block in blocks]
            for step, piece in enumerate(pieces, first):
                flat[pl.ds(4 * step + q, leaf_count, stride=rank), :] = piece
    tst_ref[...] = flat[:, 0:rank].astype(BF)
    fill_block_diagonal(basis_ref, diag)

    odd = lax.rem(lax.axis_index("leaf"), 2) == 1
    base = HALO * leaf // 128 * 64
    for t in range(HALO * leaf // 128):
        rows = slice(64 * t, 64 * t + 64)
        at = points - HALO * leaf + 128 * t
        head, tail = x_ref[:, 128 * t : 128 * t + 128], x_ref[:, at : at + 128]
        side[rows, :] = jnp.where(odd, head, tail)
        halo_ref[:, 128 * t : 128 * t + 128] = jnp.where(odd, tail, head)

    def put(at, left, right):
        rows = left.shape[0]
        both = jnp.where(low_half(rows), left, right)
        own[at : at + rows, :] = both
        side[base + at : base + at + rows, :] = both

    parent_count = leaf_count // 8
    skels = []
    for quad in range(leaf_count // 4):
        x = x_ref[:, 256 * quad : 256 * quad + 256]
        skels.append(
            matmul_nt(
                diag[128 * quad : 128 * quad + 128, :], jnp.concatenate([x, x], 0)
            ).astype(BF)
        )
    parents = [
        matmul_tn(
            tst_ref[256 * p : 256 * p + 256, :], jnp.concatenate(skels[2 * p : 2 * p + 2], 0)
        ).astype(BF)
        for p in range(parent_count)
    ]
    for quad, skel in enumerate(skels):
        put(64 * quad, skel[:64], skel[64:])
    for m in range((parent_count + 1) // 2):
        put(16 * leaf_count + 32 * m, parents[2 * m], parents[min(2 * m + 1, parent_count - 1)])


def place(r, leaf_count):
    safe = jnp.minimum(r, leaf_count - 1)
    return pl.multiple_of((safe >> 2) * 64 + (safe & 1) * 32, 32), (safe >> 1) & 1


def join_kernel(base, own_ref, one_ref, out_ref):
    size = own_ref.shape[0]
    out_ref[:size, :] = own_ref[...]
    out_ref[size:, :] = one_ref[base:, :]


def near_kernel(
    x_ref,
    one_ref,
    two_ref,
    near_ref,
    source_hbm,
    out_ref,
    source_ref,
    held,
    twice,
    sems,
):
    leaf_count, leaf, depth = near_ref.shape
    count = source_hbm.shape[0]
    quads = leaf_count // 4
    copy_source = pltpu.make_async_copy(source_hbm, source_ref, sems.at[quads])
    copy_source.start()

    def copy(quad):
        part = pl.ds(4 * quad, 4)
        return pltpu.make_async_copy(near_ref.at[part], held.at[part], sems.at[quad])

    for quad in range(quads):
        copy(quad).start()

    low = low_half(leaf)

    def spread(parts):
        others = [swapped(value) for value, _ in parts]
        for (value, at), other in zip(parts, others):
            twice[at] = jnp.where(low, value, other)
            twice[at + 1] = jnp.where(low, other, value)

    odd = lax.rem(lax.axis_index("leaf"), 2) == 1
    after = HALO + leaf_count
    at_one, at_two = jnp.where(odd, 0, after), jnp.where(odd, after, 0)
    halos = range(HALO // 2)
    spread([(one_ref[64 * n : 64 * n + 64, :], at_one + 2 * n) for n in halos])
    spread([(two_ref[:, 128 * n : 128 * n + 128], at_two + 2 * n) for n in halos])
    for first in range(0, leaf_count // 2, 5):
        spread(
            [(x_ref[:, 128 * n : 128 * n + 128], HALO + 2 * n) for n in range(first, first + 5)]
        )
    copy_source.wait()

    def product(i):
        pieces = [
            jnp.where(low, twice[source_ref[2 * m, i]], twice[source_ref[2 * m + 1, i]])
            for m in range(count // 2)
        ]
        if count % 2:
            pieces.append(twice[source_ref[count - 1, i]][:, :leaf])
        return matmul_nt(jnp.concatenate(pieces, 1), held[i])

    def body(step, carry):
        copy(2 * step).wait()
        copy(2 * step + 1).wait()
        parts = [product(8 * step + u) for u in range(8)]
        for t in range(4):
            lanes = pl.ds(pl.multiple_of(512 * step + 128 * t, 128), 128)
            out_ref[:, lanes] = jnp.concatenate(parts[2 * t : 2 * t + 2], 1)
        return carry

    lax.fori_loop(0, quads // 2, body, 0)


def split(value):
    low = low_half(value.shape[0])
    other = swapped(value)
    return jnp.where(low, value, other), jnp.where(low, other, value)


class Tables:
    def __init__(self, leaf_count, slots, window, requests):
        self.leaf_count, self.slots, self.window, self.requests = leaf_count, slots, window, requests
        self.parent_count = leaf_count // 8

    def spot(self, reach, up):
        k = jnp.where(up, 3 + reach, 4 - reach)
        return k, jnp.where(up, 4 + reach, 4 - reach)

    def put_parents(self, ref, at, block):
        tiles = range((self.parent_count + 1) // 2)
        values = [ref[at + 32 * m : at + 32 * m + 32, :] for m in tiles]
        for m, (left, right) in zip(tiles, [split(value) for value in values]):
            self.window[self.parent_count * block + 2 * m] = left
            if 2 * m + 1 < self.parent_count:
                self.window[self.parent_count * block + 2 * m + 1] = right

    def put_own(self, ref):
        for first in range(0, self.leaf_count // 4, 5):
            quads = range(first, first + 5)
            values = [ref[64 * quad : 64 * quad + 64, :] for quad in quads]
            for quad, (left, right) in zip(quads, [split(value) for value in values]):
                self.slots[4 * quad] = left[:32]
                self.slots[4 * quad + 1] = left[32:]
                self.slots[4 * quad + 2] = right[:32]
                self.slots[4 * quad + 3] = right[32:]
        self.put_parents(ref, 16 * self.leaf_count, 4)

    def look_up(self, ref, at, reach, up):
        k, block = self.spot(reach, up)
        low = low_half(32)
        asked = [self.requests[k, c] for c in range(8)]
        places = [place(r, self.leaf_count) for r in asked]
        values = [ref[pl.ds(at + row, 32), :] for row, _ in places]
        others = [swapped(value) for value in values]
        for c, r in enumerate(asked):
            value = jnp.where(low == (places[c][1] == 0), values[c], others[c])
            self.slots[self.leaf_count + 8 * k + c] = jnp.where(
                r < self.leaf_count, value, jnp.zeros_like(value)
            )
        self.put_parents(ref, at + 16 * self.leaf_count, block)


def is_odd():
    return lax.rem(lax.axis_index("leaf"), 2) == 1


def first_kernel(leaf_count, base, own_ref, one_ref, ask_ref, slots, window, requests, sem):
    copy = pltpu.make_async_copy(ask_ref, requests, sem)
    copy.start()
    tables = Tables(leaf_count, slots, window, requests)
    tables.put_own(own_ref)
    copy.wait()
    tables.look_up(one_ref, base, 1, jnp.logical_not(is_odd()))


def second_kernel(
    leaf_count, three_ref, far_ref, ask_ref, slots_in, window_in, slots, window, requests, sem
):
    copy = pltpu.make_async_copy(ask_ref, requests, sem)
    copy.start()
    copy.wait()
    tables = Tables(leaf_count, slots, window, requests)
    odd = is_odd()
    size = far_ref.shape[0] // 2
    tables.look_up(three_ref, size, 2, jnp.logical_not(odd))
    tables.look_up(three_ref, 0, 3, jnp.logical_not(odd))
    tables.look_up(far_ref, 0, 3, odd)
    tables.look_up(far_ref, size, 4, odd)


def down_kernel(
    three_over,
    far_over,
    ask_ref,
    coup_hbm,
    par_hbm,
    coup_ref,
    par_ref,
    diag,
    tst_ref,
    near_ref,
    slots_in,
    window_in,
    out_hbm,
    slots,
    window,
    requests,
    coup_source,
    par_source,
    weights,
    stack,
    outs,
    leaf_outs,
    out_ref,
    sems,
    out_sems,
):
    copies = [
        pltpu.make_async_copy(source, held, sems.at[n])
        for n, (source, held) in enumerate(
            ((ask_ref, requests), (par_hbm, par_source), (coup_hbm, coup_source))
        )
    ]
    for copy in copies:
        copy.start()
    leaf_count, rank = coup_ref.shape[:2]
    parent_count = par_ref.shape[0]
    low64 = low_half(64)
    low = low_half(rank)
    tables = Tables(leaf_count, slots, window, requests)
    odd = is_odd()
    size = far_over.shape[0] // 2
    copies[0].wait()
    tables.look_up(three_over, size, 1, odd)
    tables.look_up(three_over, 0, 2, odd)
    tables.look_up(far_over, 0, 4, jnp.logical_not(odd))
    copies[1].wait()
    copies[2].wait()
    per = par_source.shape[1]
    coup = coup_source.shape[0]
    pairs = [(2 * m, min(2 * m + 1, parent_count - 1)) for m in range((parent_count + 1) // 2)]
    for first in range(0, per, 4):
        loaded = [
            [(window[par_source[p, j]], window[par_source[q, j]]) for p, q in pairs]
            for j in range(first, first + 4)
        ]
        for j, tiles in enumerate(loaded, first):
            for m, (left, right) in enumerate(tiles):
                stack[rank * j : rank * j + rank, 128 * m : 128 * m + 128] = jnp.where(
                    low, left, right
                )
    rows = par_ref[...].reshape(parent_count * rank, per * rank)
    parent_outs = matmul(rows, stack[...]).astype(BF)
    for p in range(parent_count):
        tile = parent_outs[rank * p : rank * p + rank, 128 * (p // 2) : 128 * (p // 2) + 128]
        outs[p] = split(tile)[p % 2]

    def build(quad, carry):
        for first in range(0, coup, 4):
            loaded = [
                [
                    (slots[coup_source[j, 4 * quad + t]], slots[coup_source[j, 4 * quad + t + 1]])
                    for t in (0, 2)
                ]
                for j in range(first, first + 4)
            ]
            for j, tiles in enumerate(loaded, first):
                for t, (left, right) in enumerate(tiles):
                    weights[quad, rank * j : rank * j + rank, 128 * t : 128 * t + 128] = jnp.where(
                        low, left, right
                    )
        return carry

    quads = leaf_count // 4
    lax.fori_loop(0, quads, build, 0)
    downs = [
        matmul(tst_ref[256 * p : 256 * p + 256, :], outs[p]) for p in range(parent_count)
    ]
    for first in range(0, quads, 2):
        outs_of = []
        for quad in range(first, first + 2):
            rows = coup_ref[4 * quad : 4 * quad + 4].reshape(4 * rank, coup * rank)
            coupled = matmul(rows, weights[quad])
            coupled = jnp.concatenate([coupled[:64, :128], coupled[64:, 128:]], 0)
            down = downs[quad // 2][128 * (quad % 2) : 128 * (quad % 2) + 128]
            outs_of.append((coupled + down).astype(BF))
        for quad, leaf_out in enumerate(outs_of, first):
            leaf_outs[128 * quad : 128 * quad + 128, :] = leaf_out
    def send(p):
        part = pl.ds(512 * p, 512)
        return pltpu.make_async_copy(out_ref.at[:, part], out_hbm.at[:, part], out_sems.at[p])

    for first in range(0, quads, 2):
        tiles = []
        for quad in range(first, first + 2):
            rows = slice(128 * quad, 128 * quad + 128)
            far = matmul_tn(leaf_outs[rows, :], diag[rows, :])
            for t in range(2):
                lanes = slice(256 * quad + 128 * t, 256 * quad + 128 * t + 128)
                tile = jnp.where(
                    low64, far[:64, 128 * t : 128 * t + 128], far[64:, 128 * t : 128 * t + 128]
                )
                tiles.append((lanes, (near_ref[:, lanes] + tile).astype(BF)))
        for lanes, tile in tiles:
            out_ref[:, lanes] = tile
        send(first // 2).start()
    for p in range(parent_count):
        send(p).wait()


def in_hbm(array):
    return pltpu.with_memory_space_constraint(array, pltpu.HBM)


def params(mib):
    return pltpu.CompilerParams(vmem_limit_bytes=mib << 20)


def cost(flops, size):
    return pl.CostEstimate(flops=flops, bytes_accessed=size, transcendentals=0)


def shards(
    rhs,
    basis,
    transfer,
    near_rows,
    near_source,
    far_request,
    coup_rows,
    coup_source,
    par_rows,
    par_source,
):
    leaf_count, leaf, rank = basis.shape
    points, rhs_count = rhs.shape
    parent_count = par_rows.shape[0]
    near_count = near_source.shape[1]
    coup_count = coup_source.shape[1]
    base = HALO // 2 * rhs_count
    parent_rows = rank * ((parent_count + 1) // 2)
    packed = base + 16 * leaf_count + parent_rows
    count = lax.axis_size("leaf")

    x = rhs.T
    trans = transfer.transpose(1, 2, 0).reshape(rank * rank, leaf_count)
    shape = jax.ShapeDtypeStruct
    vmem, hbm = (pl.BlockSpec(memory_space=kind) for kind in (VMEM, pltpu.HBM))
    basis_t = basis.transpose(0, 2, 1)
    inputs = (x, basis_t, trans, far_request[0])
    x, basis_t, trans, ask = pl.pallas_call(
        load_kernel,
        out_shape=tuple(shape(held.shape, held.dtype) for held in inputs),
        in_specs=[hbm] * 4,
        out_specs=(vmem,) * 4,
        scratch_shapes=[DMA((4,))],
        compiler_params=params(8),
        cost_estimate=cost(10**6, 2 * 10**6),
        name="load",
    )(*(in_hbm(held) for held in inputs))

    def exchange(block, begin, distance=1):
        pairs = [(i, i + distance) for i in range(begin, count - distance, 2)]
        return lax.ppermute(block, "leaf", pairs + [(b, a) for a, b in pairs])

    side, halo, own, tst, diag = pl.pallas_call(
        up_kernel,
        out_shape=(
            shape((packed, 128), BF),
            shape((rhs_count, HALO * leaf), BF),
            shape((packed - base, 128), BF),
            shape((rank * leaf_count, rank), BF),
            shape((rank * leaf_count, 256), BF),
        ),
        in_specs=[vmem] * 3,
        out_specs=(vmem,) * 5,
        scratch_shapes=[VMEM((rank * leaf_count, 128), F32)],
        compiler_params=params(8),
        cost_estimate=cost(10**9, 2 * 10**6),
        name="upward",
    )(x, basis_t, trans)
    one = exchange(side, 0)
    two = exchange(halo, 1)
    both = pl.pallas_call(
        functools.partial(join_kernel, base),
        out_shape=shape((2 * (packed - base), 128), BF),
        in_specs=[vmem] * 2,
        out_specs=vmem,
        compiler_params=params(8),
        cost_estimate=cost(10**6, 10**6),
        name="join",
    )(own, one)
    far = exchange(both, 1, 3)
    three = exchange(both, 0, 3)
    table_shapes = (
        shape((leaf_count + 64, rank, 128), BF),
        shape((9 * parent_count, rank, 128), BF),
    )
    tables = pl.pallas_call(
        functools.partial(first_kernel, leaf_count, base),
        out_shape=table_shapes,
        in_specs=[vmem] * 3,
        out_specs=(vmem,) * 2,
        scratch_shapes=[SMEM(ask.shape, jnp.int32), pltpu.SemaphoreType.DMA],
        compiler_params=params(8),
        cost_estimate=cost(10**6, 10**6),
        name="first_tables",
    )(own, one, ask)
    near = pl.pallas_call(
        near_kernel,
        out_shape=shape((rhs_count, points), F32),
        in_specs=[vmem, vmem, vmem, hbm, hbm],
        out_specs=vmem,
        scratch_shapes=[
            SMEM((near_count, leaf_count), jnp.int32),
            VMEM(near_rows.shape, BF),
            VMEM((leaf_count + 2 * HALO, leaf, 128), BF),
            DMA((leaf_count // 4 + 1,)),
        ],
        compiler_params=params(20),
        cost_estimate=cost(35 * 10**8, 9 * 10**5 * 5),
        name="near",
    )(x, one, two, in_hbm(near_rows), in_hbm(near_source.T))

    three, far, near = lax.optimization_barrier((three, far, near))
    three_over = exchange(three, 0)
    far_over = exchange(far, 0)

    tables = pl.pallas_call(
        functools.partial(second_kernel, leaf_count),
        out_shape=table_shapes,
        in_specs=[vmem] * 5,
        out_specs=(vmem,) * 2,
        scratch_shapes=[SMEM(ask.shape, jnp.int32), pltpu.SemaphoreType.DMA],
        input_output_aliases={3: 0, 4: 1},
        compiler_params=params(8),
        cost_estimate=cost(10**6, 10**6),
        name="second_tables",
    )(three, far, ask, *tables)

    product, _, _ = pl.pallas_call(
        down_kernel,
        out_shape=(shape((rhs_count, points), BF),) + table_shapes,
        in_specs=[vmem] * 3 + [hbm] * 2 + [vmem] * 7,
        out_specs=(hbm, vmem, vmem),
        input_output_aliases={10: 1, 11: 2},
        scratch_shapes=[
            SMEM(ask.shape, jnp.int32),
            SMEM((coup_count, leaf_count), jnp.int32),
            SMEM(par_source.shape, jnp.int32),
            VMEM((leaf_count // 4, coup_count * rank, 256), BF),
            VMEM((par_source.shape[1] * rank, 128 * ((parent_count + 1) // 2)), BF),
            VMEM((parent_count, rank, 128), BF),
            VMEM((rank * leaf_count, 128), BF),
            VMEM((rhs_count, points), BF),
            DMA((3,)),
            DMA((parent_count,)),
        ],
        compiler_params=params(12),
        cost_estimate=cost(10**9, 4 * 10**6),
        name="downward",
    )(
        three_over,
        far_over,
        ask,
        in_hbm(coup_source.T),
        in_hbm(par_source),
        coup_rows,
        par_rows,
        diag,
        tst,
        near,
        *tables,
    )
    return product.T


def solution(mesh):
    split = ("groups", "leaf")
    return jax.shard_map(
        shards,
        mesh=mesh,
        in_specs=(
            P(split, None),
            P(split, None, None),
            P(split, None, None),
            P(split, None, None),
            P(split, None),
            P(split, None, None),
            P(split, None, None),
            P(split, None),
            P(split, None, None),
            P(split, None),
        ),
        out_specs=P(split, None),
        check_vma=False,
    )
```

```python
import functools

import jax
import jax.numpy as jnp
from jax import lax
from jax.experimental import pallas as pl
from jax.experimental.pallas import tpu as pltpu
from jax.sharding import PartitionSpec as P

HALO = 16
BF = jnp.bfloat16
F32 = jnp.float32
VMEM = pltpu.VMEM
SMEM = pltpu.SMEM
DMA = pltpu.SemaphoreType.DMA


def low_half(rows):
    return lax.broadcasted_iota(jnp.int32, (rows, 128), 1) < 64


def swapped(value):
    return pltpu.roll(value, 64, 1)


def matmul(a, b):
    return jnp.dot(a, b, preferred_element_type=F32)


def matmul_nt(a, b):
    return lax.dot_general(a, b, (((1,), (1,)), ((), ())), preferred_element_type=F32)


def matmul_tn(a, b):
    return lax.dot_general(a, b, (((0,), (0,)), ((), ())), preferred_element_type=F32)


def fill_block_diagonal(basis_ref, diag):
    leaf_count, rank, leaf = basis_ref.shape
    blank = jnp.zeros((rank, leaf), BF)
    empty = jnp.zeros((rank, 2 * leaf), BF)
    for i in range(leaf_count):
        at = 128 * (1 - i % 4 // 2)
        diag[rank * i : rank * (i + 1), at : at + 128] = empty
    for first in range(0, leaf_count, 8):
        tiles = []
        for i in range(first, first + 8):
            block = basis_ref[i]
            tiles.append(jnp.concatenate([blank, block] if i % 2 else [block, blank], 1))
        for i, tile in enumerate(tiles, first):
            at = 128 * (i % 4 // 2)
            diag[rank * i : rank * (i + 1), at : at + 128] = tile


def load_kernel(*refs):
    count = len(refs) // 2
    sems = refs[-1]
    copies = [
        pltpu.make_async_copy(refs[n], refs[count + n], sems.at[n]) for n in range(count)
    ]
    for copy in copies:
        copy.start()
    for copy in copies:
        copy.wait()


def up_kernel(
    x_ref, basis_ref, trans_ref, side, halo_ref, own, tst_ref, diag, flat
):
    points = x_ref.shape[1]
    leaf_count, rank, leaf = basis_ref.shape
    for first in range(0, rank // 4, 4):
        blocks = [
            trans_ref[128 * step : 128 * step + 128, :].astype(F32).T
            for step in range(first, first + 4)
        ]
        for q in range(4):
            pieces = [block if q == 0 else pltpu.roll(block, 128 - 32 * q, 1) for block in blocks]
            for step, piece in enumerate(pieces, first):
                flat[pl.ds(4 * step + q, leaf_count, stride=rank), :] = piece
    tst_ref[...] = flat[:, 0:rank].astype(BF)
    fill_block_diagonal(basis_ref, diag)

    odd = lax.rem(lax.axis_index("leaf"), 2) == 1
    base = HALO * leaf // 128 * 64
    for t in range(HALO * leaf // 128):
        rows = slice(64 * t, 64 * t + 64)
        at = points - HALO * leaf + 128 * t
        head, tail = x_ref[:, 128 * t : 128 * t + 128], x_ref[:, at : at + 128]
        side[rows, :] = jnp.where(odd, head, tail)
        halo_ref[:, 128 * t : 128 * t + 128] = jnp.where(odd, tail, head)

    def put(at, left, right):
        rows = left.shape[0]
        both = jnp.where(low_half(rows), left, right)
        own[at : at + rows, :] = both
        side[base + at : base + at + rows, :] = both

    parent_count = leaf_count // 8
    skels = []
    for quad in range(leaf_count // 4):
        x = x_ref[:, 256 * quad : 256 * quad + 256]
        skels.append(
            matmul_nt(
                diag[128 * quad : 128 * quad + 128, :], jnp.concatenate([x, x], 0)
            ).astype(BF)
        )
    parents = [
        matmul_tn(
            tst_ref[256 * p : 256 * p + 256, :], jnp.concatenate(skels[2 * p : 2 * p + 2], 0)
        ).astype(BF)
        for p in range(parent_count)
    ]
    for quad, skel in enumerate(skels):
        put(64 * quad, skel[:64], skel[64:])
    for m in range((parent_count + 1) // 2):
        put(16 * leaf_count + 32 * m, parents[2 * m], parents[min(2 * m + 1, parent_count - 1)])


def place(r, leaf_count):
    safe = jnp.minimum(r, leaf_count - 1)
    return pl.multiple_of((safe >> 2) * 64 + (safe & 1) * 32, 32), (safe >> 1) & 1


def join_kernel(base, own_ref, one_ref, out_ref):
    size = own_ref.shape[0]
    out_ref[:size, :] = own_ref[...]
    out_ref[size:, :] = one_ref[base:, :]


def near_kernel(
    x_ref,
    one_ref,
    two_ref,
    near_ref,
    source_hbm,
    out_ref,
    source_ref,
    held,
    twice,
    sems,
):
    leaf_count, leaf, depth = near_ref.shape
    count = source_hbm.shape[0]
    quads = leaf_count // 4
    copy_source = pltpu.make_async_copy(source_hbm, source_ref, sems.at[quads])
    copy_source.start()

    def copy(quad):
        part = pl.ds(4 * quad, 4)
        return pltpu.make_async_copy(near_ref.at[part], held.at[part], sems.at[quad])

    for quad in range(quads):
        copy(quad).start()

    low = low_half(leaf)

    def spread(parts):
        others = [swapped(value) for value, _ in parts]
        for (value, at), other in zip(parts, others):
            twice[at] = jnp.where(low, value, other)
            twice[at + 1] = jnp.where(low, other, value)

    odd = lax.rem(lax.axis_index("leaf"), 2) == 1
    after = HALO + leaf_count
    at_one, at_two = jnp.where(odd, 0, after), jnp.where(odd, after, 0)
    halos = range(HALO // 2)
    spread([(one_ref[64 * n : 64 * n + 64, :], at_one + 2 * n) for n in halos])
    spread([(two_ref[:, 128 * n : 128 * n + 128], at_two + 2 * n) for n in halos])
    for first in range(0, leaf_count // 2, 5):
        spread(
            [(x_ref[:, 128 * n : 128 * n + 128], HALO + 2 * n) for n in range(first, first + 5)]
        )
    copy_source.wait()

    def product(i):
        pieces = [
            jnp.where(low, twice[source_ref[2 * m, i]], twice[source_ref[2 * m + 1, i]])
            for m in range(count // 2)
        ]
        if count % 2:
            pieces.append(twice[source_ref[count - 1, i]][:, :leaf])
        return matmul_nt(jnp.concatenate(pieces, 1), held[i])

    def body(step, carry):
        copy(2 * step).wait()
        copy(2 * step + 1).wait()
        parts = [product(8 * step + u) for u in range(8)]
        for t in range(4):
            lanes = pl.ds(pl.multiple_of(512 * step + 128 * t, 128), 128)
            out_ref[:, lanes] = jnp.concatenate(parts[2 * t : 2 * t + 2], 1)
        return carry

    lax.fori_loop(0, quads // 2, body, 0)


def split(value):
    low = low_half(value.shape[0])
    other = swapped(value)
    return jnp.where(low, value, other), jnp.where(low, other, value)


class Tables:
    def __init__(self, leaf_count, slots, window, requests):
        self.leaf_count, self.slots, self.window, self.requests = leaf_count, slots, window, requests
        self.parent_count = leaf_count // 8

    def put_parents(self, ref, at, reach, up):
        block = jnp.where(up, 4 + reach, 4 - reach)
        at = at + 16 * self.leaf_count
        tiles = range((self.parent_count + 1) // 2)
        values = [ref[at + 32 * m : at + 32 * m + 32, :] for m in tiles]
        for m, (left, right) in zip(tiles, [split(value) for value in values]):
            self.window[self.parent_count * block + 2 * m] = left
            if 2 * m + 1 < self.parent_count:
                self.window[self.parent_count * block + 2 * m + 1] = right

    def put_own(self, ref):
        for first in range(0, self.leaf_count // 4, 5):
            quads = range(first, first + 5)
            values = [ref[64 * quad : 64 * quad + 64, :] for quad in quads]
            for quad, (left, right) in zip(quads, [split(value) for value in values]):
                self.slots[4 * quad] = left[:32]
                self.slots[4 * quad + 1] = left[32:]
                self.slots[4 * quad + 2] = right[:32]
                self.slots[4 * quad + 3] = right[32:]
        self.put_parents(ref, 0, 0, False)

    def look_up(self, ref, at, reach, up):
        k = jnp.where(up, 3 + reach, 4 - reach)
        low = low_half(32)
        asked = [self.requests[k, c] for c in range(8)]
        places = [place(r, self.leaf_count) for r in asked]
        values = [ref[pl.ds(at + row, 32), :] for row, _ in places]
        others = [swapped(value) for value in values]
        for c, r in enumerate(asked):
            value = jnp.where(low == (places[c][1] == 0), values[c], others[c])
            self.slots[self.leaf_count + 8 * k + c] = jnp.where(
                r < self.leaf_count, value, jnp.zeros_like(value)
            )


def is_odd():
    return lax.rem(lax.axis_index("leaf"), 2) == 1


def first_kernel(leaf_count, base, own_ref, one_ref, ask_ref, slots, window, requests, sem):
    copy = pltpu.make_async_copy(ask_ref, requests, sem)
    copy.start()
    tables = Tables(leaf_count, slots, window, requests)
    place_of_one = (one_ref, base, 1, jnp.logical_not(is_odd()))
    tables.put_own(own_ref)
    tables.put_parents(*place_of_one)
    copy.wait()
    tables.look_up(*place_of_one)


def second_kernel(
    leaf_count, three_ref, far_ref, ask_ref, slots_in, window_in, slots, window, requests, sem
):
    copy = pltpu.make_async_copy(ask_ref, requests, sem)
    copy.start()
    tables = Tables(leaf_count, slots, window, requests)
    odd = is_odd()
    size = far_ref.shape[0] // 2
    places = (
        (three_ref, size, 2, jnp.logical_not(odd)),
        (three_ref, 0, 3, jnp.logical_not(odd)),
        (far_ref, 0, 3, odd),
        (far_ref, size, 4, odd),
    )
    for where in places:
        tables.put_parents(*where)
    copy.wait()
    for where in places:
        tables.look_up(*where)


def down_kernel(
    three_over,
    far_over,
    ask_ref,
    coup_hbm,
    par_hbm,
    coup_ref,
    par_ref,
    diag,
    tst_ref,
    near_ref,
    slots_in,
    window_in,
    out_hbm,
    slots,
    window,
    requests,
    coup_source,
    par_source,
    weights,
    stack,
    outs,
    leaf_outs,
    out_ref,
    sems,
    out_sems,
):
    copies = [
        pltpu.make_async_copy(source, held, sems.at[n])
        for n, (source, held) in enumerate(
            ((ask_ref, requests), (par_hbm, par_source), (coup_hbm, coup_source))
        )
    ]
    for copy in copies:
        copy.start()
    leaf_count, rank = coup_ref.shape[:2]
    parent_count = par_ref.shape[0]
    low64 = low_half(64)
    low = low_half(rank)
    tables = Tables(leaf_count, slots, window, requests)
    odd = is_odd()
    size = far_over.shape[0] // 2
    places = (
        (three_over, size, 1, odd),
        (three_over, 0, 2, odd),
        (far_over, 0, 4, jnp.logical_not(odd)),
    )
    for where in places:
        tables.put_parents(*where)
    copies[0].wait()
    for where in places:
        tables.look_up(*where)
    copies[1].wait()
    copies[2].wait()
    per = par_source.shape[1]
    coup = coup_source.shape[0]
    pairs = [(2 * m, min(2 * m + 1, parent_count - 1)) for m in range((parent_count + 1) // 2)]
    for first in range(0, per, 4):
        loaded = [
            [(window[par_source[p, j]], window[par_source[q, j]]) for p, q in pairs]
            for j in range(first, first + 4)
        ]
        for j, tiles in enumerate(loaded, first):
            for m, (left, right) in enumerate(tiles):
                stack[rank * j : rank * j + rank, 128 * m : 128 * m + 128] = jnp.where(
                    low, left, right
                )
    rows = par_ref[...].reshape(parent_count * rank, per * rank)
    parent_outs = matmul(rows, stack[...]).astype(BF)
    for p in range(parent_count):
        tile = parent_outs[rank * p : rank * p + rank, 128 * (p // 2) : 128 * (p // 2) + 128]
        outs[p] = split(tile)[p % 2]

    def build(quad):
        for first in range(0, coup, 4):
            loaded = [
                [
                    (slots[coup_source[j, 4 * quad + t]], slots[coup_source[j, 4 * quad + t + 1]])
                    for t in (0, 2)
                ]
                for j in range(first, first + 4)
            ]
            for j, tiles in enumerate(loaded, first):
                for t, (left, right) in enumerate(tiles):
                    weights[quad, rank * j : rank * j + rank, 128 * t : 128 * t + 128] = jnp.where(
                        low, left, right
                    )

    quads = leaf_count // 4
    build(0)
    build(1)
    downs = [
        matmul(tst_ref[256 * p : 256 * p + 256, :], outs[p]) for p in range(parent_count)
    ]
    for quad in range(quads):
        if quad + 2 < quads:
            build(quad + 2)
        rows = coup_ref[4 * quad : 4 * quad + 4].reshape(4 * rank, coup * rank)
        coupled = matmul(rows, weights[quad])
        coupled = jnp.concatenate([coupled[:64, :128], coupled[64:, 128:]], 0)
        down = downs[quad // 2][128 * (quad % 2) : 128 * (quad % 2) + 128]
        leaf_outs[128 * quad : 128 * quad + 128, :] = (coupled + down).astype(BF)

    def send(p):
        part = pl.ds(512 * p, 512)
        return pltpu.make_async_copy(out_ref.at[:, part], out_hbm.at[:, part], out_sems.at[p])

    for first in range(0, quads, 2):
        tiles = []
        for quad in range(first, first + 2):
            rows = slice(128 * quad, 128 * quad + 128)
            far = matmul_tn(leaf_outs[rows, :], diag[rows, :])
            for t in range(2):
                lanes = slice(256 * quad + 128 * t, 256 * quad + 128 * t + 128)
                tile = jnp.where(
                    low64, far[:64, 128 * t : 128 * t + 128], far[64:, 128 * t : 128 * t + 128]
                )
                tiles.append((lanes, (near_ref[:, lanes] + tile).astype(BF)))
        for lanes, tile in tiles:
            out_ref[:, lanes] = tile
        send(first // 2).start()
    for p in range(parent_count):
        send(p).wait()


def in_hbm(array):
    return pltpu.with_memory_space_constraint(array, pltpu.HBM)


def params(mib):
    return pltpu.CompilerParams(vmem_limit_bytes=mib << 20)


def cost(flops, size):
    return pl.CostEstimate(flops=flops, bytes_accessed=size, transcendentals=0)


def shards(
    rhs,
    basis,
    transfer,
    near_rows,
    near_source,
    far_request,
    coup_rows,
    coup_source,
    par_rows,
    par_source,
):
    leaf_count, leaf, rank = basis.shape
    points, rhs_count = rhs.shape
    parent_count = par_rows.shape[0]
    near_count = near_source.shape[1]
    coup_count = coup_source.shape[1]
    base = HALO // 2 * rhs_count
    parent_rows = rank * ((parent_count + 1) // 2)
    packed = base + 16 * leaf_count + parent_rows
    count = lax.axis_size("leaf")

    x = rhs.T
    trans = transfer.transpose(1, 2, 0).reshape(rank * rank, leaf_count)
    shape = jax.ShapeDtypeStruct
    vmem, hbm = (pl.BlockSpec(memory_space=kind) for kind in (VMEM, pltpu.HBM))
    basis_t = basis.transpose(0, 2, 1)
    inputs = (x, basis_t, trans, far_request[0])
    x, basis_t, trans, ask = pl.pallas_call(
        load_kernel,
        out_shape=tuple(shape(held.shape, held.dtype) for held in inputs),
        in_specs=[hbm] * 4,
        out_specs=(vmem,) * 4,
        scratch_shapes=[DMA((4,))],
        compiler_params=params(8),
        cost_estimate=cost(10**6, 2 * 10**6),
        name="load",
    )(*(in_hbm(held) for held in inputs))

    def exchange(block, begin, distance=1):
        pairs = [(i, i + distance) for i in range(begin, count - distance, 2)]
        return lax.ppermute(block, "leaf", pairs + [(b, a) for a, b in pairs])

    side, halo, own, tst, diag = pl.pallas_call(
        up_kernel,
        out_shape=(
            shape((packed, 128), BF),
            shape((rhs_count, HALO * leaf), BF),
            shape((packed - base, 128), BF),
            shape((rank * leaf_count, rank), BF),
            shape((rank * leaf_count, 256), BF),
        ),
        in_specs=[vmem] * 3,
        out_specs=(vmem,) * 5,
        scratch_shapes=[VMEM((rank * leaf_count, 128), F32)],
        compiler_params=params(8),
        cost_estimate=cost(10**9, 2 * 10**6),
        name="upward",
    )(x, basis_t, trans)
    one = exchange(side, 0)
    two = exchange(halo, 1)
    both = pl.pallas_call(
        functools.partial(join_kernel, base),
        out_shape=shape((2 * (packed - base), 128), BF),
        in_specs=[vmem] * 2,
        out_specs=vmem,
        compiler_params=params(8),
        cost_estimate=cost(10**6, 10**6),
        name="join",
    )(own, one)
    far = exchange(both, 1, 3)
    three = exchange(both, 0, 3)
    table_shapes = (
        shape((leaf_count + 64, rank, 128), BF),
        shape((9 * parent_count, rank, 128), BF),
    )
    tables = pl.pallas_call(
        functools.partial(first_kernel, leaf_count, base),
        out_shape=table_shapes,
        in_specs=[vmem] * 3,
        out_specs=(vmem,) * 2,
        scratch_shapes=[SMEM(ask.shape, jnp.int32), pltpu.SemaphoreType.DMA],
        compiler_params=params(8),
        cost_estimate=cost(10**6, 10**6),
        name="first_tables",
    )(own, one, ask)
    near = pl.pallas_call(
        near_kernel,
        out_shape=shape((rhs_count, points), F32),
        in_specs=[vmem, vmem, vmem, hbm, hbm],
        out_specs=vmem,
        scratch_shapes=[
            SMEM((near_count, leaf_count), jnp.int32),
            VMEM(near_rows.shape, BF),
            VMEM((leaf_count + 2 * HALO, leaf, 128), BF),
            DMA((leaf_count // 4 + 1,)),
        ],
        compiler_params=params(20),
        cost_estimate=cost(35 * 10**8, 9 * 10**5 * 5),
        name="near",
    )(x, one, two, in_hbm(near_rows), in_hbm(near_source.T))

    three, far, near, tables = lax.optimization_barrier((three, far, near, tables))
    three_over = exchange(three, 0)
    far_over = exchange(far, 0)

    tables = pl.pallas_call(
        functools.partial(second_kernel, leaf_count),
        out_shape=table_shapes,
        in_specs=[vmem] * 5,
        out_specs=(vmem,) * 2,
        scratch_shapes=[SMEM(ask.shape, jnp.int32), pltpu.SemaphoreType.DMA],
        input_output_aliases={3: 0, 4: 1},
        compiler_params=params(8),
        cost_estimate=cost(10**6, 10**6),
        name="second_tables",
    )(three, far, ask, *tables)

    product, _, _ = pl.pallas_call(
        down_kernel,
        out_shape=(shape((rhs_count, points), BF),) + table_shapes,
        in_specs=[vmem] * 3 + [hbm] * 2 + [vmem] * 7,
        out_specs=(hbm, vmem, vmem),
        input_output_aliases={10: 1, 11: 2},
        scratch_shapes=[
            SMEM(ask.shape, jnp.int32),
            SMEM((coup_count, leaf_count), jnp.int32),
            SMEM(par_source.shape, jnp.int32),
            VMEM((leaf_count // 4, coup_count * rank, 256), BF),
            VMEM((par_source.shape[1] * rank, 128 * ((parent_count + 1) // 2)), BF),
            VMEM((parent_count, rank, 128), BF),
            VMEM((rank * leaf_count, 128), BF),
            VMEM((rhs_count, points), BF),
            DMA((3,)),
            DMA((parent_count,)),
        ],
        compiler_params=params(12),
        cost_estimate=cost(10**9, 4 * 10**6),
        name="downward",
    )(
        three_over,
        far_over,
        ask,
        in_hbm(coup_source.T),
        in_hbm(par_source),
        coup_rows,
        par_rows,
        diag,
        tst,
        near,
        *tables,
    )
    return product.T


def solution(mesh):
    split = ("groups", "leaf")
    return jax.shard_map(
        shards,
        mesh=mesh,
        in_specs=(
            P(split, None),
            P(split, None, None),
            P(split, None, None),
            P(split, None, None),
            P(split, None),
            P(split, None, None),
            P(split, None, None),
            P(split, None),
            P(split, None, None),
            P(split, None),
        ),
        out_specs=P(split, None),
        check_vma=False,
    )
```

```python
import functools

import jax
import jax.numpy as jnp
from jax import lax
from jax.experimental import pallas as pl
from jax.experimental.pallas import tpu as pltpu
from jax.sharding import PartitionSpec as P

HALO = 16
BF = jnp.bfloat16
F32 = jnp.float32
VMEM = pltpu.VMEM
SMEM = pltpu.SMEM
DMA = pltpu.SemaphoreType.DMA


def low_half(rows):
    return lax.broadcasted_iota(jnp.int32, (rows, 128), 1) < 64


def swapped(value):
    return pltpu.roll(value, 64, 1)


def matmul(a, b):
    return jnp.dot(a, b, preferred_element_type=F32)


def matmul_nt(a, b):
    return lax.dot_general(a, b, (((1,), (1,)), ((), ())), preferred_element_type=F32)


def matmul_tn(a, b):
    return lax.dot_general(a, b, (((0,), (0,)), ((), ())), preferred_element_type=F32)


def fill_block_diagonal(basis_ref, diag):
    leaf_count, rank, leaf = basis_ref.shape
    blank = jnp.zeros((rank, leaf), BF)
    empty = jnp.zeros((rank, 2 * leaf), BF)
    for i in range(leaf_count):
        at = 128 * (1 - i % 4 // 2)
        diag[rank * i : rank * (i + 1), at : at + 128] = empty
    for first in range(0, leaf_count, 8):
        tiles = []
        for i in range(first, first + 8):
            block = basis_ref[i]
            tiles.append(jnp.concatenate([blank, block] if i % 2 else [block, blank], 1))
        for i, tile in enumerate(tiles, first):
            at = 128 * (i % 4 // 2)
            diag[rank * i : rank * (i + 1), at : at + 128] = tile


def load_kernel(*refs):
    count = len(refs) // 2
    sems = refs[-1]
    copies = [
        pltpu.make_async_copy(refs[n], refs[count + n], sems.at[n]) for n in range(count)
    ]
    for copy in copies:
        copy.start()
    for copy in copies:
        copy.wait()


def up_kernel(
    x_ref, basis_ref, trans_ref, side, halo_ref, own, tst_ref, diag, flat
):
    points = x_ref.shape[1]
    leaf_count, rank, leaf = basis_ref.shape
    for first in range(0, rank // 4, 4):
        blocks = [
            trans_ref[128 * step : 128 * step + 128, :].astype(F32).T
            for step in range(first, first + 4)
        ]
        for q in range(4):
            pieces = [block if q == 0 else pltpu.roll(block, 128 - 32 * q, 1) for block in blocks]
            for step, piece in enumerate(pieces, first):
                flat[pl.ds(4 * step + q, leaf_count, stride=rank), :] = piece
    tst_ref[...] = flat[:, 0:rank].astype(BF)
    fill_block_diagonal(basis_ref, diag)

    odd = lax.rem(lax.axis_index("leaf"), 2) == 1
    base = HALO * leaf // 128 * 64
    for t in range(HALO * leaf // 128):
        rows = slice(64 * t, 64 * t + 64)
        at = points - HALO * leaf + 128 * t
        head, tail = x_ref[:, 128 * t : 128 * t + 128], x_ref[:, at : at + 128]
        side[rows, :] = jnp.where(odd, head, tail)
        halo_ref[:, 128 * t : 128 * t + 128] = jnp.where(odd, tail, head)

    def put(at, left, right):
        rows = left.shape[0]
        both = jnp.where(low_half(rows), left, right)
        own[at : at + rows, :] = both
        side[base + at : base + at + rows, :] = both

    parent_count = leaf_count // 8
    skels = []
    for quad in range(leaf_count // 4):
        x = x_ref[:, 256 * quad : 256 * quad + 256]
        skels.append(
            matmul_nt(
                diag[128 * quad : 128 * quad + 128, :], jnp.concatenate([x, x], 0)
            ).astype(BF)
        )
    parents = [
        matmul_tn(
            tst_ref[256 * p : 256 * p + 256, :], jnp.concatenate(skels[2 * p : 2 * p + 2], 0)
        ).astype(BF)
        for p in range(parent_count)
    ]
    for quad, skel in enumerate(skels):
        put(64 * quad, skel[:64], skel[64:])
    for m in range((parent_count + 1) // 2):
        put(16 * leaf_count + 32 * m, parents[2 * m], parents[min(2 * m + 1, parent_count - 1)])


def place(r, leaf_count):
    safe = jnp.minimum(r, leaf_count - 1)
    return pl.multiple_of((safe >> 2) * 64 + (safe & 1) * 32, 32), (safe >> 1) & 1


def wanted(requests, reach, up):
    row = requests[pl.ds(jnp.where(up, 3 + reach, 4 - reach), 1), :]
    return [row[0, c] for c in range(8)]


def join_kernel(base, own_ref, one_ref, out_ref):
    size = own_ref.shape[0]
    out_ref[:size, :] = own_ref[...]
    out_ref[size:, :] = one_ref[base:, :]


def near_kernel(
    x_ref,
    one_ref,
    two_ref,
    near_ref,
    source_hbm,
    out_ref,
    source_ref,
    held,
    twice,
    sems,
):
    leaf_count, leaf, depth = near_ref.shape
    count = source_hbm.shape[0]
    quads = leaf_count // 4
    copy_source = pltpu.make_async_copy(source_hbm, source_ref, sems.at[quads])
    copy_source.start()

    def copy(quad):
        part = pl.ds(4 * quad, 4)
        return pltpu.make_async_copy(near_ref.at[part], held.at[part], sems.at[quad])

    for quad in range(quads):
        copy(quad).start()

    low = low_half(leaf)

    def spread(parts):
        others = [swapped(value) for value, _ in parts]
        for (value, at), other in zip(parts, others):
            twice[at] = jnp.where(low, value, other)
            twice[at + 1] = jnp.where(low, other, value)

    odd = lax.rem(lax.axis_index("leaf"), 2) == 1
    after = HALO + leaf_count
    at_one, at_two = jnp.where(odd, 0, after), jnp.where(odd, after, 0)
    halos = range(HALO // 2)
    spread([(one_ref[64 * n : 64 * n + 64, :], at_one + 2 * n) for n in halos])
    spread([(two_ref[:, 128 * n : 128 * n + 128], at_two + 2 * n) for n in halos])
    for first in range(0, leaf_count // 2, 5):
        spread(
            [(x_ref[:, 128 * n : 128 * n + 128], HALO + 2 * n) for n in range(first, first + 5)]
        )
    copy_source.wait()

    def product(i):
        pieces = [
            jnp.where(low, twice[source_ref[2 * m, i]], twice[source_ref[2 * m + 1, i]])
            for m in range(count // 2)
        ]
        if count % 2:
            pieces.append(twice[source_ref[count - 1, i]][:, :leaf])
        return matmul_nt(jnp.concatenate(pieces, 1), held[i])

    def body(step, carry):
        copy(2 * step).wait()
        copy(2 * step + 1).wait()
        parts = [product(8 * step + u) for u in range(8)]
        for t in range(4):
            lanes = pl.ds(pl.multiple_of(512 * step + 128 * t, 128), 128)
            out_ref[:, lanes] = jnp.concatenate(parts[2 * t : 2 * t + 2], 1)
        return carry

    lax.fori_loop(0, quads // 2, body, 0)


def split(value):
    low = low_half(value.shape[0])
    other = swapped(value)
    return jnp.where(low, value, other), jnp.where(low, other, value)


class Tables:
    def __init__(self, leaf_count, slots, window, requests):
        self.leaf_count, self.slots, self.window, self.requests = leaf_count, slots, window, requests
        self.parent_count = leaf_count // 8

    def put_parents(self, ref, at, reach, up):
        block = jnp.where(up, 4 + reach, 4 - reach)
        tiles = range((self.parent_count + 1) // 2)
        values = [ref[at + 32 * m : at + 32 * m + 32, :] for m in tiles]
        for m, (left, right) in zip(tiles, [split(value) for value in values]):
            self.window[self.parent_count * block + 2 * m] = left
            if 2 * m + 1 < self.parent_count:
                self.window[self.parent_count * block + 2 * m + 1] = right

    def put_own(self, ref):
        for first in range(0, self.leaf_count // 4, 5):
            quads = range(first, first + 5)
            values = [ref[64 * quad : 64 * quad + 64, :] for quad in quads]
            for quad, (left, right) in zip(quads, [split(value) for value in values]):
                self.slots[4 * quad] = left[:32]
                self.slots[4 * quad + 1] = left[32:]
                self.slots[4 * quad + 2] = right[:32]
                self.slots[4 * quad + 3] = right[32:]
        self.put_parents(ref, 16 * self.leaf_count, 0, False)

    def put_reply(self, ref, at, reach, up):
        k = jnp.where(up, 3 + reach, 4 - reach)
        values = [ref[at + 32 * m : at + 32 * m + 32, :] for m in range(4)]
        for m, (left, right) in enumerate([split(value) for value in values]):
            self.slots[self.leaf_count + 8 * k + 2 * m] = left
            self.slots[self.leaf_count + 8 * k + 2 * m + 1] = right

    def look_up(self, ref, at, reach, up):
        k = jnp.where(up, 3 + reach, 4 - reach)
        low = low_half(32)
        asked = wanted(self.requests, reach, up)
        places = [place(r, self.leaf_count) for r in asked]
        values = [ref[pl.ds(at + row, 32), :] for row, _ in places]
        others = [swapped(value) for value in values]
        for c, r in enumerate(asked):
            value = jnp.where(low == (places[c][1] == 0), values[c], others[c])
            self.slots[self.leaf_count + 8 * k + c] = jnp.where(
                r < self.leaf_count, value, jnp.zeros_like(value)
            )


def is_odd():
    return lax.rem(lax.axis_index("leaf"), 2) == 1


def first_kernel(leaf_count, base, own_ref, one_ref, requests, slots, window):
    tables = Tables(leaf_count, slots, window, requests)
    inward = jnp.logical_not(is_odd())
    tables.look_up(one_ref, base, 1, inward)
    tables.put_parents(one_ref, base + 16 * leaf_count, 1, inward)
    tables.put_own(own_ref)


def hand_kernel(leaf_count, three_ref, far_ref, requests, out_ref):
    outward = jnp.logical_not(is_odd())
    low = low_half(32)
    size = far_ref.shape[0] // 2
    parents = 16 * leaf_count
    places = (
        (three_ref, size, 1, outward),
        (three_ref, 0, 2, outward),
        (far_ref, 0, 4, is_odd()),
    )
    for n, (ref, at, reach, up) in enumerate(places):
        asked = wanted(requests, reach, up)
        values = []
        for c, r in enumerate(asked):
            row, high = place(r, leaf_count)
            value = ref[pl.ds(at + row, 32), :]
            value = jnp.where(high != c % 2, swapped(value), value)
            values.append(jnp.where(r < leaf_count, value, jnp.zeros_like(value)))
        for m in range(4):
            row = 128 * n + 32 * m
            out_ref[row : row + 32, :] = jnp.where(low, values[2 * m], values[2 * m + 1])
        rows = 384 + (size - parents) * n
        out_ref[rows : rows + size - parents, :] = ref[at + parents : at + size, :]


def second_kernel(leaf_count, three_ref, far_ref, requests, slots_in, window_in, slots, window):
    tables = Tables(leaf_count, slots, window, requests)
    odd = is_odd()
    size = far_ref.shape[0] // 2
    for ref, at, reach, up in (
        (three_ref, size, 2, jnp.logical_not(odd)),
        (three_ref, 0, 3, jnp.logical_not(odd)),
        (far_ref, 0, 3, odd),
        (far_ref, size, 4, odd),
    ):
        tables.look_up(ref, at, reach, up)
        tables.put_parents(ref, at + 16 * leaf_count, reach, up)


def down_kernel(
    over_ref,
    coup_hbm,
    par_hbm,
    coup_ref,
    par_ref,
    diag,
    tst_ref,
    near_ref,
    slots_in,
    window_in,
    out_hbm,
    slots,
    window,
    coup_source,
    par_source,
    weights,
    stack,
    outs,
    leaf_outs,
    out_ref,
    sems,
    out_sems,
):
    copies = [
        pltpu.make_async_copy(source, held, sems.at[n])
        for n, (source, held) in enumerate(((par_hbm, par_source), (coup_hbm, coup_source)))
    ]
    for copy in copies:
        copy.start()
    leaf_count, rank = coup_ref.shape[:2]
    parent_count = par_ref.shape[0]
    low64 = low_half(64)
    low = low_half(rank)
    tables = Tables(leaf_count, slots, window, None)
    odd = is_odd()
    parent_size = (over_ref.shape[0] - 384) // 3
    for n, (reach, up) in enumerate(((1, odd), (2, odd), (4, jnp.logical_not(odd)))):
        tables.put_reply(over_ref, 128 * n, reach, up)
        tables.put_parents(over_ref, 384 + parent_size * n, reach, up)
    for copy in copies:
        copy.wait()
    per = par_source.shape[1]
    coup = coup_source.shape[0]
    pairs = [(2 * m, min(2 * m + 1, parent_count - 1)) for m in range((parent_count + 1) // 2)]
    for first in range(0, per, 4):
        loaded = [
            [(window[par_source[p, j]], window[par_source[q, j]]) for p, q in pairs]
            for j in range(first, first + 4)
        ]
        for j, tiles in enumerate(loaded, first):
            for m, (left, right) in enumerate(tiles):
                stack[rank * j : rank * j + rank, 128 * m : 128 * m + 128] = jnp.where(
                    low, left, right
                )
    rows = par_ref[...].reshape(parent_count * rank, per * rank)
    parent_outs = matmul(rows, stack[...]).astype(BF)
    for p in range(parent_count):
        tile = parent_outs[rank * p : rank * p + rank, 128 * (p // 2) : 128 * (p // 2) + 128]
        outs[p] = split(tile)[p % 2]

    def build(quad):
        for first in range(0, coup, 4):
            loaded = [
                [
                    (slots[coup_source[j, 4 * quad + t]], slots[coup_source[j, 4 * quad + t + 1]])
                    for t in (0, 2)
                ]
                for j in range(first, first + 4)
            ]
            for j, tiles in enumerate(loaded, first):
                for t, (left, right) in enumerate(tiles):
                    weights[quad, rank * j : rank * j + rank, 128 * t : 128 * t + 128] = jnp.where(
                        low, left, right
                    )

    quads = leaf_count // 4
    build(0)
    build(1)
    downs = [
        matmul(tst_ref[256 * p : 256 * p + 256, :], outs[p]) for p in range(parent_count)
    ]
    for quad in range(quads):
        if quad + 2 < quads:
            build(quad + 2)
        rows = coup_ref[4 * quad : 4 * quad + 4].reshape(4 * rank, coup * rank)
        coupled = matmul(rows, weights[quad])
        coupled = jnp.concatenate([coupled[:64, :128], coupled[64:, 128:]], 0)
        down = downs[quad // 2][128 * (quad % 2) : 128 * (quad % 2) + 128]
        leaf_outs[128 * quad : 128 * quad + 128, :] = (coupled + down).astype(BF)

    def send(p):
        part = pl.ds(512 * p, 512)
        return pltpu.make_async_copy(out_ref.at[:, part], out_hbm.at[:, part], out_sems.at[p])

    for first in range(0, quads, 2):
        tiles = []
        for quad in range(first, first + 2):
            rows = slice(128 * quad, 128 * quad + 128)
            far = matmul_tn(leaf_outs[rows, :], diag[rows, :])
            for t in range(2):
                lanes = slice(256 * quad + 128 * t, 256 * quad + 128 * t + 128)
                tile = jnp.where(
                    low64, far[:64, 128 * t : 128 * t + 128], far[64:, 128 * t : 128 * t + 128]
                )
                tiles.append((lanes, (near_ref[:, lanes] + tile).astype(BF)))
        for lanes, tile in tiles:
            out_ref[:, lanes] = tile
        send(first // 2).start()
    for p in range(parent_count):
        send(p).wait()


def in_hbm(array):
    return pltpu.with_memory_space_constraint(array, pltpu.HBM)


def params(mib):
    return pltpu.CompilerParams(vmem_limit_bytes=mib << 20)


def cost(flops, size):
    return pl.CostEstimate(flops=flops, bytes_accessed=size, transcendentals=0)


def shards(
    rhs,
    basis,
    transfer,
    near_rows,
    near_source,
    far_request,
    coup_rows,
    coup_source,
    par_rows,
    par_source,
):
    leaf_count, leaf, rank = basis.shape
    points, rhs_count = rhs.shape
    parent_count = par_rows.shape[0]
    near_count = near_source.shape[1]
    coup_count = coup_source.shape[1]
    base = HALO // 2 * rhs_count
    parent_rows = rank * ((parent_count + 1) // 2)
    packed = base + 16 * leaf_count + parent_rows
    count = lax.axis_size("leaf")

    x = rhs.T
    trans = transfer.transpose(1, 2, 0).reshape(rank * rank, leaf_count)
    shape = jax.ShapeDtypeStruct
    vmem, hbm = (pl.BlockSpec(memory_space=kind) for kind in (VMEM, pltpu.HBM))
    basis_t = basis.transpose(0, 2, 1)
    inputs = (x, basis_t, trans, far_request[0])
    x, basis_t, trans, ask = pl.pallas_call(
        load_kernel,
        out_shape=tuple(shape(held.shape, held.dtype) for held in inputs),
        in_specs=[hbm] * 4,
        out_specs=(vmem,) * 4,
        scratch_shapes=[DMA((4,))],
        compiler_params=params(8),
        cost_estimate=cost(10**6, 2 * 10**6),
        name="load",
    )(*(in_hbm(held) for held in inputs))

    def exchange(block, begin, distance=1):
        pairs = [(i, i + distance) for i in range(begin, count - distance, 2)]
        return lax.ppermute(block, "leaf", pairs + [(b, a) for a, b in pairs])

    other_ask = exchange(far_request[0], 0)
    side, halo, own, tst, diag = pl.pallas_call(
        up_kernel,
        out_shape=(
            shape((packed, 128), BF),
            shape((rhs_count, HALO * leaf), BF),
            shape((packed - base, 128), BF),
            shape((rank * leaf_count, rank), BF),
            shape((rank * leaf_count, 256), BF),
        ),
        in_specs=[vmem] * 3,
        out_specs=(vmem,) * 5,
        scratch_shapes=[VMEM((rank * leaf_count, 128), F32)],
        compiler_params=params(8),
        cost_estimate=cost(10**9, 2 * 10**6),
        name="upward",
    )(x, basis_t, trans)
    one = exchange(side, 0)
    two = exchange(halo, 1)
    both = pl.pallas_call(
        functools.partial(join_kernel, base),
        out_shape=shape((2 * (packed - base), 128), BF),
        in_specs=[vmem] * 2,
        out_specs=vmem,
        compiler_params=params(8),
        cost_estimate=cost(10**6, 10**6),
        name="join",
    )(own, one)
    far = exchange(both, 1, 3)
    three = exchange(both, 0, 3)
    table_shapes = (
        shape((leaf_count + 64, rank, 128), BF),
        shape((9 * parent_count, rank, 128), BF),
    )
    tables = pl.pallas_call(
        functools.partial(first_kernel, leaf_count, base),
        out_shape=table_shapes,
        in_specs=[vmem] * 3,
        out_specs=(vmem,) * 2,
        compiler_params=params(8),
        cost_estimate=cost(10**6, 10**6),
        name="first_tables",
    )(own, one, ask)
    near = pl.pallas_call(
        near_kernel,
        out_shape=shape((rhs_count, points), F32),
        in_specs=[vmem, vmem, vmem, hbm, hbm],
        out_specs=vmem,
        scratch_shapes=[
            SMEM((near_count, leaf_count), jnp.int32),
            VMEM(near_rows.shape, BF),
            VMEM((leaf_count + 2 * HALO, leaf, 128), BF),
            DMA((leaf_count // 4 + 1,)),
        ],
        compiler_params=params(20),
        cost_estimate=cost(35 * 10**8, 9 * 10**5 * 5),
        name="near",
    )(x, one, two, in_hbm(near_rows), in_hbm(near_source.T))

    three, far, near, tables = lax.optimization_barrier((three, far, near, tables))
    hand = pl.pallas_call(
        functools.partial(hand_kernel, leaf_count),
        out_shape=shape((384 + 3 * parent_rows, 128), BF),
        in_specs=[vmem] * 3,
        out_specs=vmem,
        compiler_params=params(8),
        cost_estimate=cost(10**6, 10**6),
        name="hand_over",
    )(three, far, other_ask)
    over = exchange(hand, 0)

    tables = pl.pallas_call(
        functools.partial(second_kernel, leaf_count),
        out_shape=table_shapes,
        in_specs=[vmem] * 5,
        out_specs=(vmem,) * 2,
        input_output_aliases={3: 0, 4: 1},
        compiler_params=params(8),
        cost_estimate=cost(10**6, 10**6),
        name="second_tables",
    )(three, far, ask, *tables)

    product, _, _ = pl.pallas_call(
        down_kernel,
        out_shape=(shape((rhs_count, points), BF),) + table_shapes,
        in_specs=[vmem] + [hbm] * 2 + [vmem] * 7,
        out_specs=(hbm, vmem, vmem),
        input_output_aliases={8: 1, 9: 2},
        scratch_shapes=[
            SMEM((coup_count, leaf_count), jnp.int32),
            SMEM(par_source.shape, jnp.int32),
            VMEM((leaf_count // 4, coup_count * rank, 256), BF),
            VMEM((par_source.shape[1] * rank, 128 * ((parent_count + 1) // 2)), BF),
            VMEM((parent_count, rank, 128), BF),
            VMEM((rank * leaf_count, 128), BF),
            VMEM((rhs_count, points), BF),
            DMA((2,)),
            DMA((parent_count,)),
        ],
        compiler_params=params(12),
        cost_estimate=cost(10**9, 4 * 10**6),
        name="downward",
    )(
        over,
        in_hbm(coup_source.T),
        in_hbm(par_source),
        coup_rows,
        par_rows,
        diag,
        tst,
        near,
        *tables,
    )
    return product.T


def solution(mesh):
    split = ("groups", "leaf")
    return jax.shard_map(
        shards,
        mesh=mesh,
        in_specs=(
            P(split, None),
            P(split, None, None),
            P(split, None, None),
            P(split, None, None),
            P(split, None),
            P(split, None, None),
            P(split, None, None),
            P(split, None),
            P(split, None, None),
            P(split, None),
        ),
        out_specs=P(split, None),
        check_vma=False,
    )
```

```python
import functools

import jax
import jax.numpy as jnp
from jax import lax
from jax.experimental import pallas as pl
from jax.experimental.pallas import tpu as pltpu
from jax.sharding import PartitionSpec as P

HALO = 16
BF = jnp.bfloat16
F32 = jnp.float32
VMEM = pltpu.VMEM
SMEM = pltpu.SMEM
DMA = pltpu.SemaphoreType.DMA


def low_half(rows):
    return lax.broadcasted_iota(jnp.int32, (rows, 128), 1) < 64


def swapped(value):
    return pltpu.roll(value, 64, 1)


def matmul(a, b):
    return jnp.dot(a, b, preferred_element_type=F32)


def matmul_nt(a, b):
    return lax.dot_general(a, b, (((1,), (1,)), ((), ())), preferred_element_type=F32)


def matmul_tn(a, b):
    return lax.dot_general(a, b, (((0,), (0,)), ((), ())), preferred_element_type=F32)


def fill_block_diagonal(basis_ref, diag):
    leaf_count, rank, leaf = basis_ref.shape
    blank = jnp.zeros((rank, leaf), BF)
    empty = jnp.zeros((rank, 2 * leaf), BF)
    for i in range(leaf_count):
        at = 128 * (1 - i % 4 // 2)
        diag[rank * i : rank * (i + 1), at : at + 128] = empty
    for first in range(0, leaf_count, 8):
        tiles = []
        for i in range(first, first + 8):
            block = basis_ref[i]
            tiles.append(jnp.concatenate([blank, block] if i % 2 else [block, blank], 1))
        for i, tile in enumerate(tiles, first):
            at = 128 * (i % 4 // 2)
            diag[rank * i : rank * (i + 1), at : at + 128] = tile


def load_kernel(*refs):
    count = len(refs) // 2
    sems = refs[-1]
    copies = [
        pltpu.make_async_copy(refs[n], refs[count + n], sems.at[n]) for n in range(count)
    ]
    for copy in copies:
        copy.start()
    for copy in copies:
        copy.wait()


def up_kernel(
    x_ref, basis_ref, trans_ref, side, halo_ref, own, tst_ref, diag, flat
):
    points = x_ref.shape[1]
    leaf_count, rank, leaf = basis_ref.shape
    for first in range(0, rank // 4, 4):
        blocks = [
            trans_ref[128 * step : 128 * step + 128, :].astype(F32).T
            for step in range(first, first + 4)
        ]
        for q in range(4):
            pieces = [block if q == 0 else pltpu.roll(block, 128 - 32 * q, 1) for block in blocks]
            for step, piece in enumerate(pieces, first):
                flat[pl.ds(4 * step + q, leaf_count, stride=rank), :] = piece
    tst_ref[...] = flat[:, 0:rank].astype(BF)
    fill_block_diagonal(basis_ref, diag)

    odd = lax.rem(lax.axis_index("leaf"), 2) == 1
    base = HALO * leaf // 128 * 64
    for t in range(HALO * leaf // 128):
        rows = slice(64 * t, 64 * t + 64)
        at = points - HALO * leaf + 128 * t
        head, tail = x_ref[:, 128 * t : 128 * t + 128], x_ref[:, at : at + 128]
        side[rows, :] = jnp.where(odd, head, tail)
        halo_ref[:, 128 * t : 128 * t + 128] = jnp.where(odd, tail, head)

    def put(at, left, right):
        rows = left.shape[0]
        both = jnp.where(low_half(rows), left, right)
        own[at : at + rows, :] = both
        side[base + at : base + at + rows, :] = both

    parent_count = leaf_count // 8
    skels = []
    for quad in range(leaf_count // 4):
        x = x_ref[:, 256 * quad : 256 * quad + 256]
        skels.append(
            matmul_nt(
                diag[128 * quad : 128 * quad + 128, :], jnp.concatenate([x, x], 0)
            ).astype(BF)
        )
    parents = [
        matmul_tn(
            tst_ref[256 * p : 256 * p + 256, :], jnp.concatenate(skels[2 * p : 2 * p + 2], 0)
        ).astype(BF)
        for p in range(parent_count)
    ]
    for quad, skel in enumerate(skels):
        put(64 * quad, skel[:64], skel[64:])
    for m in range((parent_count + 1) // 2):
        put(16 * leaf_count + 32 * m, parents[2 * m], parents[min(2 * m + 1, parent_count - 1)])


def place(r, leaf_count):
    safe = jnp.minimum(r, leaf_count - 1)
    return pl.multiple_of((safe >> 2) * 64 + (safe & 1) * 32, 32), (safe >> 1) & 1


def wanted(requests, reach, up):
    row = requests[pl.ds(jnp.where(up, 3 + reach, 4 - reach), 1), :]
    return [row[0, c] for c in range(8)]


def join_kernel(base, own_ref, one_ref, out_ref):
    size = own_ref.shape[0]
    out_ref[:size, :] = own_ref[...]
    out_ref[size:, :] = one_ref[base:, :]


def near_kernel(
    x_ref,
    one_ref,
    two_ref,
    near_ref,
    source_hbm,
    out_ref,
    source_ref,
    held,
    twice,
    sems,
):
    leaf_count, leaf, depth = near_ref.shape
    count = source_hbm.shape[0]
    quads = leaf_count // 4
    copy_source = pltpu.make_async_copy(source_hbm, source_ref, sems.at[quads])
    copy_source.start()

    def copy(quad):
        part = pl.ds(4 * quad, 4)
        return pltpu.make_async_copy(near_ref.at[part], held.at[part], sems.at[quad])

    for quad in range(quads):
        copy(quad).start()

    low = low_half(leaf)

    def spread(parts):
        others = [swapped(value) for value, _ in parts]
        for (value, at), other in zip(parts, others):
            twice[at] = jnp.where(low, value, other)
            twice[at + 1] = jnp.where(low, other, value)

    odd = lax.rem(lax.axis_index("leaf"), 2) == 1
    after = HALO + leaf_count
    at_one, at_two = jnp.where(odd, 0, after), jnp.where(odd, after, 0)
    halos = range(HALO // 2)
    spread([(one_ref[64 * n : 64 * n + 64, :], at_one + 2 * n) for n in halos])
    spread([(two_ref[:, 128 * n : 128 * n + 128], at_two + 2 * n) for n in halos])
    for first in range(0, leaf_count // 2, 5):
        spread(
            [(x_ref[:, 128 * n : 128 * n + 128], HALO + 2 * n) for n in range(first, first + 5)]
        )
    copy_source.wait()

    def product(i):
        pieces = [
            jnp.where(low, twice[source_ref[2 * m, i]], twice[source_ref[2 * m + 1, i]])
            for m in range(count // 2)
        ]
        if count % 2:
            pieces.append(twice[source_ref[count - 1, i]][:, :leaf])
        return matmul_nt(jnp.concatenate(pieces, 1), held[i])

    def body(step, carry):
        copy(2 * step).wait()
        copy(2 * step + 1).wait()
        parts = [product(8 * step + u) for u in range(8)]
        for t in range(4):
            lanes = pl.ds(pl.multiple_of(512 * step + 128 * t, 128), 128)
            out_ref[:, lanes] = jnp.concatenate(parts[2 * t : 2 * t + 2], 1)
        return carry

    lax.fori_loop(0, quads // 2, body, 0)


def split(value):
    low = low_half(value.shape[0])
    other = swapped(value)
    return jnp.where(low, value, other), jnp.where(low, other, value)


class Tables:
    def __init__(self, leaf_count, slots, window, requests):
        self.leaf_count, self.slots, self.window, self.requests = leaf_count, slots, window, requests
        self.parent_count = leaf_count // 8

    def put_parents(self, ref, at, reach, up):
        block = jnp.where(up, 4 + reach, 4 - reach)
        tiles = range((self.parent_count + 1) // 2)
        values = [ref[at + 32 * m : at + 32 * m + 32, :] for m in tiles]
        for m, (left, right) in zip(tiles, [split(value) for value in values]):
            self.window[self.parent_count * block + 2 * m] = left
            if 2 * m + 1 < self.parent_count:
                self.window[self.parent_count * block + 2 * m + 1] = right

    def put_own(self, ref):
        for first in range(0, self.leaf_count // 4, 5):
            quads = range(first, first + 5)
            values = [ref[64 * quad : 64 * quad + 64, :] for quad in quads]
            for quad, (left, right) in zip(quads, [split(value) for value in values]):
                self.slots[4 * quad] = left[:32]
                self.slots[4 * quad + 1] = left[32:]
                self.slots[4 * quad + 2] = right[:32]
                self.slots[4 * quad + 3] = right[32:]
        self.put_parents(ref, 16 * self.leaf_count, 0, False)

    def put_reply(self, ref, at, reach, up):
        k = jnp.where(up, 3 + reach, 4 - reach)
        values = [ref[at + 32 * m : at + 32 * m + 32, :] for m in range(4)]
        for m, (left, right) in enumerate([split(value) for value in values]):
            self.slots[self.leaf_count + 8 * k + 2 * m] = left
            self.slots[self.leaf_count + 8 * k + 2 * m + 1] = right

    def look_up(self, ref, at, reach, up):
        k = jnp.where(up, 3 + reach, 4 - reach)
        low = low_half(32)
        asked = wanted(self.requests, reach, up)
        places = [place(r, self.leaf_count) for r in asked]
        values = [ref[pl.ds(at + row, 32), :] for row, _ in places]
        others = [swapped(value) for value in values]
        for c, r in enumerate(asked):
            value = jnp.where(low == (places[c][1] == 0), values[c], others[c])
            self.slots[self.leaf_count + 8 * k + c] = jnp.where(
                r < self.leaf_count, value, jnp.zeros_like(value)
            )


def is_odd():
    return lax.rem(lax.axis_index("leaf"), 2) == 1


def first_kernel(leaf_count, base, own_ref, one_ref, requests, slots, window):
    tables = Tables(leaf_count, slots, window, requests)
    inward = jnp.logical_not(is_odd())
    tables.look_up(one_ref, base, 1, inward)
    tables.put_parents(one_ref, base + 16 * leaf_count, 1, inward)
    tables.put_own(own_ref)


def hand_kernel(leaf_count, three_ref, far_ref, requests, out_ref):
    outward = jnp.logical_not(is_odd())
    low = low_half(32)
    size = far_ref.shape[0] // 2
    parents = 16 * leaf_count
    places = (
        (three_ref, size, 1, outward),
        (three_ref, 0, 2, outward),
        (far_ref, 0, 4, is_odd()),
    )
    for n, (ref, at, reach, up) in enumerate(places):
        asked = wanted(requests, reach, up)
        values = []
        for c, r in enumerate(asked):
            row, high = place(r, leaf_count)
            value = ref[pl.ds(at + row, 32), :]
            value = jnp.where(high != c % 2, swapped(value), value)
            values.append(jnp.where(r < leaf_count, value, jnp.zeros_like(value)))
        for m in range(4):
            row = 128 * n + 32 * m
            out_ref[row : row + 32, :] = jnp.where(low, values[2 * m], values[2 * m + 1])
        rows = 384 + (size - parents) * n
        out_ref[rows : rows + size - parents, :] = ref[at + parents : at + size, :]


def second_kernel(leaf_count, three_ref, far_ref, requests, slots_in, window_in, slots, window):
    tables = Tables(leaf_count, slots, window, requests)
    odd = is_odd()
    size = far_ref.shape[0] // 2
    for ref, at, reach, up in (
        (three_ref, size, 2, jnp.logical_not(odd)),
        (three_ref, 0, 3, jnp.logical_not(odd)),
        (far_ref, 0, 3, odd),
        (far_ref, size, 4, odd),
    ):
        tables.look_up(ref, at, reach, up)
        tables.put_parents(ref, at + 16 * leaf_count, reach, up)


def down_kernel(
    over_ref,
    coup_hbm,
    par_rows,
    coup_ref,
    par_ref,
    diag,
    tst_ref,
    near_ref,
    slots_in,
    window_in,
    out_hbm,
    slots,
    window,
    coup_source,
    weights,
    stack,
    outs,
    out_ref,
    sem,
    out_sems,
):
    copy = pltpu.make_async_copy(coup_hbm, coup_source, sem)
    copy.start()
    leaf_count, rank = coup_ref.shape[:2]
    parent_count = par_ref.shape[0]
    low64 = low_half(64)
    low = low_half(rank)
    tables = Tables(leaf_count, slots, window, None)
    odd = is_odd()
    parent_size = (over_ref.shape[0] - 384) // 3
    for n, (reach, up) in enumerate(((1, odd), (2, odd), (4, jnp.logical_not(odd)))):
        tables.put_reply(over_ref, 128 * n, reach, up)
        tables.put_parents(over_ref, 384 + parent_size * n, reach, up)
    per = par_ref.shape[2] // rank
    par_source = par_rows[...]
    coup = coup_source.shape[0]
    pairs = [(2 * m, min(2 * m + 1, parent_count - 1)) for m in range((parent_count + 1) // 2)]
    for first in range(0, per, 4):
        loaded = [
            [(window[par_source[p, j]], window[par_source[q, j]]) for p, q in pairs]
            for j in range(first, first + 4)
        ]
        for j, tiles in enumerate(loaded, first):
            for m, (left, right) in enumerate(tiles):
                stack[rank * j : rank * j + rank, 128 * m : 128 * m + 128] = jnp.where(
                    low, left, right
                )
    rows = par_ref[...].reshape(parent_count * rank, per * rank)
    parent_outs = matmul(rows, stack[...]).astype(BF)
    for p in range(parent_count):
        tile = parent_outs[rank * p : rank * p + rank, 128 * (p // 2) : 128 * (p // 2) + 128]
        outs[p] = split(tile)[p % 2]

    def build(quad):
        for first in range(0, coup, 4):
            loaded = [
                [
                    (slots[coup_source[j, 4 * quad + t]], slots[coup_source[j, 4 * quad + t + 1]])
                    for t in (0, 2)
                ]
                for j in range(first, first + 4)
            ]
            for j, tiles in enumerate(loaded, first):
                for t, (left, right) in enumerate(tiles):
                    weights[quad, rank * j : rank * j + rank, 128 * t : 128 * t + 128] = jnp.where(
                        low, left, right
                    )

    quads = leaf_count // 4
    downs = [
        matmul(tst_ref[256 * p : 256 * p + 256, :], outs[p]) for p in range(parent_count)
    ]

    def couple(quad):
        rows = coup_ref[4 * quad : 4 * quad + 4].reshape(4 * rank, coup * rank)
        coupled = matmul(rows, weights[quad])
        coupled = jnp.concatenate([coupled[:64, :128], coupled[64:, 128:]], 0)
        down = downs[quad // 2][128 * (quad % 2) : 128 * (quad % 2) + 128]
        return (coupled + down).astype(BF)

    def send(quad):
        part = pl.ds(256 * quad, 256)
        return pltpu.make_async_copy(out_ref.at[:, part], out_hbm.at[:, part], out_sems.at[quad])

    def finish(quad, leaf_out):
        far = matmul_tn(leaf_out, diag[128 * quad : 128 * quad + 128, :])
        for t in range(2):
            lanes = slice(256 * quad + 128 * t, 256 * quad + 128 * t + 128)
            tile = jnp.where(
                low64, far[:64, 128 * t : 128 * t + 128], far[64:, 128 * t : 128 * t + 128]
            )
            out_ref[:, lanes] = (near_ref[:, lanes] + tile).astype(BF)
        send(quad).start()

    copy.wait()
    build(0)
    build(1)
    waiting = None
    for quad in range(quads):
        if quad + 2 < quads:
            build(quad + 2)
        leaf_out = couple(quad)
        if waiting is not None:
            finish(quad - 1, waiting)
        waiting = leaf_out
    finish(quads - 1, waiting)
    for quad in range(quads):
        send(quad).wait()


def in_hbm(array):
    return pltpu.with_memory_space_constraint(array, pltpu.HBM)


def params(mib):
    return pltpu.CompilerParams(vmem_limit_bytes=mib << 20)


def cost(flops, size):
    return pl.CostEstimate(flops=flops, bytes_accessed=size, transcendentals=0)


def shards(
    rhs,
    basis,
    transfer,
    near_rows,
    near_source,
    far_request,
    coup_rows,
    coup_source,
    par_rows,
    par_source,
):
    leaf_count, leaf, rank = basis.shape
    points, rhs_count = rhs.shape
    parent_count = par_rows.shape[0]
    near_count = near_source.shape[1]
    coup_count = coup_source.shape[1]
    base = HALO // 2 * rhs_count
    parent_rows = rank * ((parent_count + 1) // 2)
    packed = base + 16 * leaf_count + parent_rows
    count = lax.axis_size("leaf")

    x = rhs.T
    trans = transfer.transpose(1, 2, 0).reshape(rank * rank, leaf_count)
    shape = jax.ShapeDtypeStruct
    vmem, hbm = (pl.BlockSpec(memory_space=kind) for kind in (VMEM, pltpu.HBM))
    basis_t = basis.transpose(0, 2, 1)
    inputs = (x, basis_t, trans, far_request[0])
    x, basis_t, trans, ask = pl.pallas_call(
        load_kernel,
        out_shape=tuple(shape(held.shape, held.dtype) for held in inputs),
        in_specs=[hbm] * 4,
        out_specs=(vmem,) * 4,
        scratch_shapes=[DMA((4,))],
        compiler_params=params(8),
        cost_estimate=cost(10**6, 2 * 10**6),
        name="load",
    )(*(in_hbm(held) for held in inputs))

    def exchange(block, begin, distance=1):
        pairs = [(i, i + distance) for i in range(begin, count - distance, 2)]
        return lax.ppermute(block, "leaf", pairs + [(b, a) for a, b in pairs])

    other_ask = exchange(far_request[0], 0)
    side, halo, own, tst, diag = pl.pallas_call(
        up_kernel,
        out_shape=(
            shape((packed, 128), BF),
            shape((rhs_count, HALO * leaf), BF),
            shape((packed - base, 128), BF),
            shape((rank * leaf_count, rank), BF),
            shape((rank * leaf_count, 256), BF),
        ),
        in_specs=[vmem] * 3,
        out_specs=(vmem,) * 5,
        scratch_shapes=[VMEM((rank * leaf_count, 128), F32)],
        compiler_params=params(8),
        cost_estimate=cost(10**9, 2 * 10**6),
        name="upward",
    )(x, basis_t, trans)
    one = exchange(side, 0)
    two = exchange(halo, 1)
    both = pl.pallas_call(
        functools.partial(join_kernel, base),
        out_shape=shape((2 * (packed - base), 128), BF),
        in_specs=[vmem] * 2,
        out_specs=vmem,
        compiler_params=params(8),
        cost_estimate=cost(10**6, 10**6),
        name="join",
    )(own, one)
    far = exchange(both, 1, 3)
    three = exchange(both, 0, 3)
    table_shapes = (
        shape((leaf_count + 64, rank, 128), BF),
        shape((9 * parent_count, rank, 128), BF),
    )
    tables = pl.pallas_call(
        functools.partial(first_kernel, leaf_count, base),
        out_shape=table_shapes,
        in_specs=[vmem] * 3,
        out_specs=(vmem,) * 2,
        compiler_params=params(8),
        cost_estimate=cost(10**6, 10**6),
        name="first_tables",
    )(own, one, ask)
    near = pl.pallas_call(
        near_kernel,
        out_shape=shape((rhs_count, points), F32),
        in_specs=[vmem, vmem, vmem, hbm, hbm],
        out_specs=vmem,
        scratch_shapes=[
            SMEM((near_count, leaf_count), jnp.int32),
            VMEM(near_rows.shape, BF),
            VMEM((leaf_count + 2 * HALO, leaf, 128), BF),
            DMA((leaf_count // 4 + 1,)),
        ],
        compiler_params=params(20),
        cost_estimate=cost(35 * 10**8, 9 * 10**5 * 5),
        name="near",
    )(x, one, two, in_hbm(near_rows), in_hbm(near_source.T))

    three, far, near, tables = lax.optimization_barrier((three, far, near, tables))
    hand = pl.pallas_call(
        functools.partial(hand_kernel, leaf_count),
        out_shape=shape((384 + 3 * parent_rows, 128), BF),
        in_specs=[vmem] * 3,
        out_specs=vmem,
        compiler_params=params(8),
        cost_estimate=cost(10**6, 10**6),
        name="hand_over",
    )(three, far, other_ask)
    over = exchange(hand, 0)

    tables = pl.pallas_call(
        functools.partial(second_kernel, leaf_count),
        out_shape=table_shapes,
        in_specs=[vmem] * 5,
        out_specs=(vmem,) * 2,
        input_output_aliases={3: 0, 4: 1},
        compiler_params=params(8),
        cost_estimate=cost(10**6, 10**6),
        name="second_tables",
    )(three, far, ask, *tables)

    product, _, _ = pl.pallas_call(
        down_kernel,
        out_shape=(shape((rhs_count, points), BF),) + table_shapes,
        in_specs=[vmem, hbm] + [vmem] * 8,
        out_specs=(hbm, vmem, vmem),
        input_output_aliases={8: 1, 9: 2},
        scratch_shapes=[
            SMEM((coup_count, leaf_count), jnp.int32),
            VMEM((leaf_count // 4, coup_count * rank, 256), BF),
            VMEM((par_source.shape[1] * rank, 128 * ((parent_count + 1) // 2)), BF),
            VMEM((parent_count, rank, 128), BF),
            VMEM((rhs_count, points), BF),
            pltpu.SemaphoreType.DMA,
            DMA((leaf_count // 4,)),
        ],
        compiler_params=params(12),
        cost_estimate=cost(10**9, 4 * 10**6),
        name="downward",
    )(
        over,
        in_hbm(coup_source.T),
        par_source,
        coup_rows,
        par_rows,
        diag,
        tst,
        near,
        *tables,
    )
    return product.T


def solution(mesh):
    split = ("groups", "leaf")
    return jax.shard_map(
        shards,
        mesh=mesh,
        in_specs=(
            P(split, None),
            P(split, None, None),
            P(split, None, None),
            P(split, None, None),
            P(split, None),
            P(split, None, None),
            P(split, None, None),
            P(split, None),
            P(split, None, None),
            P(split, None),
        ),
        out_specs=P(split, None),
        check_vma=False,
    )
```

```python
import functools

import jax
import jax.numpy as jnp
from jax import lax
from jax.experimental import pallas as pl
from jax.experimental.pallas import tpu as pltpu
from jax.sharding import PartitionSpec as P

HALO = 16
BF = jnp.bfloat16
F32 = jnp.float32
VMEM = pltpu.VMEM
SMEM = pltpu.SMEM
DMA = pltpu.SemaphoreType.DMA


def low_half(rows):
    return lax.broadcasted_iota(jnp.int32, (rows, 128), 1) < 64


def swapped(value):
    return pltpu.roll(value, 64, 1)


def matmul(a, b):
    return jnp.dot(a, b, preferred_element_type=F32)


def matmul_nt(a, b):
    return lax.dot_general(a, b, (((1,), (1,)), ((), ())), preferred_element_type=F32)


def matmul_tn(a, b):
    return lax.dot_general(a, b, (((0,), (0,)), ((), ())), preferred_element_type=F32)


def fill_block_diagonal(basis_ref, diag):
    leaf_count, rank, leaf = basis_ref.shape
    blank = jnp.zeros((rank, leaf), BF)
    empty = jnp.zeros((rank, 2 * leaf), BF)
    for i in range(leaf_count):
        at = 128 * (1 - i % 4 // 2)
        diag[rank * i : rank * (i + 1), at : at + 128] = empty
    for first in range(0, leaf_count, 8):
        tiles = []
        for i in range(first, first + 8):
            block = basis_ref[i]
            tiles.append(jnp.concatenate([blank, block] if i % 2 else [block, blank], 1))
        for i, tile in enumerate(tiles, first):
            at = 128 * (i % 4 // 2)
            diag[rank * i : rank * (i + 1), at : at + 128] = tile


def load_kernel(*refs):
    count = len(refs) // 2
    sems = refs[-1]
    copies = [
        pltpu.make_async_copy(refs[n], refs[count + n], sems.at[n]) for n in range(count)
    ]
    for copy in copies:
        copy.start()
    for copy in copies:
        copy.wait()


def up_kernel(
    x_ref, basis_ref, trans_ref, side, halo_ref, own, tst_ref, diag, flat
):
    points = x_ref.shape[1]
    leaf_count, rank, leaf = basis_ref.shape
    for first in range(0, rank // 4, 4):
        blocks = [
            trans_ref[128 * step : 128 * step + 128, :].astype(F32).T
            for step in range(first, first + 4)
        ]
        for q in range(4):
            pieces = [block if q == 0 else pltpu.roll(block, 128 - 32 * q, 1) for block in blocks]
            for step, piece in enumerate(pieces, first):
                flat[pl.ds(4 * step + q, leaf_count, stride=rank), :] = piece
    tst_ref[...] = flat[:, 0:rank].astype(BF)
    fill_block_diagonal(basis_ref, diag)

    odd = lax.rem(lax.axis_index("leaf"), 2) == 1
    base = HALO * leaf // 128 * 64
    for t in range(HALO * leaf // 128):
        rows = slice(64 * t, 64 * t + 64)
        at = points - HALO * leaf + 128 * t
        head, tail = x_ref[:, 128 * t : 128 * t + 128], x_ref[:, at : at + 128]
        side[rows, :] = jnp.where(odd, head, tail)
        halo_ref[:, 128 * t : 128 * t + 128] = jnp.where(odd, tail, head)

    def put(at, left, right):
        rows = left.shape[0]
        both = jnp.where(low_half(rows), left, right)
        own[at : at + rows, :] = both
        side[base + at : base + at + rows, :] = both

    parent_count = leaf_count // 8
    skels = []
    for quad in range(leaf_count // 4):
        x = x_ref[:, 256 * quad : 256 * quad + 256]
        skels.append(
            matmul_nt(
                diag[128 * quad : 128 * quad + 128, :], jnp.concatenate([x, x], 0)
            ).astype(BF)
        )
    parents = [
        matmul_tn(
            tst_ref[256 * p : 256 * p + 256, :], jnp.concatenate(skels[2 * p : 2 * p + 2], 0)
        ).astype(BF)
        for p in range(parent_count)
    ]
    for quad, skel in enumerate(skels):
        put(64 * quad, skel[:64], skel[64:])
    for m in range((parent_count + 1) // 2):
        put(16 * leaf_count + 32 * m, parents[2 * m], parents[min(2 * m + 1, parent_count - 1)])


def place(r, leaf_count):
    safe = jnp.minimum(r, leaf_count - 1)
    return pl.multiple_of((safe >> 2) * 64 + (safe & 1) * 32, 32), (safe >> 1) & 1


def wanted(requests, reach, up):
    row = requests[pl.ds(jnp.where(up, 3 + reach, 4 - reach), 1), :]
    return [row[0, c] for c in range(8)]


def join_kernel(base, own_ref, one_ref, out_ref):
    size = own_ref.shape[0]
    out_ref[:size, :] = own_ref[...]
    out_ref[size:, :] = one_ref[base:, :]


def near_kernel(
    x_ref,
    one_ref,
    two_ref,
    near_ref,
    source_hbm,
    out_ref,
    source_ref,
    held,
    twice,
    sems,
):
    leaf_count, leaf, depth = near_ref.shape
    count = source_hbm.shape[0]
    quads = leaf_count // 4
    copy_source = pltpu.make_async_copy(source_hbm, source_ref, sems.at[quads])
    copy_source.start()

    def copy(quad):
        part = pl.ds(4 * quad, 4)
        return pltpu.make_async_copy(near_ref.at[part], held.at[part], sems.at[quad])

    for quad in range(quads):
        copy(quad).start()

    low = low_half(leaf)

    def spread(parts):
        others = [swapped(value) for value, _ in parts]
        for (value, at), other in zip(parts, others):
            twice[at] = jnp.where(low, value, other)
            twice[at + 1] = jnp.where(low, other, value)

    odd = lax.rem(lax.axis_index("leaf"), 2) == 1
    after = HALO + leaf_count
    at_one, at_two = jnp.where(odd, 0, after), jnp.where(odd, after, 0)
    halos = range(HALO // 2)
    spread([(one_ref[64 * n : 64 * n + 64, :], at_one + 2 * n) for n in halos])
    spread([(two_ref[:, 128 * n : 128 * n + 128], at_two + 2 * n) for n in halos])
    for first in range(0, leaf_count // 2, 5):
        spread(
            [(x_ref[:, 128 * n : 128 * n + 128], HALO + 2 * n) for n in range(first, first + 5)]
        )
    copy_source.wait()

    def product(i):
        pieces = [
            jnp.where(low, twice[source_ref[2 * m, i]], twice[source_ref[2 * m + 1, i]])
            for m in range(count // 2)
        ]
        if count % 2:
            pieces.append(twice[source_ref[count - 1, i]][:, :leaf])
        return matmul_nt(jnp.concatenate(pieces, 1), held[i])

    def body(step, carry):
        tiles = []

        def store(t):
            lanes = pl.ds(pl.multiple_of(64 * quads * 2 * step + 128 * t, 128), 128)
            out_ref[:, lanes] = tiles[t]

        for t in range(quads):
            if t % 2 == 0:
                copy(quads // 2 * step + t // 2).wait()
            i = 2 * quads * step + 2 * t
            tiles.append(jnp.concatenate([product(i), product(i + 1)], 1))
            if t >= 3:
                store(t - 3)
        for t in range(quads - 3, quads):
            store(t)
        return carry

    lax.fori_loop(0, 2, body, 0)


def split(value):
    low = low_half(value.shape[0])
    other = swapped(value)
    return jnp.where(low, value, other), jnp.where(low, other, value)


class Tables:
    def __init__(self, leaf_count, slots, window, requests):
        self.leaf_count, self.slots, self.window, self.requests = leaf_count, slots, window, requests
        self.parent_count = leaf_count // 8

    def put_parents(self, ref, at, reach, up):
        block = jnp.where(up, 4 + reach, 4 - reach)
        tiles = range((self.parent_count + 1) // 2)
        values = [ref[at + 32 * m : at + 32 * m + 32, :] for m in tiles]
        for m, (left, right) in zip(tiles, [split(value) for value in values]):
            self.window[self.parent_count * block + 2 * m] = left
            if 2 * m + 1 < self.parent_count:
                self.window[self.parent_count * block + 2 * m + 1] = right

    def put_own(self, ref):
        for first in range(0, self.leaf_count // 4, 5):
            quads = range(first, first + 5)
            values = [ref[64 * quad : 64 * quad + 64, :] for quad in quads]
            for quad, (left, right) in zip(quads, [split(value) for value in values]):
                self.slots[4 * quad] = left[:32]
                self.slots[4 * quad + 1] = left[32:]
                self.slots[4 * quad + 2] = right[:32]
                self.slots[4 * quad + 3] = right[32:]
        self.put_parents(ref, 16 * self.leaf_count, 0, False)

    def put_reply(self, ref, at, reach, up):
        k = jnp.where(up, 3 + reach, 4 - reach)
        values = [ref[at + 32 * m : at + 32 * m + 32, :] for m in range(4)]
        for m, (left, right) in enumerate([split(value) for value in values]):
            self.slots[self.leaf_count + 8 * k + 2 * m] = left
            self.slots[self.leaf_count + 8 * k + 2 * m + 1] = right

    def look_up(self, ref, at, reach, up):
        k = jnp.where(up, 3 + reach, 4 - reach)
        low = low_half(32)
        asked = wanted(self.requests, reach, up)
        places = [place(r, self.leaf_count) for r in asked]
        values = [ref[pl.ds(at + row, 32), :] for row, _ in places]
        others = [swapped(value) for value in values]
        for c, r in enumerate(asked):
            value = jnp.where(low == (places[c][1] == 0), values[c], others[c])
            self.slots[self.leaf_count + 8 * k + c] = jnp.where(
                r < self.leaf_count, value, jnp.zeros_like(value)
            )


def is_odd():
    return lax.rem(lax.axis_index("leaf"), 2) == 1


def first_kernel(leaf_count, base, own_ref, one_ref, requests, slots, window):
    tables = Tables(leaf_count, slots, window, requests)
    inward = jnp.logical_not(is_odd())
    tables.look_up(one_ref, base, 1, inward)
    tables.put_parents(one_ref, base + 16 * leaf_count, 1, inward)
    tables.put_own(own_ref)


def hand_kernel(leaf_count, three_ref, far_ref, requests, out_ref):
    outward = jnp.logical_not(is_odd())
    low = low_half(32)
    size = far_ref.shape[0] // 2
    parents = 16 * leaf_count
    places = (
        (three_ref, size, 1, outward),
        (three_ref, 0, 2, outward),
        (far_ref, 0, 4, is_odd()),
    )
    for n, (ref, at, reach, up) in enumerate(places):
        asked = wanted(requests, reach, up)
        values = []
        for c, r in enumerate(asked):
            row, high = place(r, leaf_count)
            value = ref[pl.ds(at + row, 32), :]
            value = jnp.where(high != c % 2, swapped(value), value)
            values.append(jnp.where(r < leaf_count, value, jnp.zeros_like(value)))
        for m in range(4):
            row = 128 * n + 32 * m
            out_ref[row : row + 32, :] = jnp.where(low, values[2 * m], values[2 * m + 1])
        rows = 384 + (size - parents) * n
        out_ref[rows : rows + size - parents, :] = ref[at + parents : at + size, :]


def second_kernel(leaf_count, three_ref, far_ref, requests, slots_in, window_in, slots, window):
    tables = Tables(leaf_count, slots, window, requests)
    odd = is_odd()
    size = far_ref.shape[0] // 2
    for ref, at, reach, up in (
        (three_ref, size, 2, jnp.logical_not(odd)),
        (three_ref, 0, 3, jnp.logical_not(odd)),
        (far_ref, 0, 3, odd),
        (far_ref, size, 4, odd),
    ):
        tables.look_up(ref, at, reach, up)
        tables.put_parents(ref, at + 16 * leaf_count, reach, up)


def down_kernel(
    over_ref,
    coup_hbm,
    par_rows,
    coup_ref,
    par_ref,
    diag,
    tst_ref,
    near_ref,
    slots_in,
    window_in,
    out_hbm,
    slots,
    window,
    coup_source,
    weights,
    stack,
    outs,
    leaf_outs,
    out_ref,
    sem,
    out_sems,
):
    copy = pltpu.make_async_copy(coup_hbm, coup_source, sem)
    copy.start()
    leaf_count, rank = coup_ref.shape[:2]
    parent_count = par_ref.shape[0]
    low64 = low_half(64)
    low = low_half(rank)
    tables = Tables(leaf_count, slots, window, None)
    odd = is_odd()
    parent_size = (over_ref.shape[0] - 384) // 3
    for n, (reach, up) in enumerate(((1, odd), (2, odd), (4, jnp.logical_not(odd)))):
        tables.put_reply(over_ref, 128 * n, reach, up)
        tables.put_parents(over_ref, 384 + parent_size * n, reach, up)
    per = par_ref.shape[2] // rank
    par_source = par_rows[...]
    coup = coup_source.shape[0]
    pairs = [(2 * m, min(2 * m + 1, parent_count - 1)) for m in range((parent_count + 1) // 2)]
    for first in range(0, per, 4):
        loaded = [
            [(window[par_source[p, j]], window[par_source[q, j]]) for p, q in pairs]
            for j in range(first, first + 4)
        ]
        for j, tiles in enumerate(loaded, first):
            for m, (left, right) in enumerate(tiles):
                stack[rank * j : rank * j + rank, 128 * m : 128 * m + 128] = jnp.where(
                    low, left, right
                )
    rows = par_ref[...].reshape(parent_count * rank, per * rank)
    parent_outs = matmul(rows, stack[...]).astype(BF)
    for p in range(parent_count):
        tile = parent_outs[rank * p : rank * p + rank, 128 * (p // 2) : 128 * (p // 2) + 128]
        outs[p] = split(tile)[p % 2]

    def build(quad):
        for first in range(0, coup, 4):
            loaded = [
                [
                    (slots[coup_source[j, 4 * quad + t]], slots[coup_source[j, 4 * quad + t + 1]])
                    for t in (0, 2)
                ]
                for j in range(first, first + 4)
            ]
            for j, tiles in enumerate(loaded, first):
                for t, (left, right) in enumerate(tiles):
                    weights[quad, rank * j : rank * j + rank, 128 * t : 128 * t + 128] = jnp.where(
                        low, left, right
                    )

    quads = leaf_count // 4
    downs = [
        matmul(tst_ref[256 * p : 256 * p + 256, :], outs[p]) for p in range(parent_count)
    ]
    copy.wait()
    build(0)
    build(1)
    for quad in range(quads):
        if quad + 2 < quads:
            build(quad + 2)
        rows = coup_ref[4 * quad : 4 * quad + 4].reshape(4 * rank, coup * rank)
        coupled = matmul(rows, weights[quad])
        coupled = jnp.concatenate([coupled[:64, :128], coupled[64:, 128:]], 0)
        down = downs[quad // 2][128 * (quad % 2) : 128 * (quad % 2) + 128]
        leaf_outs[128 * quad : 128 * quad + 128, :] = (coupled + down).astype(BF)

    def send(p):
        part = pl.ds(512 * p, 512)
        return pltpu.make_async_copy(out_ref.at[:, part], out_hbm.at[:, part], out_sems.at[p])

    for first in range(0, quads, 2):
        tiles = []
        for quad in range(first, first + 2):
            rows = slice(128 * quad, 128 * quad + 128)
            far = matmul_tn(leaf_outs[rows, :], diag[rows, :])
            for t in range(2):
                lanes = slice(256 * quad + 128 * t, 256 * quad + 128 * t + 128)
                tile = jnp.where(
                    low64, far[:64, 128 * t : 128 * t + 128], far[64:, 128 * t : 128 * t + 128]
                )
                tiles.append((lanes, (near_ref[:, lanes] + tile).astype(BF)))
        for lanes, tile in tiles:
            out_ref[:, lanes] = tile
        send(first // 2).start()
    for p in range(parent_count):
        send(p).wait()


def in_hbm(array):
    return pltpu.with_memory_space_constraint(array, pltpu.HBM)


def params(mib):
    return pltpu.CompilerParams(vmem_limit_bytes=mib << 20)


def cost(flops, size):
    return pl.CostEstimate(flops=flops, bytes_accessed=size, transcendentals=0)


def shards(
    rhs,
    basis,
    transfer,
    near_rows,
    near_source,
    far_request,
    coup_rows,
    coup_source,
    par_rows,
    par_source,
):
    leaf_count, leaf, rank = basis.shape
    points, rhs_count = rhs.shape
    parent_count = par_rows.shape[0]
    near_count = near_source.shape[1]
    coup_count = coup_source.shape[1]
    base = HALO // 2 * rhs_count
    parent_rows = rank * ((parent_count + 1) // 2)
    packed = base + 16 * leaf_count + parent_rows
    count = lax.axis_size("leaf")

    x = rhs.T
    trans = transfer.transpose(1, 2, 0).reshape(rank * rank, leaf_count)
    shape = jax.ShapeDtypeStruct
    vmem, hbm = (pl.BlockSpec(memory_space=kind) for kind in (VMEM, pltpu.HBM))
    basis_t = basis.transpose(0, 2, 1)
    inputs = (x, basis_t, trans, far_request[0])
    x, basis_t, trans, ask = pl.pallas_call(
        load_kernel,
        out_shape=tuple(shape(held.shape, held.dtype) for held in inputs),
        in_specs=[hbm] * 4,
        out_specs=(vmem,) * 4,
        scratch_shapes=[DMA((4,))],
        compiler_params=params(8),
        cost_estimate=cost(10**6, 2 * 10**6),
        name="load",
    )(*(in_hbm(held) for held in inputs))

    def exchange(block, begin, distance=1):
        pairs = [(i, i + distance) for i in range(begin, count - distance, 2)]
        return lax.ppermute(block, "leaf", pairs + [(b, a) for a, b in pairs])

    other_ask = exchange(far_request[0], 0)
    side, halo, own, tst, diag = pl.pallas_call(
        up_kernel,
        out_shape=(
            shape((packed, 128), BF),
            shape((rhs_count, HALO * leaf), BF),
            shape((packed - base, 128), BF),
            shape((rank * leaf_count, rank), BF),
            shape((rank * leaf_count, 256), BF),
        ),
        in_specs=[vmem] * 3,
        out_specs=(vmem,) * 5,
        scratch_shapes=[VMEM((rank * leaf_count, 128), F32)],
        compiler_params=params(8),
        cost_estimate=cost(10**9, 2 * 10**6),
        name="upward",
    )(x, basis_t, trans)
    one = exchange(side, 0)
    two = exchange(halo, 1)
    both = pl.pallas_call(
        functools.partial(join_kernel, base),
        out_shape=shape((2 * (packed - base), 128), BF),
        in_specs=[vmem] * 2,
        out_specs=vmem,
        compiler_params=params(8),
        cost_estimate=cost(10**6, 10**6),
        name="join",
    )(own, one)
    far = exchange(both, 1, 3)
    three = exchange(both, 0, 3)
    table_shapes = (
        shape((leaf_count + 64, rank, 128), BF),
        shape((9 * parent_count, rank, 128), BF),
    )
    tables = pl.pallas_call(
        functools.partial(first_kernel, leaf_count, base),
        out_shape=table_shapes,
        in_specs=[vmem] * 3,
        out_specs=(vmem,) * 2,
        compiler_params=params(8),
        cost_estimate=cost(10**6, 10**6),
        name="first_tables",
    )(own, one, ask)
    near = pl.pallas_call(
        near_kernel,
        out_shape=shape((rhs_count, points), F32),
        in_specs=[vmem, vmem, vmem, hbm, hbm],
        out_specs=vmem,
        scratch_shapes=[
            SMEM((near_count, leaf_count), jnp.int32),
            VMEM(near_rows.shape, BF),
            VMEM((leaf_count + 2 * HALO, leaf, 128), BF),
            DMA((leaf_count // 4 + 1,)),
        ],
        compiler_params=params(20),
        cost_estimate=cost(35 * 10**8, 9 * 10**5 * 5),
        name="near",
    )(x, one, two, in_hbm(near_rows), in_hbm(near_source.T))

    three, far, near, tables = lax.optimization_barrier((three, far, near, tables))
    hand = pl.pallas_call(
        functools.partial(hand_kernel, leaf_count),
        out_shape=shape((384 + 3 * parent_rows, 128), BF),
        in_specs=[vmem] * 3,
        out_specs=vmem,
        compiler_params=params(8),
        cost_estimate=cost(10**6, 10**6),
        name="hand_over",
    )(three, far, other_ask)
    over = exchange(hand, 0)

    tables = pl.pallas_call(
        functools.partial(second_kernel, leaf_count),
        out_shape=table_shapes,
        in_specs=[vmem] * 5,
        out_specs=(vmem,) * 2,
        input_output_aliases={3: 0, 4: 1},
        compiler_params=params(8),
        cost_estimate=cost(10**6, 10**6),
        name="second_tables",
    )(three, far, ask, *tables)

    product, _, _ = pl.pallas_call(
        down_kernel,
        out_shape=(shape((rhs_count, points), BF),) + table_shapes,
        in_specs=[vmem, hbm] + [vmem] * 8,
        out_specs=(hbm, vmem, vmem),
        input_output_aliases={8: 1, 9: 2},
        scratch_shapes=[
            SMEM((coup_count, leaf_count), jnp.int32),
            VMEM((leaf_count // 4, coup_count * rank, 256), BF),
            VMEM((par_source.shape[1] * rank, 128 * ((parent_count + 1) // 2)), BF),
            VMEM((parent_count, rank, 128), BF),
            VMEM((rank * leaf_count, 128), BF),
            VMEM((rhs_count, points), BF),
            pltpu.SemaphoreType.DMA,
            DMA((parent_count,)),
        ],
        compiler_params=params(12),
        cost_estimate=cost(10**9, 4 * 10**6),
        name="downward",
    )(
        over,
        in_hbm(coup_source.T),
        par_source,
        coup_rows,
        par_rows,
        diag,
        tst,
        near,
        *tables,
    )
    return product.T


def solution(mesh):
    split = ("groups", "leaf")
    return jax.shard_map(
        shards,
        mesh=mesh,
        in_specs=(
            P(split, None),
            P(split, None, None),
            P(split, None, None),
            P(split, None, None),
            P(split, None),
            P(split, None, None),
            P(split, None, None),
            P(split, None),
            P(split, None, None),
            P(split, None),
        ),
        out_specs=P(split, None),
        check_vma=False,
    )
```

```python
import functools

import jax
import jax.numpy as jnp
from jax import lax
from jax.experimental import pallas as pl
from jax.experimental.pallas import tpu as pltpu
from jax.sharding import PartitionSpec as P

HALO = 16
BF = jnp.bfloat16
F32 = jnp.float32
VMEM = pltpu.VMEM
SMEM = pltpu.SMEM
DMA = pltpu.SemaphoreType.DMA


def low_half(rows):
    return lax.broadcasted_iota(jnp.int32, (rows, 128), 1) < 64


def swapped(value):
    return pltpu.roll(value, 64, 1)


def matmul(a, b):
    return jnp.dot(a, b, preferred_element_type=F32)


def matmul_nt(a, b):
    return lax.dot_general(a, b, (((1,), (1,)), ((), ())), preferred_element_type=F32)


def matmul_tn(a, b):
    return lax.dot_general(a, b, (((0,), (0,)), ((), ())), preferred_element_type=F32)


def fill_block_diagonal(basis_ref, diag):
    leaf_count, rank, leaf = basis_ref.shape
    blank = jnp.zeros((rank, leaf), BF)
    empty = jnp.zeros((rank, 2 * leaf), BF)
    for i in range(leaf_count):
        at = 128 * (1 - i % 4 // 2)
        diag[rank * i : rank * (i + 1), at : at + 128] = empty
    for first in range(0, leaf_count, 8):
        tiles = []
        for i in range(first, first + 8):
            block = basis_ref[i]
            tiles.append(jnp.concatenate([blank, block] if i % 2 else [block, blank], 1))
        for i, tile in enumerate(tiles, first):
            at = 128 * (i % 4 // 2)
            diag[rank * i : rank * (i + 1), at : at + 128] = tile


def load_kernel(*refs):
    count = len(refs) // 2
    sems = refs[-1]
    copies = [
        pltpu.make_async_copy(refs[n], refs[count + n], sems.at[n]) for n in range(count)
    ]
    for copy in copies:
        copy.start()
    for copy in copies:
        copy.wait()


def up_kernel(
    x_ref, basis_ref, trans_ref, side, halo_ref, own, tst_ref, diag, flat
):
    points = x_ref.shape[1]
    leaf_count, rank, leaf = basis_ref.shape
    for first in range(0, rank // 4, 4):
        blocks = [
            trans_ref[128 * step : 128 * step + 128, :].astype(F32).T
            for step in range(first, first + 4)
        ]
        for q in range(4):
            pieces = [block if q == 0 else pltpu.roll(block, 128 - 32 * q, 1) for block in blocks]
            for step, piece in enumerate(pieces, first):
                flat[pl.ds(4 * step + q, leaf_count, stride=rank), :] = piece
    tst_ref[...] = flat[:, 0:rank].astype(BF)
    fill_block_diagonal(basis_ref, diag)

    odd = lax.rem(lax.axis_index("leaf"), 2) == 1
    base = HALO * leaf // 128 * 64
    for t in range(HALO * leaf // 128):
        rows = slice(64 * t, 64 * t + 64)
        at = points - HALO * leaf + 128 * t
        head, tail = x_ref[:, 128 * t : 128 * t + 128], x_ref[:, at : at + 128]
        side[rows, :] = jnp.where(odd, head, tail)
        halo_ref[:, 128 * t : 128 * t + 128] = jnp.where(odd, tail, head)

    def put(at, left, right):
        rows = left.shape[0]
        both = jnp.where(low_half(rows), left, right)
        own[at : at + rows, :] = both
        side[base + at : base + at + rows, :] = both

    parent_count = leaf_count // 8
    skels = []
    for quad in range(leaf_count // 4):
        x = x_ref[:, 256 * quad : 256 * quad + 256]
        skels.append(
            matmul_nt(
                diag[128 * quad : 128 * quad + 128, :], jnp.concatenate([x, x], 0)
            ).astype(BF)
        )
    parents = [
        matmul_tn(
            tst_ref[256 * p : 256 * p + 256, :], jnp.concatenate(skels[2 * p : 2 * p + 2], 0)
        ).astype(BF)
        for p in range(parent_count)
    ]
    for quad, skel in enumerate(skels):
        put(64 * quad, skel[:64], skel[64:])
    for m in range((parent_count + 1) // 2):
        put(16 * leaf_count + 32 * m, parents[2 * m], parents[min(2 * m + 1, parent_count - 1)])


def place(r, leaf_count):
    safe = jnp.minimum(r, leaf_count - 1)
    return pl.multiple_of((safe >> 2) * 64 + (safe & 1) * 32, 32), (safe >> 1) & 1


def wanted(requests, reach, up):
    row = requests[pl.ds(jnp.where(up, 3 + reach, 4 - reach), 1), :]
    return [row[0, c] for c in range(8)]


def join_kernel(base, own_ref, one_ref, out_ref):
    size = own_ref.shape[0]
    out_ref[:size, :] = own_ref[...]
    out_ref[size:, :] = one_ref[base:, :]


def near_kernel(
    x_ref,
    one_ref,
    two_ref,
    near_ref,
    source_hbm,
    out_ref,
    source_ref,
    held,
    twice,
    sems,
):
    leaf_count, leaf, depth = near_ref.shape
    count = source_hbm.shape[0]
    quads = leaf_count // 4
    copy_source = pltpu.make_async_copy(source_hbm, source_ref, sems.at[quads])
    copy_source.start()

    def copy(quad):
        part = pl.ds(4 * quad, 4)
        return pltpu.make_async_copy(near_ref.at[part], held.at[part], sems.at[quad])

    for quad in range(quads):
        copy(quad).start()

    low = low_half(leaf)

    def spread(parts):
        others = [swapped(value) for value, _ in parts]
        for (value, at), other in zip(parts, others):
            twice[at] = jnp.where(low, value, other)
            twice[at + 1] = jnp.where(low, other, value)

    odd = lax.rem(lax.axis_index("leaf"), 2) == 1
    after = HALO + leaf_count
    at_one, at_two = jnp.where(odd, 0, after), jnp.where(odd, after, 0)
    halos = range(HALO // 2)
    spread([(one_ref[64 * n : 64 * n + 64, :], at_one + 2 * n) for n in halos])
    spread([(two_ref[:, 128 * n : 128 * n + 128], at_two + 2 * n) for n in halos])
    for first in range(0, leaf_count // 2, 5):
        spread(
            [(x_ref[:, 128 * n : 128 * n + 128], HALO + 2 * n) for n in range(first, first + 5)]
        )
    copy_source.wait()

    def product(i):
        pieces = [
            jnp.where(low, twice[source_ref[2 * m, i]], twice[source_ref[2 * m + 1, i]])
            for m in range(count // 2)
        ]
        if count % 2:
            pieces.append(twice[source_ref[count - 1, i]][:, :leaf])
        return matmul_nt(jnp.concatenate(pieces, 1), held[i])

    def body(step, carry):
        copy(2 * step).wait()
        copy(2 * step + 1).wait()
        parts = [product(8 * step + u) for u in range(8)]
        for t in range(4):
            lanes = pl.ds(pl.multiple_of(512 * step + 128 * t, 128), 128)
            out_ref[:, lanes] = jnp.concatenate(parts[2 * t : 2 * t + 2], 1)
        return carry

    lax.fori_loop(0, quads // 2, body, 0)


def split(value):
    low = low_half(value.shape[0])
    other = swapped(value)
    return jnp.where(low, value, other), jnp.where(low, other, value)


class Tables:
    def __init__(self, leaf_count, slots, window, requests):
        self.leaf_count, self.slots, self.window, self.requests = leaf_count, slots, window, requests
        self.parent_count = leaf_count // 8

    def put_parents(self, ref, at, reach, up):
        block = jnp.where(up, 4 + reach, 4 - reach)
        tiles = range((self.parent_count + 1) // 2)
        values = [ref[at + 32 * m : at + 32 * m + 32, :] for m in tiles]
        for m, (left, right) in zip(tiles, [split(value) for value in values]):
            self.window[self.parent_count * block + 2 * m] = left
            if 2 * m + 1 < self.parent_count:
                self.window[self.parent_count * block + 2 * m + 1] = right

    def put_own(self, ref):
        for first in range(0, self.leaf_count // 4, 5):
            quads = range(first, first + 5)
            values = [ref[64 * quad : 64 * quad + 64, :] for quad in quads]
            for quad, (left, right) in zip(quads, [split(value) for value in values]):
                self.slots[4 * quad] = left[:32]
                self.slots[4 * quad + 1] = left[32:]
                self.slots[4 * quad + 2] = right[:32]
                self.slots[4 * quad + 3] = right[32:]
        self.put_parents(ref, 16 * self.leaf_count, 0, False)

    def put_reply(self, ref, at, reach, up):
        k = jnp.where(up, 3 + reach, 4 - reach)
        values = [ref[at + 32 * m : at + 32 * m + 32, :] for m in range(4)]
        for m, (left, right) in enumerate([split(value) for value in values]):
            self.slots[self.leaf_count + 8 * k + 2 * m] = left
            self.slots[self.leaf_count + 8 * k + 2 * m + 1] = right

    def look_up(self, ref, at, reach, up):
        k = jnp.where(up, 3 + reach, 4 - reach)
        low = low_half(32)
        asked = wanted(self.requests, reach, up)
        places = [place(r, self.leaf_count) for r in asked]
        values = [ref[pl.ds(at + row, 32), :] for row, _ in places]
        others = [swapped(value) for value in values]
        for c, r in enumerate(asked):
            value = jnp.where(low == (places[c][1] == 0), values[c], others[c])
            self.slots[self.leaf_count + 8 * k + c] = jnp.where(
                r < self.leaf_count, value, jnp.zeros_like(value)
            )


def is_odd():
    return lax.rem(lax.axis_index("leaf"), 2) == 1


def first_kernel(leaf_count, base, own_ref, one_ref, requests, slots, window):
    tables = Tables(leaf_count, slots, window, requests)
    inward = jnp.logical_not(is_odd())
    tables.look_up(one_ref, base, 1, inward)
    tables.put_parents(one_ref, base + 16 * leaf_count, 1, inward)
    tables.put_own(own_ref)


def hand_kernel(leaf_count, three_ref, far_ref, requests, out_ref):
    outward = jnp.logical_not(is_odd())
    low = low_half(32)
    size = far_ref.shape[0] // 2
    parents = 16 * leaf_count
    places = (
        (three_ref, size, 1, outward),
        (three_ref, 0, 2, outward),
        (far_ref, 0, 4, is_odd()),
    )
    for n, (ref, at, reach, up) in enumerate(places):
        asked = wanted(requests, reach, up)
        values = []
        for c, r in enumerate(asked):
            row, high = place(r, leaf_count)
            value = ref[pl.ds(at + row, 32), :]
            value = jnp.where(high != c % 2, swapped(value), value)
            values.append(jnp.where(r < leaf_count, value, jnp.zeros_like(value)))
        for m in range(4):
            row = 128 * n + 32 * m
            out_ref[row : row + 32, :] = jnp.where(low, values[2 * m], values[2 * m + 1])
        rows = 384 + (size - parents) * n
        out_ref[rows : rows + size - parents, :] = ref[at + parents : at + size, :]


def second_kernel(leaf_count, three_ref, far_ref, requests, slots_in, window_in, slots, window):
    tables = Tables(leaf_count, slots, window, requests)
    odd = is_odd()
    size = far_ref.shape[0] // 2
    for ref, at, reach, up in (
        (three_ref, size, 2, jnp.logical_not(odd)),
        (three_ref, 0, 3, jnp.logical_not(odd)),
        (far_ref, 0, 3, odd),
        (far_ref, size, 4, odd),
    ):
        tables.look_up(ref, at, reach, up)
        tables.put_parents(ref, at + 16 * leaf_count, reach, up)


def down_kernel(
    over_ref,
    coup_hbm,
    par_hbm,
    coup_ref,
    par_ref,
    diag,
    tst_ref,
    near_ref,
    slots_in,
    window_in,
    out_hbm,
    slots,
    window,
    coup_source,
    par_source,
    weights,
    stack,
    outs,
    leaf_outs,
    out_ref,
    sems,
    out_sem,
):
    copies = [
        pltpu.make_async_copy(source, held, sems.at[n])
        for n, (source, held) in enumerate(((par_hbm, par_source), (coup_hbm, coup_source)))
    ]
    for copy in copies:
        copy.start()
    leaf_count, rank = coup_ref.shape[:2]
    parent_count = par_ref.shape[0]
    low64 = low_half(64)
    low = low_half(rank)
    tables = Tables(leaf_count, slots, window, None)
    odd = is_odd()
    parent_size = (over_ref.shape[0] - 384) // 3
    for n, (reach, up) in enumerate(((1, odd), (2, odd), (4, jnp.logical_not(odd)))):
        tables.put_reply(over_ref, 128 * n, reach, up)
        tables.put_parents(over_ref, 384 + parent_size * n, reach, up)
    for copy in copies:
        copy.wait()
    per = par_source.shape[1]
    coup = coup_source.shape[0]
    pairs = [(2 * m, min(2 * m + 1, parent_count - 1)) for m in range((parent_count + 1) // 2)]
    for first in range(0, per, 4):
        loaded = [
            [(window[par_source[p, j]], window[par_source[q, j]]) for p, q in pairs]
            for j in range(first, first + 4)
        ]
        for j, tiles in enumerate(loaded, first):
            for m, (left, right) in enumerate(tiles):
                stack[rank * j : rank * j + rank, 128 * m : 128 * m + 128] = jnp.where(
                    low, left, right
                )
    rows = par_ref[...].reshape(parent_count * rank, per * rank)
    parent_outs = matmul(rows, stack[...]).astype(BF)
    for p in range(parent_count):
        tile = parent_outs[rank * p : rank * p + rank, 128 * (p // 2) : 128 * (p // 2) + 128]
        outs[p] = split(tile)[p % 2]

    def build(quad):
        for first in range(0, coup, 4):
            loaded = [
                [
                    (slots[coup_source[j, 4 * quad + t]], slots[coup_source[j, 4 * quad + t + 1]])
                    for t in (0, 2)
                ]
                for j in range(first, first + 4)
            ]
            for j, tiles in enumerate(loaded, first):
                for t, (left, right) in enumerate(tiles):
                    weights[quad, rank * j : rank * j + rank, 128 * t : 128 * t + 128] = jnp.where(
                        low, left, right
                    )

    def couple(p):
        down = matmul(tst_ref[pl.ds(pl.multiple_of(256 * p, 256), 256), :], outs[p])
        results = []
        for half in range(2):
            rows = coup_ref[pl.ds(8 * p + 4 * half, 4)].reshape(4 * rank, coup * rank)
            coupled = matmul(rows, weights[2 * p + half])
            coupled = jnp.concatenate([coupled[:64, :128], coupled[64:, 128:]], 0)
            results.append((coupled + down[128 * half : 128 * half + 128]).astype(BF))
        return jnp.concatenate(results, 0)

    def finish(p):
        tiles = []
        for half in range(2):
            rows = pl.ds(pl.multiple_of(256 * p + 128 * half, 128), 128)
            far = matmul_tn(leaf_outs[rows, :], diag[rows, :])
            for t in range(2):
                lanes = pl.ds(pl.multiple_of(512 * p + 256 * half + 128 * t, 128), 128)
                tile = jnp.where(
                    low64, far[:64, 128 * t : 128 * t + 128], far[64:, 128 * t : 128 * t + 128]
                )
                tiles.append((lanes, (near_ref[:, lanes] + tile).astype(BF)))
        return tiles

    def body(p, carry):
        tiles = finish(jnp.clip(p - 1, 0, parent_count - 1))
        now = jnp.clip(p, 0, parent_count - 1)
        leaf_out = couple(now)
        later = jnp.clip(p + 1, 0, parent_count - 1)
        build(2 * later)
        build(2 * later + 1)
        for lanes, tile in tiles:
            out_ref[:, lanes] = tile
        leaf_outs[pl.ds(pl.multiple_of(256 * now, 256), 256), :] = leaf_out
        return carry

    lax.fori_loop(-1, parent_count + 1, body, 0)
    copy = pltpu.make_async_copy(out_ref, out_hbm, out_sem)
    copy.start()
    copy.wait()


def in_hbm(array):
    return pltpu.with_memory_space_constraint(array, pltpu.HBM)


def params(mib):
    return pltpu.CompilerParams(vmem_limit_bytes=mib << 20)


def cost(flops, size):
    return pl.CostEstimate(flops=flops, bytes_accessed=size, transcendentals=0)


def shards(
    rhs,
    basis,
    transfer,
    near_rows,
    near_source,
    far_request,
    coup_rows,
    coup_source,
    par_rows,
    par_source,
):
    leaf_count, leaf, rank = basis.shape
    points, rhs_count = rhs.shape
    parent_count = par_rows.shape[0]
    near_count = near_source.shape[1]
    coup_count = coup_source.shape[1]
    base = HALO // 2 * rhs_count
    parent_rows = rank * ((parent_count + 1) // 2)
    packed = base + 16 * leaf_count + parent_rows
    count = lax.axis_size("leaf")

    x = rhs.T
    trans = transfer.transpose(1, 2, 0).reshape(rank * rank, leaf_count)
    shape = jax.ShapeDtypeStruct
    vmem, hbm = (pl.BlockSpec(memory_space=kind) for kind in (VMEM, pltpu.HBM))
    basis_t = basis.transpose(0, 2, 1)
    inputs = (x, basis_t, trans, far_request[0])
    x, basis_t, trans, ask = pl.pallas_call(
        load_kernel,
        out_shape=tuple(shape(held.shape, held.dtype) for held in inputs),
        in_specs=[hbm] * 4,
        out_specs=(vmem,) * 4,
        scratch_shapes=[DMA((4,))],
        compiler_params=params(8),
        cost_estimate=cost(10**6, 2 * 10**6),
        name="load",
    )(*(in_hbm(held) for held in inputs))

    def exchange(block, begin, distance=1):
        pairs = [(i, i + distance) for i in range(begin, count - distance, 2)]
        return lax.ppermute(block, "leaf", pairs + [(b, a) for a, b in pairs])

    other_ask = exchange(far_request[0], 0)
    side, halo, own, tst, diag = pl.pallas_call(
        up_kernel,
        out_shape=(
            shape((packed, 128), BF),
            shape((rhs_count, HALO * leaf), BF),
            shape((packed - base, 128), BF),
            shape((rank * leaf_count, rank), BF),
            shape((rank * leaf_count, 256), BF),
        ),
        in_specs=[vmem] * 3,
        out_specs=(vmem,) * 5,
        scratch_shapes=[VMEM((rank * leaf_count, 128), F32)],
        compiler_params=params(8),
        cost_estimate=cost(10**9, 2 * 10**6),
        name="upward",
    )(x, basis_t, trans)
    one = exchange(side, 0)
    two = exchange(halo, 1)
    both = pl.pallas_call(
        functools.partial(join_kernel, base),
        out_shape=shape((2 * (packed - base), 128), BF),
        in_specs=[vmem] * 2,
        out_specs=vmem,
        compiler_params=params(8),
        cost_estimate=cost(10**6, 10**6),
        name="join",
    )(own, one)
    far = exchange(both, 1, 3)
    three = exchange(both, 0, 3)
    table_shapes = (
        shape((leaf_count + 64, rank, 128), BF),
        shape((9 * parent_count, rank, 128), BF),
    )
    tables = pl.pallas_call(
        functools.partial(first_kernel, leaf_count, base),
        out_shape=table_shapes,
        in_specs=[vmem] * 3,
        out_specs=(vmem,) * 2,
        compiler_params=params(8),
        cost_estimate=cost(10**6, 10**6),
        name="first_tables",
    )(own, one, ask)
    near = pl.pallas_call(
        near_kernel,
        out_shape=shape((rhs_count, points), F32),
        in_specs=[vmem, vmem, vmem, hbm, hbm],
        out_specs=vmem,
        scratch_shapes=[
            SMEM((near_count, leaf_count), jnp.int32),
            VMEM(near_rows.shape, BF),
            VMEM((leaf_count + 2 * HALO, leaf, 128), BF),
            DMA((leaf_count // 4 + 1,)),
        ],
        compiler_params=params(20),
        cost_estimate=cost(35 * 10**8, 9 * 10**5 * 5),
        name="near",
    )(x, one, two, in_hbm(near_rows), in_hbm(near_source.T))

    three, far, near, tables = lax.optimization_barrier((three, far, near, tables))
    hand = pl.pallas_call(
        functools.partial(hand_kernel, leaf_count),
        out_shape=shape((384 + 3 * parent_rows, 128), BF),
        in_specs=[vmem] * 3,
        out_specs=vmem,
        compiler_params=params(8),
        cost_estimate=cost(10**6, 10**6),
        name="hand_over",
    )(three, far, other_ask)
    over = exchange(hand, 0)

    tables = pl.pallas_call(
        functools.partial(second_kernel, leaf_count),
        out_shape=table_shapes,
        in_specs=[vmem] * 5,
        out_specs=(vmem,) * 2,
        input_output_aliases={3: 0, 4: 1},
        compiler_params=params(8),
        cost_estimate=cost(10**6, 10**6),
        name="second_tables",
    )(three, far, ask, *tables)

    product, _, _ = pl.pallas_call(
        down_kernel,
        out_shape=(shape((rhs_count, points), BF),) + table_shapes,
        in_specs=[vmem] + [hbm] * 2 + [vmem] * 7,
        out_specs=(hbm, vmem, vmem),
        input_output_aliases={8: 1, 9: 2},
        scratch_shapes=[
            SMEM((coup_count, leaf_count), jnp.int32),
            SMEM(par_source.shape, jnp.int32),
            VMEM((leaf_count // 4, coup_count * rank, 256), BF),
            VMEM((par_source.shape[1] * rank, 128 * ((parent_count + 1) // 2)), BF),
            VMEM((parent_count, rank, 128), BF),
            VMEM((rank * leaf_count, 128), BF),
            VMEM((rhs_count, points), BF),
            DMA((2,)),
            pltpu.SemaphoreType.DMA,
        ],
        compiler_params=params(12),
        cost_estimate=cost(10**9, 4 * 10**6),
        name="downward",
    )(
        over,
        in_hbm(coup_source.T),
        in_hbm(par_source),
        coup_rows,
        par_rows,
        diag,
        tst,
        near,
        *tables,
    )
    return product.T


def solution(mesh):
    split = ("groups", "leaf")
    return jax.shard_map(
        shards,
        mesh=mesh,
        in_specs=(
            P(split, None),
            P(split, None, None),
            P(split, None, None),
            P(split, None, None),
            P(split, None),
            P(split, None, None),
            P(split, None, None),
            P(split, None),
            P(split, None, None),
            P(split, None),
        ),
        out_specs=P(split, None),
        check_vma=False,
    )
```

```python
import functools

import jax
import jax.numpy as jnp
from jax import lax
from jax.experimental import pallas as pl
from jax.experimental.pallas import tpu as pltpu
from jax.sharding import PartitionSpec as P

HALO = 16
BF = jnp.bfloat16
F32 = jnp.float32
VMEM = pltpu.VMEM
SMEM = pltpu.SMEM
DMA = pltpu.SemaphoreType.DMA


def low_half(rows):
    return lax.broadcasted_iota(jnp.int32, (rows, 128), 1) < 64


def swapped(value):
    return pltpu.roll(value, 64, 1)


def matmul(a, b):
    return jnp.dot(a, b, preferred_element_type=F32)


def matmul_nt(a, b):
    return lax.dot_general(a, b, (((1,), (1,)), ((), ())), preferred_element_type=F32)


def matmul_tn(a, b):
    return lax.dot_general(a, b, (((0,), (0,)), ((), ())), preferred_element_type=F32)


def fill_block_diagonal(basis_ref, diag):
    leaf_count, rank, leaf = basis_ref.shape
    blank = jnp.zeros((rank, leaf), BF)
    empty = jnp.zeros((rank, 2 * leaf), BF)
    for i in range(leaf_count):
        at = 128 * (1 - i % 4 // 2)
        diag[rank * i : rank * (i + 1), at : at + 128] = empty
    for first in range(0, leaf_count, 8):
        tiles = []
        for i in range(first, first + 8):
            block = basis_ref[i]
            tiles.append(jnp.concatenate([blank, block] if i % 2 else [block, blank], 1))
        for i, tile in enumerate(tiles, first):
            at = 128 * (i % 4 // 2)
            diag[rank * i : rank * (i + 1), at : at + 128] = tile


def load_kernel(*refs):
    count = len(refs) // 2
    sems = refs[-1]
    copies = [
        pltpu.make_async_copy(refs[n], refs[count + n], sems.at[n]) for n in range(count)
    ]
    for copy in copies:
        copy.start()
    for copy in copies:
        copy.wait()


def up_kernel(
    x_ref, basis_ref, trans_ref, side, halo_ref, own, tst_ref, diag, flat
):
    points = x_ref.shape[1]
    leaf_count, rank, leaf = basis_ref.shape
    for first in range(0, rank // 4, 4):
        blocks = [
            trans_ref[128 * step : 128 * step + 128, :].astype(F32).T
            for step in range(first, first + 4)
        ]
        for q in range(4):
            pieces = [block if q == 0 else pltpu.roll(block, 128 - 32 * q, 1) for block in blocks]
            for step, piece in enumerate(pieces, first):
                flat[pl.ds(4 * step + q, leaf_count, stride=rank), :] = piece
    tst_ref[...] = flat[:, 0:rank].astype(BF)
    fill_block_diagonal(basis_ref, diag)

    odd = lax.rem(lax.axis_index("leaf"), 2) == 1
    base = HALO * leaf // 128 * 64
    for t in range(HALO * leaf // 128):
        rows = slice(64 * t, 64 * t + 64)
        at = points - HALO * leaf + 128 * t
        head, tail = x_ref[:, 128 * t : 128 * t + 128], x_ref[:, at : at + 128]
        side[rows, :] = jnp.where(odd, head, tail)
        halo_ref[:, 128 * t : 128 * t + 128] = jnp.where(odd, tail, head)

    def put(at, left, right):
        rows = left.shape[0]
        both = jnp.where(low_half(rows), left, right)
        own[at : at + rows, :] = both
        side[base + at : base + at + rows, :] = both

    parent_count = leaf_count // 8
    skels = []
    for quad in range(leaf_count // 4):
        x = x_ref[:, 256 * quad : 256 * quad + 256]
        skels.append(
            matmul_nt(
                diag[128 * quad : 128 * quad + 128, :], jnp.concatenate([x, x], 0)
            ).astype(BF)
        )
    parents = [
        matmul_tn(
            tst_ref[256 * p : 256 * p + 256, :], jnp.concatenate(skels[2 * p : 2 * p + 2], 0)
        ).astype(BF)
        for p in range(parent_count)
    ]
    for quad, skel in enumerate(skels):
        put(64 * quad, skel[:64], skel[64:])
    for m in range((parent_count + 1) // 2):
        put(16 * leaf_count + 32 * m, parents[2 * m], parents[min(2 * m + 1, parent_count - 1)])


def place(r, leaf_count):
    safe = jnp.minimum(r, leaf_count - 1)
    return pl.multiple_of((safe >> 2) * 64 + (safe & 1) * 32, 32), (safe >> 1) & 1


def wanted(requests, reach, up):
    row = requests[pl.ds(jnp.where(up, 3 + reach, 4 - reach), 1), :]
    return [row[0, c] for c in range(8)]


def join_kernel(base, own_ref, one_ref, out_ref):
    size = own_ref.shape[0]
    out_ref[:size, :] = own_ref[...]
    out_ref[size:, :] = one_ref[base:, :]


def near_kernel(
    x_ref,
    one_ref,
    two_ref,
    near_ref,
    source_hbm,
    out_ref,
    source_ref,
    held,
    twice,
    sems,
):
    leaf_count, leaf, depth = near_ref.shape
    count = source_hbm.shape[0]
    quads = leaf_count // 4
    copy_source = pltpu.make_async_copy(source_hbm, source_ref, sems.at[quads])
    copy_source.start()

    def copy(quad):
        part = pl.ds(4 * quad, 4)
        return pltpu.make_async_copy(near_ref.at[part], held.at[part], sems.at[quad])

    for quad in range(quads):
        copy(quad).start()

    low = low_half(leaf)

    def spread(parts):
        others = [swapped(value) for value, _ in parts]
        for (value, at), other in zip(parts, others):
            twice[at] = jnp.where(low, value, other)
            twice[at + 1] = jnp.where(low, other, value)

    odd = lax.rem(lax.axis_index("leaf"), 2) == 1
    after = HALO + leaf_count
    at_one, at_two = jnp.where(odd, 0, after), jnp.where(odd, after, 0)
    halos = range(HALO // 2)
    spread([(one_ref[64 * n : 64 * n + 64, :], at_one + 2 * n) for n in halos])
    spread([(two_ref[:, 128 * n : 128 * n + 128], at_two + 2 * n) for n in halos])
    for first in range(0, leaf_count // 2, 5):
        spread(
            [(x_ref[:, 128 * n : 128 * n + 128], HALO + 2 * n) for n in range(first, first + 5)]
        )
    copy_source.wait()

    def product(i):
        pieces = [
            jnp.where(low, twice[source_ref[2 * m, i]], twice[source_ref[2 * m + 1, i]])
            for m in range(count // 2)
        ]
        if count % 2:
            pieces.append(twice[source_ref[count - 1, i]][:, :leaf])
        return matmul_nt(jnp.concatenate(pieces, 1), held[i])

    def body(step, carry):
        copy(2 * step).wait()
        copy(2 * step + 1).wait()
        parts = [product(8 * step + u) for u in range(8)]
        for t in range(4):
            lanes = pl.ds(pl.multiple_of(512 * step + 128 * t, 128), 128)
            out_ref[:, lanes] = jnp.concatenate(parts[2 * t : 2 * t + 2], 1)
        return carry

    lax.fori_loop(0, quads // 2, body, 0)


def split(value):
    low = low_half(value.shape[0])
    other = swapped(value)
    return jnp.where(low, value, other), jnp.where(low, other, value)


class Tables:
    def __init__(self, leaf_count, slots, window, requests):
        self.leaf_count, self.slots, self.window, self.requests = leaf_count, slots, window, requests
        self.parent_count = leaf_count // 8

    def put_parents(self, ref, at, reach, up):
        block = jnp.where(up, 4 + reach, 4 - reach)
        tiles = range((self.parent_count + 1) // 2)
        values = [ref[at + 32 * m : at + 32 * m + 32, :] for m in tiles]
        for m, (left, right) in zip(tiles, [split(value) for value in values]):
            self.window[self.parent_count * block + 2 * m] = left
            if 2 * m + 1 < self.parent_count:
                self.window[self.parent_count * block + 2 * m + 1] = right

    def put_own(self, ref):
        for first in range(0, self.leaf_count // 4, 5):
            quads = range(first, first + 5)
            values = [ref[64 * quad : 64 * quad + 64, :] for quad in quads]
            for quad, (left, right) in zip(quads, [split(value) for value in values]):
                self.slots[4 * quad] = left[:32]
                self.slots[4 * quad + 1] = left[32:]
                self.slots[4 * quad + 2] = right[:32]
                self.slots[4 * quad + 3] = right[32:]
        self.put_parents(ref, 16 * self.leaf_count, 0, False)

    def put_reply(self, ref, at, reach, up):
        k = jnp.where(up, 3 + reach, 4 - reach)
        values = [ref[at + 32 * m : at + 32 * m + 32, :] for m in range(4)]
        for m, (left, right) in enumerate([split(value) for value in values]):
            self.slots[self.leaf_count + 8 * k + 2 * m] = left
            self.slots[self.leaf_count + 8 * k + 2 * m + 1] = right

    def look_up(self, ref, at, reach, up):
        k = jnp.where(up, 3 + reach, 4 - reach)
        low = low_half(32)
        asked = wanted(self.requests, reach, up)
        places = [place(r, self.leaf_count) for r in asked]
        values = [ref[pl.ds(at + row, 32), :] for row, _ in places]
        others = [swapped(value) for value in values]
        for c, r in enumerate(asked):
            value = jnp.where(low == (places[c][1] == 0), values[c], others[c])
            self.slots[self.leaf_count + 8 * k + c] = jnp.where(
                r < self.leaf_count, value, jnp.zeros_like(value)
            )


def is_odd():
    return lax.rem(lax.axis_index("leaf"), 2) == 1


def first_kernel(leaf_count, base, own_ref, one_ref, requests, slots, window):
    tables = Tables(leaf_count, slots, window, requests)
    inward = jnp.logical_not(is_odd())
    tables.look_up(one_ref, base, 1, inward)
    tables.put_parents(one_ref, base + 16 * leaf_count, 1, inward)
    tables.put_own(own_ref)


def hand_kernel(leaf_count, three_ref, far_ref, requests, out_ref):
    outward = jnp.logical_not(is_odd())
    low = low_half(32)
    size = far_ref.shape[0] // 2
    parents = 16 * leaf_count
    places = (
        (three_ref, size, 1, outward),
        (three_ref, 0, 2, outward),
        (far_ref, 0, 4, is_odd()),
    )
    for n, (ref, at, reach, up) in enumerate(places):
        asked = wanted(requests, reach, up)
        values = []
        for c, r in enumerate(asked):
            row, high = place(r, leaf_count)
            value = ref[pl.ds(at + row, 32), :]
            value = jnp.where(high != c % 2, swapped(value), value)
            values.append(jnp.where(r < leaf_count, value, jnp.zeros_like(value)))
        for m in range(4):
            row = 128 * n + 32 * m
            out_ref[row : row + 32, :] = jnp.where(low, values[2 * m], values[2 * m + 1])
        rows = 384 + (size - parents) * n
        out_ref[rows : rows + size - parents, :] = ref[at + parents : at + size, :]


def second_kernel(leaf_count, three_ref, far_ref, requests, slots_in, window_in, slots, window):
    tables = Tables(leaf_count, slots, window, requests)
    odd = is_odd()
    size = far_ref.shape[0] // 2
    for ref, at, reach, up in (
        (three_ref, size, 2, jnp.logical_not(odd)),
        (three_ref, 0, 3, jnp.logical_not(odd)),
        (far_ref, 0, 3, odd),
        (far_ref, size, 4, odd),
    ):
        tables.look_up(ref, at, reach, up)
        tables.put_parents(ref, at + 16 * leaf_count, reach, up)


def down_kernel(
    over_ref,
    coup_hbm,
    par_hbm,
    coup_ref,
    par_ref,
    diag,
    tst_ref,
    near_ref,
    slots_in,
    window_in,
    out_hbm,
    slots,
    window,
    coup_source,
    par_source,
    stack,
    outs,
    leaf_outs,
    out_ref,
    sems,
    out_sems,
):
    copies = [
        pltpu.make_async_copy(source, held, sems.at[n])
        for n, (source, held) in enumerate(((par_hbm, par_source), (coup_hbm, coup_source)))
    ]
    for copy in copies:
        copy.start()
    leaf_count, rank = coup_ref.shape[:2]
    parent_count = par_ref.shape[0]
    low64 = low_half(64)
    low = low_half(rank)
    tables = Tables(leaf_count, slots, window, None)
    odd = is_odd()
    parent_size = (over_ref.shape[0] - 384) // 3
    for n, (reach, up) in enumerate(((1, odd), (2, odd), (4, jnp.logical_not(odd)))):
        tables.put_reply(over_ref, 128 * n, reach, up)
        tables.put_parents(over_ref, 384 + parent_size * n, reach, up)
    for copy in copies:
        copy.wait()
    per = par_source.shape[1]
    coup = coup_source.shape[0]
    pairs = [(2 * m, min(2 * m + 1, parent_count - 1)) for m in range((parent_count + 1) // 2)]
    for first in range(0, per, 4):
        loaded = [
            [(window[par_source[p, j]], window[par_source[q, j]]) for p, q in pairs]
            for j in range(first, first + 4)
        ]
        for j, tiles in enumerate(loaded, first):
            for m, (left, right) in enumerate(tiles):
                stack[rank * j : rank * j + rank, 128 * m : 128 * m + 128] = jnp.where(
                    low, left, right
                )
    rows = par_ref[...].reshape(parent_count * rank, per * rank)
    parent_outs = matmul(rows, stack[...]).astype(BF)
    for p in range(parent_count):
        tile = parent_outs[rank * p : rank * p + rank, 128 * (p // 2) : 128 * (p // 2) + 128]
        outs[p] = split(tile)[p % 2]

    def couple(i):
        pieces = [
            jnp.where(low, slots[coup_source[j, i]], slots[coup_source[j, i + 1]])
            for j in range(coup)
        ]
        rows = coup_ref[i : i + 2].reshape(2 * rank, coup * rank)
        return matmul(rows, jnp.concatenate(pieces, 0))

    quads = leaf_count // 4
    downs = [
        matmul(tst_ref[256 * p : 256 * p + 256, :], outs[p]) for p in range(parent_count)
    ]
    for quad in range(quads):
        coupled = jnp.concatenate([couple(4 * quad), couple(4 * quad + 2)], 0)
        down = downs[quad // 2][128 * (quad % 2) : 128 * (quad % 2) + 128]
        leaf_outs[128 * quad : 128 * quad + 128, :] = (coupled + down).astype(BF)

    def send(p):
        part = pl.ds(512 * p, 512)
        return pltpu.make_async_copy(out_ref.at[:, part], out_hbm.at[:, part], out_sems.at[p])

    for first in range(0, quads, 2):
        tiles = []
        for quad in range(first, first + 2):
            rows = slice(128 * quad, 128 * quad + 128)
            far = matmul_tn(leaf_outs[rows, :], diag[rows, :])
            for t in range(2):
                lanes = slice(256 * quad + 128 * t, 256 * quad + 128 * t + 128)
                tile = jnp.where(
                    low64, far[:64, 128 * t : 128 * t + 128], far[64:, 128 * t : 128 * t + 128]
                )
                tiles.append((lanes, (near_ref[:, lanes] + tile).astype(BF)))
        for lanes, tile in tiles:
            out_ref[:, lanes] = tile
        send(first // 2).start()
    for p in range(parent_count):
        send(p).wait()


def in_hbm(array):
    return pltpu.with_memory_space_constraint(array, pltpu.HBM)


def params(mib):
    return pltpu.CompilerParams(vmem_limit_bytes=mib << 20)


def cost(flops, size):
    return pl.CostEstimate(flops=flops, bytes_accessed=size, transcendentals=0)


def shards(
    rhs,
    basis,
    transfer,
    near_rows,
    near_source,
    far_request,
    coup_rows,
    coup_source,
    par_rows,
    par_source,
):
    leaf_count, leaf, rank = basis.shape
    points, rhs_count = rhs.shape
    parent_count = par_rows.shape[0]
    near_count = near_source.shape[1]
    coup_count = coup_source.shape[1]
    base = HALO // 2 * rhs_count
    parent_rows = rank * ((parent_count + 1) // 2)
    packed = base + 16 * leaf_count + parent_rows
    count = lax.axis_size("leaf")

    x = rhs.T
    trans = transfer.transpose(1, 2, 0).reshape(rank * rank, leaf_count)
    shape = jax.ShapeDtypeStruct
    vmem, hbm = (pl.BlockSpec(memory_space=kind) for kind in (VMEM, pltpu.HBM))
    basis_t = basis.transpose(0, 2, 1)
    inputs = (x, basis_t, trans, far_request[0])
    x, basis_t, trans, ask = pl.pallas_call(
        load_kernel,
        out_shape=tuple(shape(held.shape, held.dtype) for held in inputs),
        in_specs=[hbm] * 4,
        out_specs=(vmem,) * 4,
        scratch_shapes=[DMA((4,))],
        compiler_params=params(8),
        cost_estimate=cost(10**6, 2 * 10**6),
        name="load",
    )(*(in_hbm(held) for held in inputs))

    def exchange(block, begin, distance=1):
        pairs = [(i, i + distance) for i in range(begin, count - distance, 2)]
        return lax.ppermute(block, "leaf", pairs + [(b, a) for a, b in pairs])

    other_ask = exchange(far_request[0], 0)
    side, halo, own, tst, diag = pl.pallas_call(
        up_kernel,
        out_shape=(
            shape((packed, 128), BF),
            shape((rhs_count, HALO * leaf), BF),
            shape((packed - base, 128), BF),
            shape((rank * leaf_count, rank), BF),
            shape((rank * leaf_count, 256), BF),
        ),
        in_specs=[vmem] * 3,
        out_specs=(vmem,) * 5,
        scratch_shapes=[VMEM((rank * leaf_count, 128), F32)],
        compiler_params=params(8),
        cost_estimate=cost(10**9, 2 * 10**6),
        name="upward",
    )(x, basis_t, trans)
    one = exchange(side, 0)
    two = exchange(halo, 1)
    both = pl.pallas_call(
        functools.partial(join_kernel, base),
        out_shape=shape((2 * (packed - base), 128), BF),
        in_specs=[vmem] * 2,
        out_specs=vmem,
        compiler_params=params(8),
        cost_estimate=cost(10**6, 10**6),
        name="join",
    )(own, one)
    far = exchange(both, 1, 3)
    three = exchange(both, 0, 3)
    table_shapes = (
        shape((leaf_count + 64, rank, 128), BF),
        shape((9 * parent_count, rank, 128), BF),
    )
    tables = pl.pallas_call(
        functools.partial(first_kernel, leaf_count, base),
        out_shape=table_shapes,
        in_specs=[vmem] * 3,
        out_specs=(vmem,) * 2,
        compiler_params=params(8),
        cost_estimate=cost(10**6, 10**6),
        name="first_tables",
    )(own, one, ask)
    near = pl.pallas_call(
        near_kernel,
        out_shape=shape((rhs_count, points), F32),
        in_specs=[vmem, vmem, vmem, hbm, hbm],
        out_specs=vmem,
        scratch_shapes=[
            SMEM((near_count, leaf_count), jnp.int32),
            VMEM(near_rows.shape, BF),
            VMEM((leaf_count + 2 * HALO, leaf, 128), BF),
            DMA((leaf_count // 4 + 1,)),
        ],
        compiler_params=params(20),
        cost_estimate=cost(35 * 10**8, 9 * 10**5 * 5),
        name="near",
    )(x, one, two, in_hbm(near_rows), in_hbm(near_source.T))

    three, far, near, tables = lax.optimization_barrier((three, far, near, tables))
    hand = pl.pallas_call(
        functools.partial(hand_kernel, leaf_count),
        out_shape=shape((384 + 3 * parent_rows, 128), BF),
        in_specs=[vmem] * 3,
        out_specs=vmem,
        compiler_params=params(8),
        cost_estimate=cost(10**6, 10**6),
        name="hand_over",
    )(three, far, other_ask)
    over = exchange(hand, 0)

    tables = pl.pallas_call(
        functools.partial(second_kernel, leaf_count),
        out_shape=table_shapes,
        in_specs=[vmem] * 5,
        out_specs=(vmem,) * 2,
        input_output_aliases={3: 0, 4: 1},
        compiler_params=params(8),
        cost_estimate=cost(10**6, 10**6),
        name="second_tables",
    )(three, far, ask, *tables)

    product, _, _ = pl.pallas_call(
        down_kernel,
        out_shape=(shape((rhs_count, points), BF),) + table_shapes,
        in_specs=[vmem] + [hbm] * 2 + [vmem] * 7,
        out_specs=(hbm, vmem, vmem),
        input_output_aliases={8: 1, 9: 2},
        scratch_shapes=[
            SMEM((coup_count, leaf_count), jnp.int32),
            SMEM(par_source.shape, jnp.int32),
            VMEM((par_source.shape[1] * rank, 128 * ((parent_count + 1) // 2)), BF),
            VMEM((parent_count, rank, 128), BF),
            VMEM((rank * leaf_count, 128), BF),
            VMEM((rhs_count, points), BF),
            DMA((2,)),
            DMA((parent_count,)),
        ],
        compiler_params=params(12),
        cost_estimate=cost(10**9, 4 * 10**6),
        name="downward",
    )(
        over,
        in_hbm(coup_source.T),
        in_hbm(par_source),
        coup_rows,
        par_rows,
        diag,
        tst,
        near,
        *tables,
    )
    return product.T


def solution(mesh):
    split = ("groups", "leaf")
    return jax.shard_map(
        shards,
        mesh=mesh,
        in_specs=(
            P(split, None),
            P(split, None, None),
            P(split, None, None),
            P(split, None, None),
            P(split, None),
            P(split, None, None),
            P(split, None, None),
            P(split, None),
            P(split, None, None),
            P(split, None),
        ),
        out_specs=P(split, None),
        check_vma=False,
    )
```

```python
import functools

import jax
import jax.numpy as jnp
from jax import lax
from jax.experimental import pallas as pl
from jax.experimental.pallas import tpu as pltpu
from jax.sharding import PartitionSpec as P

HALO = 16
BF = jnp.bfloat16
F32 = jnp.float32
VMEM = pltpu.VMEM
SMEM = pltpu.SMEM
DMA = pltpu.SemaphoreType.DMA


def low_half(rows):
    return lax.broadcasted_iota(jnp.int32, (rows, 128), 1) < 64


def swapped(value):
    return pltpu.roll(value, 64, 1)


def matmul(a, b):
    return jnp.dot(a, b, preferred_element_type=F32)


def matmul_nt(a, b):
    return lax.dot_general(a, b, (((1,), (1,)), ((), ())), preferred_element_type=F32)


def matmul_tn(a, b):
    return lax.dot_general(a, b, (((0,), (0,)), ((), ())), preferred_element_type=F32)


def fill_block_diagonal(basis_ref, diag):
    leaf_count, rank, leaf = basis_ref.shape
    blank = jnp.zeros((rank, leaf), BF)
    empty = jnp.zeros((rank, 2 * leaf), BF)
    for i in range(leaf_count):
        at = 128 * (1 - i % 4 // 2)
        diag[rank * i : rank * (i + 1), at : at + 128] = empty
    for first in range(0, leaf_count, 8):
        tiles = []
        for i in range(first, first + 8):
            block = basis_ref[i]
            tiles.append(jnp.concatenate([blank, block] if i % 2 else [block, blank], 1))
        for i, tile in enumerate(tiles, first):
            at = 128 * (i % 4 // 2)
            diag[rank * i : rank * (i + 1), at : at + 128] = tile


def load_kernel(*refs):
    count = len(refs) // 2
    sems = refs[-1]
    copies = [
        pltpu.make_async_copy(refs[n], refs[count + n], sems.at[n]) for n in range(count)
    ]
    for copy in copies:
        copy.start()
    for copy in copies:
        copy.wait()


def up_kernel(
    x_ref, basis_ref, trans_ref, side, halo_ref, own, tst_ref, diag, flat
):
    points = x_ref.shape[1]
    leaf_count, rank, leaf = basis_ref.shape
    for first in range(0, rank // 4, 4):
        blocks = [
            trans_ref[128 * step : 128 * step + 128, :].astype(F32).T
            for step in range(first, first + 4)
        ]
        for q in range(4):
            pieces = [block if q == 0 else pltpu.roll(block, 128 - 32 * q, 1) for block in blocks]
            for step, piece in enumerate(pieces, first):
                flat[pl.ds(4 * step + q, leaf_count, stride=rank), :] = piece
    tst_ref[...] = flat[:, 0:rank].astype(BF)
    fill_block_diagonal(basis_ref, diag)

    odd = lax.rem(lax.axis_index("leaf"), 2) == 1
    base = HALO * leaf // 128 * 64
    for t in range(HALO * leaf // 128):
        rows = slice(64 * t, 64 * t + 64)
        at = points - HALO * leaf + 128 * t
        head, tail = x_ref[:, 128 * t : 128 * t + 128], x_ref[:, at : at + 128]
        side[rows, :] = jnp.where(odd, head, tail)
        halo_ref[:, 128 * t : 128 * t + 128] = jnp.where(odd, tail, head)

    def put(at, left, right):
        rows = left.shape[0]
        both = jnp.where(low_half(rows), left, right)
        own[at : at + rows, :] = both
        side[base + at : base + at + rows, :] = both

    parent_count = leaf_count // 8
    skels = []
    for quad in range(leaf_count // 4):
        x = x_ref[:, 256 * quad : 256 * quad + 256]
        skels.append(
            matmul_nt(
                diag[128 * quad : 128 * quad + 128, :], jnp.concatenate([x, x], 0)
            ).astype(BF)
        )
    parents = [
        matmul_tn(
            tst_ref[256 * p : 256 * p + 256, :], jnp.concatenate(skels[2 * p : 2 * p + 2], 0)
        ).astype(BF)
        for p in range(parent_count)
    ]
    for quad, skel in enumerate(skels):
        put(64 * quad, skel[:64], skel[64:])
    for m in range((parent_count + 1) // 2):
        put(16 * leaf_count + 32 * m, parents[2 * m], parents[min(2 * m + 1, parent_count - 1)])


def place(r, leaf_count):
    safe = jnp.minimum(r, leaf_count - 1)
    return pl.multiple_of((safe >> 2) * 64 + (safe & 1) * 32, 32), (safe >> 1) & 1


def wanted(requests, reach, up):
    row = requests[pl.ds(jnp.where(up, 3 + reach, 4 - reach), 1), :]
    return [row[0, c] for c in range(8)]


def join_kernel(base, own_ref, one_ref, out_ref):
    size = own_ref.shape[0]
    out_ref[:size, :] = own_ref[...]
    out_ref[size:, :] = one_ref[base:, :]


def near_kernel(
    x_ref,
    one_ref,
    two_ref,
    near_ref,
    source_hbm,
    out_ref,
    source_ref,
    held,
    twice,
    sems,
):
    leaf_count, leaf, depth = near_ref.shape
    count = source_hbm.shape[0]
    quads = leaf_count // 4
    copy_source = pltpu.make_async_copy(source_hbm, source_ref, sems.at[quads])
    copy_source.start()

    def copy(quad):
        part = pl.ds(4 * quad, 4)
        return pltpu.make_async_copy(near_ref.at[part], held.at[part], sems.at[quad])

    for quad in range(quads):
        copy(quad).start()

    low = low_half(leaf)

    def spread(parts):
        others = [swapped(value) for value, _ in parts]
        for (value, at), other in zip(parts, others):
            twice[at] = jnp.where(low, value, other)
            twice[at + 1] = jnp.where(low, other, value)

    odd = lax.rem(lax.axis_index("leaf"), 2) == 1
    after = HALO + leaf_count
    at_one, at_two = jnp.where(odd, 0, after), jnp.where(odd, after, 0)
    halos = range(HALO // 2)
    spread([(one_ref[64 * n : 64 * n + 64, :], at_one + 2 * n) for n in halos])
    spread([(two_ref[:, 128 * n : 128 * n + 128], at_two + 2 * n) for n in halos])
    for first in range(0, leaf_count // 2, 5):
        spread(
            [(x_ref[:, 128 * n : 128 * n + 128], HALO + 2 * n) for n in range(first, first + 5)]
        )
    copy_source.wait()

    def product(i):
        pieces = [
            jnp.where(low, twice[source_ref[2 * m, i]], twice[source_ref[2 * m + 1, i]])
            for m in range(count // 2)
        ]
        if count % 2:
            pieces.append(twice[source_ref[count - 1, i]][:, :leaf])
        return matmul_nt(jnp.concatenate(pieces, 1), held[i])

    def body(step, carry):
        copy(2 * step).wait()
        copy(2 * step + 1).wait()
        parts = [product(8 * step + u) for u in range(8)]
        for t in range(4):
            lanes = pl.ds(pl.multiple_of(512 * step + 128 * t, 128), 128)
            out_ref[:, lanes] = jnp.concatenate(parts[2 * t : 2 * t + 2], 1)
        return carry

    lax.fori_loop(0, quads // 2, body, 0)


def split(value):
    low = low_half(value.shape[0])
    other = swapped(value)
    return jnp.where(low, value, other), jnp.where(low, other, value)


class Tables:
    def __init__(self, leaf_count, slots, window, requests):
        self.leaf_count, self.slots, self.window, self.requests = leaf_count, slots, window, requests
        self.parent_count = leaf_count // 8

    def put_parents(self, ref, at, reach, up):
        block = jnp.where(up, 4 + reach, 4 - reach)
        tiles = range((self.parent_count + 1) // 2)
        values = [ref[at + 32 * m : at + 32 * m + 32, :] for m in tiles]
        for m, (left, right) in zip(tiles, [split(value) for value in values]):
            self.window[self.parent_count * block + 2 * m] = left
            if 2 * m + 1 < self.parent_count:
                self.window[self.parent_count * block + 2 * m + 1] = right

    def put_own(self, ref):
        for first in range(0, self.leaf_count // 4, 5):
            quads = range(first, first + 5)
            values = [ref[64 * quad : 64 * quad + 64, :] for quad in quads]
            for quad, (left, right) in zip(quads, [split(value) for value in values]):
                self.slots[4 * quad] = left[:32]
                self.slots[4 * quad + 1] = left[32:]
                self.slots[4 * quad + 2] = right[:32]
                self.slots[4 * quad + 3] = right[32:]
        self.put_parents(ref, 16 * self.leaf_count, 0, False)

    def put_reply(self, ref, at, reach, up):
        k = jnp.where(up, 3 + reach, 4 - reach)
        values = [ref[at + 32 * m : at + 32 * m + 32, :] for m in range(4)]
        for m, (left, right) in enumerate([split(value) for value in values]):
            self.slots[self.leaf_count + 8 * k + 2 * m] = left
            self.slots[self.leaf_count + 8 * k + 2 * m + 1] = right

    def look_up(self, ref, at, reach, up):
        k = jnp.where(up, 3 + reach, 4 - reach)
        low = low_half(32)
        asked = wanted(self.requests, reach, up)
        places = [place(r, self.leaf_count) for r in asked]
        values = [ref[pl.ds(at + row, 32), :] for row, _ in places]
        others = [swapped(value) for value in values]
        for c, r in enumerate(asked):
            value = jnp.where(low == (places[c][1] == 0), values[c], others[c])
            self.slots[self.leaf_count + 8 * k + c] = jnp.where(
                r < self.leaf_count, value, jnp.zeros_like(value)
            )


def is_odd():
    return lax.rem(lax.axis_index("leaf"), 2) == 1


def first_kernel(leaf_count, base, own_ref, one_ref, requests, slots, window):
    tables = Tables(leaf_count, slots, window, requests)
    inward = jnp.logical_not(is_odd())
    tables.look_up(one_ref, base, 1, inward)
    tables.put_parents(one_ref, base + 16 * leaf_count, 1, inward)
    tables.put_own(own_ref)


def hand_kernel(leaf_count, three_ref, far_ref, requests, out_ref):
    outward = jnp.logical_not(is_odd())
    low = low_half(32)
    size = far_ref.shape[0] // 2
    parents = 16 * leaf_count
    places = (
        (three_ref, size, 1, outward),
        (three_ref, 0, 2, outward),
        (far_ref, 0, 4, is_odd()),
    )
    for n, (ref, at, reach, up) in enumerate(places):
        asked = wanted(requests, reach, up)
        values = []
        for c, r in enumerate(asked):
            row, high = place(r, leaf_count)
            value = ref[pl.ds(at + row, 32), :]
            value = jnp.where(high != c % 2, swapped(value), value)
            values.append(jnp.where(r < leaf_count, value, jnp.zeros_like(value)))
        for m in range(4):
            row = 128 * n + 32 * m
            out_ref[row : row + 32, :] = jnp.where(low, values[2 * m], values[2 * m + 1])
        rows = 384 + (size - parents) * n
        out_ref[rows : rows + size - parents, :] = ref[at + parents : at + size, :]


def second_kernel(leaf_count, three_ref, far_ref, requests, slots_in, window_in, slots, window):
    tables = Tables(leaf_count, slots, window, requests)
    odd = is_odd()
    size = far_ref.shape[0] // 2
    for ref, at, reach, up in (
        (three_ref, size, 2, jnp.logical_not(odd)),
        (three_ref, 0, 3, jnp.logical_not(odd)),
        (far_ref, 0, 3, odd),
        (far_ref, size, 4, odd),
    ):
        tables.look_up(ref, at, reach, up)
        tables.put_parents(ref, at + 16 * leaf_count, reach, up)


def down_kernel(
    over_ref,
    coup_hbm,
    par_hbm,
    coup_ref,
    par_ref,
    diag,
    tst_ref,
    near_ref,
    slots_in,
    window_in,
    out_hbm,
    slots,
    window,
    coup_source,
    par_source,
    outs,
    leaf_outs,
    out_ref,
    sems,
    out_sems,
):
    copies = [
        pltpu.make_async_copy(source, held, sems.at[n])
        for n, (source, held) in enumerate(((par_hbm, par_source), (coup_hbm, coup_source)))
    ]
    for copy in copies:
        copy.start()
    leaf_count, rank = coup_ref.shape[:2]
    parent_count = par_ref.shape[0]
    low64 = low_half(64)
    low = low_half(rank)
    tables = Tables(leaf_count, slots, window, None)
    odd = is_odd()
    parent_size = (over_ref.shape[0] - 384) // 3
    for n, (reach, up) in enumerate(((1, odd), (2, odd), (4, jnp.logical_not(odd)))):
        tables.put_reply(over_ref, 128 * n, reach, up)
        tables.put_parents(over_ref, 384 + parent_size * n, reach, up)
    for copy in copies:
        copy.wait()
    per = par_source.shape[1]
    coup = coup_source.shape[0]
    for first in range(0, parent_count, 2):
        some = range(first, min(first + 2, parent_count))
        pieces = [
            jnp.where(low, window[par_source[some[0], j]], window[par_source[some[-1], j]])
            for j in range(per)
        ]
        rows = par_ref[first : first + len(some)].reshape(len(some) * rank, per * rank)
        found = matmul(rows, jnp.concatenate(pieces, 0)).astype(BF)
        for n, p in enumerate(some):
            outs[p] = split(found[rank * n : rank * n + rank, :])[n]

    def couple(i):
        pieces = [
            jnp.where(low, slots[coup_source[j, i]], slots[coup_source[j, i + 1]])
            for j in range(coup)
        ]
        rows = coup_ref[i : i + 2].reshape(2 * rank, coup * rank)
        return matmul(rows, jnp.concatenate(pieces, 0))

    quads = leaf_count // 4
    downs = [
        matmul(tst_ref[256 * p : 256 * p + 256, :], outs[p]) for p in range(parent_count)
    ]
    for quad in range(quads):
        coupled = jnp.concatenate([couple(4 * quad), couple(4 * quad + 2)], 0)
        down = downs[quad // 2][128 * (quad % 2) : 128 * (quad % 2) + 128]
        leaf_outs[128 * quad : 128 * quad + 128, :] = (coupled + down).astype(BF)

    def send(p):
        part = pl.ds(512 * p, 512)
        return pltpu.make_async_copy(out_ref.at[:, part], out_hbm.at[:, part], out_sems.at[p])

    for first in range(0, quads, 2):
        tiles = []
        for quad in range(first, first + 2):
            rows = slice(128 * quad, 128 * quad + 128)
            far = matmul_tn(leaf_outs[rows, :], diag[rows, :])
            for t in range(2):
                lanes = slice(256 * quad + 128 * t, 256 * quad + 128 * t + 128)
                tile = jnp.where(
                    low64, far[:64, 128 * t : 128 * t + 128], far[64:, 128 * t : 128 * t + 128]
                )
                tiles.append((lanes, (near_ref[:, lanes] + tile).astype(BF)))
        for lanes, tile in tiles:
            out_ref[:, lanes] = tile
        send(first // 2).start()
    for p in range(parent_count):
        send(p).wait()


def in_hbm(array):
    return pltpu.with_memory_space_constraint(array, pltpu.HBM)


def params(mib):
    return pltpu.CompilerParams(vmem_limit_bytes=mib << 20)


def cost(flops, size):
    return pl.CostEstimate(flops=flops, bytes_accessed=size, transcendentals=0)


def shards(
    rhs,
    basis,
    transfer,
    near_rows,
    near_source,
    far_request,
    coup_rows,
    coup_source,
    par_rows,
    par_source,
):
    leaf_count, leaf, rank = basis.shape
    points, rhs_count = rhs.shape
    parent_count = par_rows.shape[0]
    near_count = near_source.shape[1]
    coup_count = coup_source.shape[1]
    base = HALO // 2 * rhs_count
    parent_rows = rank * ((parent_count + 1) // 2)
    packed = base + 16 * leaf_count + parent_rows
    count = lax.axis_size("leaf")

    x = rhs.T
    trans = transfer.transpose(1, 2, 0).reshape(rank * rank, leaf_count)
    shape = jax.ShapeDtypeStruct
    vmem, hbm = (pl.BlockSpec(memory_space=kind) for kind in (VMEM, pltpu.HBM))
    basis_t = basis.transpose(0, 2, 1)
    inputs = (x, basis_t, trans, far_request[0])
    x, basis_t, trans, ask = pl.pallas_call(
        load_kernel,
        out_shape=tuple(shape(held.shape, held.dtype) for held in inputs),
        in_specs=[hbm] * 4,
        out_specs=(vmem,) * 4,
        scratch_shapes=[DMA((4,))],
        compiler_params=params(8),
        cost_estimate=cost(10**6, 2 * 10**6),
        name="load",
    )(*(in_hbm(held) for held in inputs))

    def exchange(block, begin, distance=1):
        pairs = [(i, i + distance) for i in range(begin, count - distance, 2)]
        return lax.ppermute(block, "leaf", pairs + [(b, a) for a, b in pairs])

    other_ask = exchange(far_request[0], 0)
    side, halo, own, tst, diag = pl.pallas_call(
        up_kernel,
        out_shape=(
            shape((packed, 128), BF),
            shape((rhs_count, HALO * leaf), BF),
            shape((packed - base, 128), BF),
            shape((rank * leaf_count, rank), BF),
            shape((rank * leaf_count, 256), BF),
        ),
        in_specs=[vmem] * 3,
        out_specs=(vmem,) * 5,
        scratch_shapes=[VMEM((rank * leaf_count, 128), F32)],
        compiler_params=params(8),
        cost_estimate=cost(10**9, 2 * 10**6),
        name="upward",
    )(x, basis_t, trans)
    one = exchange(side, 0)
    two = exchange(halo, 1)
    both = pl.pallas_call(
        functools.partial(join_kernel, base),
        out_shape=shape((2 * (packed - base), 128), BF),
        in_specs=[vmem] * 2,
        out_specs=vmem,
        compiler_params=params(8),
        cost_estimate=cost(10**6, 10**6),
        name="join",
    )(own, one)
    far = exchange(both, 1, 3)
    three = exchange(both, 0, 3)
    table_shapes = (
        shape((leaf_count + 64, rank, 128), BF),
        shape((9 * parent_count, rank, 128), BF),
    )
    tables = pl.pallas_call(
        functools.partial(first_kernel, leaf_count, base),
        out_shape=table_shapes,
        in_specs=[vmem] * 3,
        out_specs=(vmem,) * 2,
        compiler_params=params(8),
        cost_estimate=cost(10**6, 10**6),
        name="first_tables",
    )(own, one, ask)
    near = pl.pallas_call(
        near_kernel,
        out_shape=shape((rhs_count, points), F32),
        in_specs=[vmem, vmem, vmem, hbm, hbm],
        out_specs=vmem,
        scratch_shapes=[
            SMEM((near_count, leaf_count), jnp.int32),
            VMEM(near_rows.shape, BF),
            VMEM((leaf_count + 2 * HALO, leaf, 128), BF),
            DMA((leaf_count // 4 + 1,)),
        ],
        compiler_params=params(20),
        cost_estimate=cost(35 * 10**8, 9 * 10**5 * 5),
        name="near",
    )(x, one, two, in_hbm(near_rows), in_hbm(near_source.T))

    three, far, near, tables = lax.optimization_barrier((three, far, near, tables))
    hand = pl.pallas_call(
        functools.partial(hand_kernel, leaf_count),
        out_shape=shape((384 + 3 * parent_rows, 128), BF),
        in_specs=[vmem] * 3,
        out_specs=vmem,
        compiler_params=params(8),
        cost_estimate=cost(10**6, 10**6),
        name="hand_over",
    )(three, far, other_ask)
    over = exchange(hand, 0)

    tables = pl.pallas_call(
        functools.partial(second_kernel, leaf_count),
        out_shape=table_shapes,
        in_specs=[vmem] * 5,
        out_specs=(vmem,) * 2,
        input_output_aliases={3: 0, 4: 1},
        compiler_params=params(8),
        cost_estimate=cost(10**6, 10**6),
        name="second_tables",
    )(three, far, ask, *tables)

    product, _, _ = pl.pallas_call(
        down_kernel,
        out_shape=(shape((rhs_count, points), BF),) + table_shapes,
        in_specs=[vmem] + [hbm] * 2 + [vmem] * 7,
        out_specs=(hbm, vmem, vmem),
        input_output_aliases={8: 1, 9: 2},
        scratch_shapes=[
            SMEM((coup_count, leaf_count), jnp.int32),
            SMEM(par_source.shape, jnp.int32),
            VMEM((parent_count, rank, 128), BF),
            VMEM((rank * leaf_count, 128), BF),
            VMEM((rhs_count, points), BF),
            DMA((2,)),
            DMA((parent_count,)),
        ],
        compiler_params=params(12),
        cost_estimate=cost(10**9, 4 * 10**6),
        name="downward",
    )(
        over,
        in_hbm(coup_source.T),
        in_hbm(par_source),
        coup_rows,
        par_rows,
        diag,
        tst,
        near,
        *tables,
    )
    return product.T


def solution(mesh):
    split = ("groups", "leaf")
    return jax.shard_map(
        shards,
        mesh=mesh,
        in_specs=(
            P(split, None),
            P(split, None, None),
            P(split, None, None),
            P(split, None, None),
            P(split, None),
            P(split, None, None),
            P(split, None, None),
            P(split, None),
            P(split, None, None),
            P(split, None),
        ),
        out_specs=P(split, None),
        check_vma=False,
    )
```
